32 devices in a mesh: groups: 2 (over y), band: 4 (over z), field: 2 (over x), wave: 2 (over core).
Axes of the slice: x: 2, y: 2, z: 4, core: 2. Of those that a mesh axis runs over, the one named last changes fastest.
Arguments:
- predicted_state: bfloat16 [64, 4, 2688], P(('groups', 'band', 'field', 'wave')), parts along dimension 0, may hold values from -6 to 6
- analysis_state: bfloat16 [64, 4, 2688], P(('groups', 'band', 'field', 'wave')), parts along dimension 0, may hold values from -6 to 6
- nodes_per_parallel: int32 [32], replicated, may hold values from 20 to 2688, as said below
- weighted_harmonic_table: bfloat16 [384, 32, 768], P(('field', 'wave'), 'band'), may hold values from -1 to 1
Outputs:
- quantity_misfit: float32 [8], P(('groups', 'band')), parts along dimension 0
- predicted_sensitivity: bfloat16 [64, 4, 2688], P(('groups', 'band', 'field', 'wave')), parts along dimension 0
The draws below stay inside these ranges and needn't reach their ends.
There are 2 independent parts, one for each index of `groups`. The reference program is written for one: setup_inputs(seed, part) draws one part's arguments, and reference() takes and returns one part's arrays. A program takes and returns all parts, laid end to end along the dimension named above; an argument that names none is the same for every part. Nothing has to cross between parts.
Inputs may be any that keep to these rules, and one draw needn't show every extreme that they name: Every entry is a multiple of 4; cycle i holds nodes_per_parallel[i] points.
All inputs are finite; a program needn't handle non-finite values.
Results may differ from the reference program's by a relative error of at most 0.014.
Values may be sent and summed in bfloat16 or wider, within the bound.
No kernel may reach another device: no remote copies, remote signals or barrier semaphores. Data moves between devices by JAX's collectives and lax.ppermute only.
A program may use at most 64 MiB of HBM per device.

```python
import math
import jax
import jax.numpy as jnp
from jax import lax

NODES_MAX = 2688
PAIRS = 384
SLOTS = 768
CYCLE_BAND = 8
PARALLELS = 32
QUANTITIES = 4
N_BAND = 4


def draw_nodes_per_parallel(key, part):
    key = jax.random.fold_in(key, 11)
    cycle_index = jnp.arange(PARALLELS, dtype=jnp.int32)
    from_pole = jnp.minimum(cycle_index, PARALLELS - 1 - cycle_index)
    top_quarter = NODES_MAX // 4
    base_quarter = 5 + from_pole * (top_quarter - 5) // (PARALLELS // 2 - 1)
    jitter = jax.random.randint(key, (PARALLELS,), -3, 4)
    quarter = jnp.clip(base_quarter + jitter, 5, top_quarter)
    quarter = jnp.where(from_pole == PARALLELS // 2 - 1, top_quarter, quarter)
    quarter = jnp.where(from_pole == 0, 5, quarter)
    return (4 * quarter).astype(jnp.int32)


def block_levels(own_key, extent, cuts, low, largest):
    level, own = 1.0, jax.random.fold_in(own_key, 6)
    for axis_at, shards_of in cuts:
        steps = jnp.exp(jax.random.uniform(jax.random.fold_in(own, axis_at), (shards_of,), jnp.float32, low / len(cuts), largest / len(cuts)))
        level = level * jnp.repeat(steps, extent[axis_at] // shards_of).reshape([-1 if axis == axis_at else 1 for axis in range(len(extent))])
    return level


def normal_values(key, extent, deviation, most, pieces=(), kind=jnp.bfloat16):
    values = jax.random.normal(key, extent, jnp.float32) * deviation
    if len(pieces) > 0:
        values = block_levels(key, extent, pieces, -0.22, 0.18) * values
    return jnp.clip(values, min=-most, max=most).astype(kind)


def setup_inputs(seed: int = 0, part: int = 0) -> dict:
    streams_of = jax.random.split(jax.random.key(seed), 5)
    part_keys = jax.random.split(jax.random.fold_in(streams_of[4], part), 5)
    return {
        "predicted_state": normal_values(part_keys[0], (PARALLELS, QUANTITIES, NODES_MAX), 1.0, 6.0, ((0, 16),)),
        "analysis_state": normal_values(part_keys[1], (PARALLELS, QUANTITIES, NODES_MAX), 1.0, 6.0, ((0, 16),)),
        "nodes_per_parallel": draw_nodes_per_parallel(jax.random.fold_in(streams_of[4], 71), part),
        "weighted_harmonic_table": normal_values(streams_of[3], (PAIRS, PARALLELS, SLOTS), PARALLELS ** -0.5, 1.0, ((0, 4), (1, 4))),
    }


full_turn = 2.0 * math.pi
spectrum_floor = 0.25
gradient_gain = 16.0

def slot_masks(pair_ids, degree_count, slot_count):
    column = jnp.arange(slot_count, dtype=jnp.int32)[None, :]
    limit = degree_count - pair_ids[:, None]
    low_side = column < limit
    high_side = (column >= limit) & (pair_ids[:, None] != degree_count - 1 - pair_ids[:, None])
    return (low_side, high_side)

def twiddle(points, start_col, col_count, pair_count, degree_count):
    slot_flat = jnp.arange(2 * pair_count, dtype=jnp.int32)
    pair_index = slot_flat // 2
    halves = slot_flat % 2
    wavenum = jnp.where(halves == 0, pair_index, degree_count - 1 - pair_index)
    usable = jnp.logical_not((halves == 1) & (pair_index == degree_count - 1 - pair_index))
    column = start_col + jnp.arange(col_count, dtype=jnp.int32)
    phases = column[:, None] * wavenum[None, :] % points
    angles = phases.astype(jnp.float32) * (full_turn / points.astype(jnp.float32))
    usable_cell = (column[:, None] < points) & (2 * wavenum[None, :] < points) & usable[None, :]
    cosine = jnp.where(usable_cell, jnp.cos(angles), 0.0)
    minus_sine = jnp.where(usable_cell, -jnp.sin(angles), 0.0)
    stacked = jnp.stack([cosine, minus_sine], axis=-1)
    return stacked.reshape(col_count, 4 * pair_count).astype(jnp.bfloat16)

def reference(predicted_state, analysis_state, nodes_per_parallel, weighted_harmonic_table):
    parallel_number, quantity_number, parallel_extent = predicted_state.shape
    pair_count, _, slot_count = weighted_harmonic_table.shape
    degree_count = slot_count - 1
    pair_ids = jnp.arange(pair_count, dtype=jnp.int32)
    low_side, high_side = slot_masks(pair_ids, degree_count, slot_count)
    low_mask = low_side.astype(jnp.float32)
    high_mask = high_side.astype(jnp.float32)
    weight = jnp.where(low_side & (pair_ids[:, None] == 0), 1.0, 2.0) * (low_mask + high_mask)
    column = jnp.arange(slot_count, dtype=jnp.int32)[None, :]
    degree_ids = jnp.where(low_side, pair_ids[:, None] + column, column - 1)
    degree_ids = jnp.where(low_side | high_side, degree_ids, degree_count).astype(jnp.int32)
    matrix_blocks = jnp.concatenate([predicted_state, analysis_state], axis=1)

    def cycle_fourier(cycle_item):
        panel, points = cycle_item
        tables = twiddle(points, 0, parallel_extent, pair_count, degree_count)
        summed = jnp.dot(panel, tables, preferred_element_type=jnp.float32)
        return (summed / jnp.sqrt(points.astype(jnp.float32))).astype(jnp.bfloat16)
    fourier = lax.map(cycle_fourier, (matrix_blocks, nodes_per_parallel))
    spread = fourier.reshape(N_BAND, CYCLE_BAND, 2, quantity_number, pair_count, 2, 2)
    band_tables = weighted_harmonic_table.reshape(pair_count, N_BAND, CYCLE_BAND, slot_count)

    def add_band(band_index, summed):
        block_vals = lax.dynamic_index_in_dim(spread, band_index, 0, keepdims=False).astype(jnp.float32)
        tables = lax.dynamic_index_in_dim(band_tables, band_index, 1, keepdims=False).astype(jnp.float32)
        low_part = jnp.einsum('rafqc,qrs->afqcs', block_vals[..., 0, :], tables)
        high_part = jnp.einsum('rafqc,qrs->afqcs', block_vals[..., 1, :], tables)
        joined = low_part * low_mask[:, None, :] + high_part * high_mask[:, None, :]
        rounded = lax.optimization_barrier(joined.astype(jnp.bfloat16))
        return summed + rounded.astype(jnp.float32)
    coefs = lax.fori_loop(0, N_BAND, add_band, jnp.zeros((2, quantity_number, pair_count, 2, slot_count), jnp.float32))
    coef_fore = coefs[0]
    coef_targ = coefs[1]
    powers = jnp.stack([lax.optimization_barrier(jnp.sum(coef_fore * coef_fore, 2)), lax.optimization_barrier(jnp.sum(coef_targ * coef_targ, 2)), lax.optimization_barrier(jnp.sum(coef_fore * coef_targ, 2))], 0) * weight
    slot_flat = jnp.transpose(powers, (2, 3, 0, 1)).reshape(pair_count * slot_count, 3 * quantity_number)
    degree_sums = jax.ops.segment_sum(slot_flat, degree_ids.reshape(-1), num_segments=degree_count + 1)
    spectra = jnp.transpose(degree_sums[:degree_count].reshape(degree_count, 3, quantity_number), (1, 2, 0))
    odd_weight = 2.0 * jnp.arange(degree_count, dtype=jnp.float32) + 1.0
    power_fore = spectra[0] / odd_weight + spectrum_floor
    power_targ = spectra[1] / odd_weight + spectrum_floor
    cross = spectra[2] / odd_weight
    root_fore = jnp.sqrt(power_fore)
    root_targ = jnp.sqrt(power_targ)
    geo_mean = root_fore * root_targ
    coherence = cross / geo_mean
    degree_term = (root_fore - root_targ) ** 2 + (power_fore + power_targ) * (1.0 - coherence)
    quantity_misfit = lax.optimization_barrier(jnp.mean(degree_term, axis=1))
    grad_power = gradient_gain * (1.0 - root_targ / root_fore + (1.0 - coherence) + (power_fore + power_targ) * coherence / (2.0 * power_fore)) / odd_weight
    grad_cross = -gradient_gain * (power_fore + power_targ) / geo_mean / odd_weight
    clipped = jnp.minimum(degree_ids, degree_count - 1)
    slot_power = grad_power[:, clipped]
    slot_cross = grad_cross[:, clipped]
    coef_grad = (weight[:, None, :] * (2.0 * slot_power[:, :, None, :] * coef_fore + slot_cross[:, :, None, :] * coef_targ)).astype(jnp.bfloat16)

    def band_back(band_index):
        tables = lax.dynamic_index_in_dim(band_tables, band_index, 1, keepdims=False).astype(jnp.float32)
        grads_wide = coef_grad.astype(jnp.float32)
        low_part = jnp.einsum('fqcs,qrs->rfqc', grads_wide * low_mask[:, None, :], tables)
        high_part = jnp.einsum('fqcs,qrs->rfqc', grads_wide * high_mask[:, None, :], tables)
        joined = jnp.stack([low_part, high_part], axis=3)
        return joined.reshape(CYCLE_BAND, quantity_number, 4 * pair_count).astype(jnp.bfloat16)
    parallel_derivatives = lax.map(band_back, jnp.arange(N_BAND, dtype=jnp.int32))
    parallel_derivatives = parallel_derivatives.reshape(parallel_number, quantity_number, 4 * pair_count)

    def parallel_derivative(cycle_item):
        values, points = cycle_item
        tables = twiddle(points, 0, parallel_extent, pair_count, degree_count)
        summed = lax.dot_general(values, tables, (((1,), (1,)), ((), ())), preferred_element_type=jnp.float32)
        return (summed / jnp.sqrt(points.astype(jnp.float32))).astype(jnp.bfloat16)
    predicted_sensitivity = lax.map(parallel_derivative, (parallel_derivatives, nodes_per_parallel))
    return (quantity_misfit, predicted_sensitivity)
```

```python
import functools
import math

import jax
import jax.numpy as jnp
import numpy as np
from jax import lax
from jax.experimental import pallas as pl
from jax.experimental.pallas import tpu as pltpu
from jax.sharding import PartitionSpec as P

spectrum_floor = 0.25
gradient_gain = 16.0
lane_width = 128
vmem_bytes = 40 * 1024 * 1024
bf16 = jnp.bfloat16
f32 = jnp.float32


def round_up(value, step):
    return -(-value // step) * step


def dot_nn(left, right):
    return lax.dot_general(left, right, (((1,), (0,)), ((), ())), preferred_element_type=f32)


def dot_nt(left, right):
    return lax.dot_general(left, right, (((1,), (1,)), ((), ())), preferred_element_type=f32)


def dot_tn(left, right):
    return lax.dot_general(left, right, (((0,), (0,)), ((), ())), preferred_element_type=f32)


def lane_wavenumbers(bands, owners, pairs_held, pairs_sub, degree_count):
    band, owner, pair = np.meshgrid(
        np.arange(bands), np.arange(owners), np.arange(pairs_sub), indexing="ij"
    )
    within = band * pairs_sub + pair
    pair_index = owner * pairs_held + within
    low = np.where(within < pairs_held, pair_index, 4 * degree_count)
    mirrored = degree_count - 1 - pair_index
    high = np.where((within < pairs_held) & (mirrored != pair_index), mirrored, 4 * degree_count)
    return np.concatenate([low.reshape(-1), high.reshape(-1)])[None, :].astype(np.float32)


def cos_and_minus_sin(wavenum, points, columns, inverse):
    quarters = (4.0 * wavenum) * columns
    turns = jnp.floor(quarters * inverse + 0.5)
    angle = (quarters - turns * points) * (0.5 * math.pi * inverse)
    square = angle * angle
    sine = angle * (1.0 + square * (-1.0 / 6 + square * (1.0 / 120 + square * (-1.0 / 5040))))
    cosine = 1.0 + square * (
        -0.5 + square * (1.0 / 24 + square * (-1.0 / 720 + square * (1.0 / 40320)))
    )
    quadrant = turns.astype(jnp.int32)
    swap = (quadrant & 1) != 0
    new_cos = jnp.where(swap, sine, cosine)
    new_sin = jnp.where(swap, cosine, sine)
    new_cos = jnp.where(((quadrant + 1) & 2) != 0, -new_cos, new_cos)
    new_sin = jnp.where((quadrant & 2) != 0, new_sin, -new_sin)
    return new_cos, new_sin


def analyse_kernel(nodes_ref, waves_ref, fore_ref, targ_ref, wire_ref, coarse_ref, fine_ref, rows_scr):
    share, fields, extent = fore_ref.shape
    steps = extent // lane_width
    both = waves_ref.shape[1]
    half_lanes = both // 2
    panel_rows = 2 * fields
    coarse_rows = coarse_ref.shape[2]
    rows_scr[...] = jnp.zeros_like(rows_scr)
    for il in range(share):
        points_i = nodes_ref[il]
        points = jnp.full((1, both), points_i, jnp.int32).astype(f32)
        inverse = 1.0 / points
        wavenum = waves_ref[...]
        resolved = 2.0 * wavenum < points

        def rows_of(count, scale):
            return (lax.broadcasted_iota(jnp.int32, (count, both), 0) * scale).astype(f32)

        coarse_c, coarse_s = cos_and_minus_sin(wavenum, points, rows_of(coarse_rows, lane_width), inverse)
        coarse_ref[il, 0] = jnp.where(resolved, coarse_c, 0.0)
        coarse_ref[il, 1] = jnp.where(resolved, coarse_s, 0.0)
        mid_c, mid_s = cos_and_minus_sin(wavenum, points, rows_of(lane_width // 8, 8), inverse)
        unit_c, unit_s = cos_and_minus_sin(wavenum, points, rows_of(8, 1), inverse)
        for g in range(lane_width // 16):
            pieces_c = []
            pieces_s = []
            for a in (2 * g, 2 * g + 1):
                step_c = mid_c[a : a + 1]
                step_s = mid_s[a : a + 1]
                pieces_c.append(step_c * unit_c - step_s * unit_s)
                pieces_s.append(step_c * unit_s + step_s * unit_c)
            fine_ref[il, 0, 16 * g : 16 * g + 16] = jnp.concatenate(pieces_c, 0).astype(bf16)
            fine_ref[il, 1, 16 * g : 16 * g + 16] = jnp.concatenate(pieces_s, 0).astype(bf16)
        panel = jnp.concatenate([fore_ref[il].astype(f32), targ_ref[il].astype(f32)], axis=0)
        column = lax.broadcasted_iota(jnp.int32, (panel_rows, extent), 1)
        panel = jnp.where(column < points_i, panel, 0.0)
        stacked = jnp.concatenate(
            [panel[:, lane_width * j : lane_width * (j + 1)] for j in range(steps)], axis=0
        ).astype(bf16)
        scale = 1.0 / jnp.sqrt(points[:, :half_lanes])
        for h in range(2):
            lanes = slice(h * half_lanes, (h + 1) * half_lanes)
            part_c = dot_nn(stacked, fine_ref[il, 0, :, lanes])
            part_s = dot_nn(stacked, fine_ref[il, 1, :, lanes])
            total_c = jnp.zeros((panel_rows, half_lanes), f32)
            total_s = jnp.zeros((panel_rows, half_lanes), f32)
            for j in range(steps):
                turn_c = coarse_ref[il, 0, j : j + 1, lanes]
                turn_s = coarse_ref[il, 1, j : j + 1, lanes]
                piece_c = part_c[j * panel_rows : (j + 1) * panel_rows]
                piece_s = part_s[j * panel_rows : (j + 1) * panel_rows]
                total_c = total_c + (turn_c * piece_c - turn_s * piece_s)
                total_s = total_s + (turn_c * piece_s + turn_s * piece_c)
            at = (il * 2 + h) * 2 * panel_rows
            rows_scr[at : at + panel_rows, :] = total_c * scale
            rows_scr[at + panel_rows : at + 2 * panel_rows, :] = total_s * scale
    wire_ref[...] = jnp.transpose(rows_scr[...]).astype(bf16)


def take_block(rows, index, width, lanes):
    if width % lane_width == 0:
        return rows[:, index * width : (index + 1) * width]
    total = rows.shape[1]
    if index > 0:
        rows = pltpu.roll(rows, total - index * width, 1)
    return rows[:, :lanes]


def join_blocks(blocks, width, total):
    if width % lane_width == 0:
        return jnp.concatenate(blocks, axis=1)
    joined = jnp.zeros((blocks[0].shape[0], total), f32)
    lane = lax.broadcasted_iota(jnp.int32, joined.shape, 1)
    for index, block in enumerate(blocks):
        wide = jnp.concatenate([block] * (total // block.shape[1]), axis=1)
        if index > 0:
            wide = pltpu.roll(wide, index * width, 1)
        here = (lane >= index * width) & (lane < (index + 1) * width)
        joined = jnp.where(here, wide, joined)
    return joined


def pair_tables(table_refs, q):
    return jnp.concatenate([t[q].astype(f32) for t in table_refs], axis=0).astype(bf16)


def project_kernel(bands, owners, pairs_held, share, place_ref, wire_ref, *refs):
    table_refs = refs[:bands]
    coef_ref, spectra_ref, flat_scr, left_scr = refs[bands:]
    sources, pairs_sub, _ = wire_ref.shape
    slot_count = table_refs[0].shape[2]
    degree_count = slot_count - 1
    panel_rows = coef_ref.shape[2]
    fields = panel_rows // 2
    block_rows = 4 * panel_rows
    band = place_ref[0]
    first = place_ref[1] * pairs_held + band * pairs_sub
    for k in range(bands):
        other = band ^ k
        for w in range(owners):
            at = (k * owners + w) * pairs_sub
            rows = wire_ref[other * owners + w].astype(f32)
            for c in range(flat_scr.shape[0]):
                flat_scr[c, at : at + pairs_sub, :] = rows[:, c * lane_width : (c + 1) * lane_width]
    slot = lax.broadcasted_iota(jnp.int32, (panel_rows, slot_count), 1)
    zero = jnp.zeros((panel_rows, slot_count), f32)
    low_power, low_cross, high_power, high_cross = zero, zero, zero, zero
    for q in reversed(range(pairs_sub)):
        received = jnp.concatenate(
            [
                flat_scr[c, pl.ds(q, sources, stride=pairs_sub), :]
                for c in range(flat_scr.shape[0])
            ],
            axis=1,
        )
        for il in range(share):
            left_scr[q, pl.ds(il, sources, stride=share), :] = take_block(
                received, il, block_rows, left_scr.shape[2]
            )
        left = left_scr[q, :, 0:block_rows].astype(bf16)
        both_halves = dot_tn(left, pair_tables(table_refs, q))
        pair = first + q
        low_side = slot < degree_count - pair
        cosines = jnp.where(
            low_side, both_halves[0:panel_rows], both_halves[2 * panel_rows : 3 * panel_rows]
        )
        sines = jnp.where(
            low_side, both_halves[panel_rows : 2 * panel_rows], both_halves[3 * panel_rows :]
        )
        coef_ref[q, 0] = cosines
        coef_ref[q, 1] = sines
        low_weight = jnp.where(pair == 0, 1.0, 2.0)
        high_weight = jnp.where(2 * pair == degree_count - 1, 0.0, 2.0)
        weight = jnp.where(low_side, low_weight, high_weight)
        power = (cosines * cosines + sines * sines) * weight
        cross = (
            cosines * pltpu.roll(cosines, fields, 0) + sines * pltpu.roll(sines, fields, 0)
        ) * weight
        low_power = pltpu.roll(low_power, 1, 1) + jnp.where(low_side, power, 0.0)
        low_cross = pltpu.roll(low_cross, 1, 1) + jnp.where(low_side, cross, 0.0)
        high_power = high_power + jnp.where(low_side, 0.0, power)
        high_cross = high_cross + jnp.where(low_side, 0.0, cross)
    spectra_ref[0] = pltpu.roll(low_power, first, 1) + pltpu.roll(high_power, slot_count - 1, 1)
    spectra_ref[1] = pltpu.roll(low_cross, first, 1) + pltpu.roll(high_cross, slot_count - 1, 1)


def tree_sum(parts):
    while len(parts) > 1:
        parts = [parts[i] + parts[i + 1] for i in range(0, len(parts), 2)]
    return parts[0]


def gradient_kernel(bands, owners, pairs_held, share, spectra_parts, place_ref, *refs):
    spectra_refs = refs[:spectra_parts]
    coef_ref = refs[spectra_parts]
    table_refs = refs[spectra_parts + 1 : spectra_parts + 1 + bands]
    wire_ref, misfit_ref, flat_scr, cycle_scr = refs[spectra_parts + 1 + bands :]
    sources, pairs_sub, _ = wire_ref.shape
    slot_count = table_refs[0].shape[2]
    degree_count = slot_count - 1
    panel_rows = coef_ref.shape[2]
    fields = panel_rows // 2
    block_rows = 4 * panel_rows
    fields_out = fields // bands
    band = place_ref[0]
    first = place_ref[1] * pairs_held + band * pairs_sub
    if block_rows < cycle_scr.shape[2]:
        cycle_scr[...] = jnp.zeros_like(cycle_scr)
    slot = lax.broadcasted_iota(jnp.int32, (panel_rows, slot_count), 1)
    row = lax.broadcasted_iota(jnp.int32, (panel_rows, slot_count), 0)
    odd_weight = (2 * slot + 1).astype(f32)
    power = tree_sum([s[0] for s in spectra_refs]) / odd_weight + spectrum_floor
    cross = tree_sum([s[1] for s in spectra_refs]) / odd_weight
    root = jnp.sqrt(power)
    other_root = pltpu.roll(root, fields, 0)
    both_power = power + pltpu.roll(power, fields, 0)
    geo_mean = root * other_root
    coherence = cross / geo_mean
    term = (root - other_root) * (root - other_root) + both_power * (1.0 - coherence)
    term = jnp.where(slot < degree_count, term, 0.0)
    mean = jnp.sum(term, axis=1, keepdims=True) / degree_count
    field_row = lax.broadcasted_iota(jnp.int32, (panel_rows, 1), 0)
    misfit_ref[...] = jnp.zeros_like(misfit_ref)
    for i in range(fields_out):
        chosen = jnp.where(field_row == band * fields_out + i, mean, 0.0)
        misfit_ref[i : i + 1, :] = jnp.broadcast_to(
            jnp.sum(chosen, axis=0, keepdims=True), (1, lane_width)
        )
    grad_power = (
        gradient_gain
        * (
            1.0
            - other_root / root
            + (1.0 - coherence)
            + both_power * coherence / (2.0 * power)
        )
        / odd_weight
    )
    grad_cross = -gradient_gain * both_power / geo_mean / odd_weight
    by_degree = jnp.where(row < fields, 2.0 * grad_power, grad_cross)
    high_grad = pltpu.roll(by_degree, 1, 1)
    low_grad = pltpu.roll(by_degree, slot_count - first, 1)
    for q in range(pairs_sub):
        pair = first + q
        low_side = slot < degree_count - pair
        low_weight = jnp.where(pair == 0, 1.0, 2.0)
        high_weight = jnp.where(2 * pair == degree_count - 1, 0.0, 2.0)
        gain = jnp.where(low_side, low_grad * low_weight, high_grad * high_weight)
        cosines = coef_ref[q, 0] * gain
        sines = coef_ref[q, 1] * gain
        cosines = cosines + pltpu.roll(cosines, fields, 0)
        sines = sines + pltpu.roll(sines, fields, 0)
        masked = jnp.concatenate(
            [
                jnp.where(low_side, cosines, 0.0),
                jnp.where(low_side, sines, 0.0),
                jnp.where(low_side, 0.0, cosines),
                jnp.where(low_side, 0.0, sines),
            ],
            axis=0,
        ).astype(bf16)
        cycle_scr[q, :, 0:block_rows] = dot_nt(pair_tables(table_refs, q), masked)
        joined = join_blocks(
            [cycle_scr[q, pl.ds(il, sources, stride=share), :] for il in range(share)],
            block_rows,
            flat_scr.shape[0] * lane_width,
        )
        for c in range(flat_scr.shape[0]):
            flat_scr[c, pl.ds(q, sources, stride=pairs_sub), :] = joined[
                :, c * lane_width : (c + 1) * lane_width
            ]
        low_grad = pltpu.roll(low_grad, slot_count - 1, 1)
    for k in range(bands):
        other = band ^ k
        for w in range(owners):
            at = (k * owners + w) * pairs_sub
            wire_ref[other * owners + w] = jnp.concatenate(
                [flat_scr[c, at : at + pairs_sub, :] for c in range(flat_scr.shape[0])], axis=1
            ).astype(bf16)


def synthesise_kernel(nodes_ref, coarse_ref, fine_ref, wire_ref, out_ref):
    share, fields, extent = out_ref.shape
    steps = extent // lane_width
    half_lanes = coarse_ref.shape[3] // 2
    panel_rows = 2 * fields
    values = jnp.transpose(wire_ref[...].astype(f32))
    column = lax.broadcasted_iota(jnp.int32, (fields, lane_width), 1)
    for il in range(share):
        points_i = nodes_ref[il]
        total = jnp.zeros((steps * panel_rows, lane_width), f32)
        for h in range(2):
            lanes = slice(h * half_lanes, (h + 1) * half_lanes)
            at = (il * 2 + h) * 2 * panel_rows
            cosines = values[at : at + panel_rows]
            sines = values[at + panel_rows : at + 2 * panel_rows]
            turned_c = []
            turned_s = []
            for j in range(steps):
                turn_c = coarse_ref[il, 0, j : j + 1, lanes]
                turn_s = coarse_ref[il, 1, j : j + 1, lanes]
                turned_c.append(cosines * turn_c + sines * turn_s)
                turned_s.append(sines * turn_c - cosines * turn_s)
            total = total + dot_nt(
                jnp.concatenate(turned_c, 0).astype(bf16), fine_ref[il, 0, :, lanes]
            )
            total = total + dot_nt(
                jnp.concatenate(turned_s, 0).astype(bf16), fine_ref[il, 1, :, lanes]
            )
        points = jnp.full((1, lane_width), points_i, jnp.int32).astype(f32)
        scale = 1.0 / jnp.sqrt(points)
        for j in range(steps):
            piece = total[j * panel_rows : j * panel_rows + fields] * scale
            piece = jnp.where(column + j * lane_width < points_i, piece, 0.0)
            out_ref[il, :, lane_width * j : lane_width * (j + 1)] = piece.astype(bf16)


def vmem_spec():
    return pl.BlockSpec(memory_space=pltpu.VMEM)


def smem_spec():
    return pl.BlockSpec(memory_space=pltpu.SMEM)


def call(body, name, scalars, arrays, out_shapes, scratch):
    return pl.pallas_call(
        body,
        name=name,
        in_specs=[smem_spec()] + [vmem_spec()] * len(arrays),
        out_specs=tuple(vmem_spec() for _ in out_shapes),
        out_shape=tuple(out_shapes),
        scratch_shapes=scratch,
        compiler_params=pltpu.CompilerParams(vmem_limit_bytes=vmem_bytes),
    )(scalars, *arrays)


def exchange(array, axes, count):
    return [array] + [
        lax.ppermute(array, axes, [(i, i ^ k) for i in range(count)]) for k in range(1, count)
    ]


def per_device(predicted_state, analysis_state, nodes_per_parallel, weighted_harmonic_table):
    share, fields, extent = predicted_state.shape
    pairs_held, cycle_band, slot_count = weighted_harmonic_table.shape
    bands = lax.axis_size("band")
    owner_axes = ("field", "wave")
    owners = lax.axis_size(owner_axes)
    group_axes = ("band", "field", "wave")
    band = lax.axis_index("band")
    owner = lax.axis_index(owner_axes)
    sources = bands * owners
    pairs_sub = -(-pairs_held // bands)
    panel_rows = 2 * fields
    wire_lanes = round_up(share * 4 * panel_rows, lane_width)
    half_lanes = sources * pairs_sub
    coarse_rows = round_up(extent // lane_width, 8)

    table = weighted_harmonic_table
    if pairs_sub * bands != pairs_held:
        table = jnp.pad(table, ((0, pairs_sub * bands - pairs_held), (0, 0), (0, 0)))
    tables = []
    for k in range(bands):
        piece = lax.dynamic_slice_in_dim(table, (band ^ k) * pairs_sub, pairs_sub, 0)
        if k > 0:
            piece = lax.ppermute(piece, "band", [(i, i ^ k) for i in range(bands)])
        tables.append(piece)

    own_start = (band * owners + owner) * share
    held_nodes = lax.dynamic_slice_in_dim(nodes_per_parallel, own_start, share, 0)
    place = jnp.stack([band, owner]).astype(jnp.int32)
    waves = jnp.asarray(lane_wavenumbers(bands, owners, pairs_held, pairs_sub, slot_count - 1))
    wire, coarse, fine = call(
        analyse_kernel,
        "analyse",
        held_nodes,
        (waves, predicted_state, analysis_state),
        (
            jax.ShapeDtypeStruct((half_lanes, wire_lanes), bf16),
            jax.ShapeDtypeStruct((share, 2, coarse_rows, 2 * half_lanes), f32),
            jax.ShapeDtypeStruct((share, 2, lane_width, 2 * half_lanes), bf16),
        ),
        [pltpu.VMEM((wire_lanes, half_lanes), f32)],
    )
    wire = lax.all_to_all(
        wire.reshape(sources, pairs_sub, wire_lanes), group_axes, 0, 0, tiled=True
    )
    coef, spectra = call(
        functools.partial(project_kernel, bands, owners, pairs_held, share),
        "project",
        place,
        (wire, *tables),
        (
            jax.ShapeDtypeStruct((pairs_sub, 2, panel_rows, slot_count), f32),
            jax.ShapeDtypeStruct((2, panel_rows, slot_count), f32),
        ),
        [
            pltpu.VMEM((wire_lanes // lane_width, sources * pairs_sub, lane_width), f32),
            pltpu.VMEM((pairs_sub, bands * cycle_band, round_up(4 * panel_rows, lane_width)), f32),
        ],
    )
    spectra = tree_sum(exchange(spectra, owner_axes, owners))
    spectra = exchange(spectra, "band", bands)
    wire, misfit = call(
        functools.partial(gradient_kernel, bands, owners, pairs_held, share, len(spectra)),
        "gradient",
        place,
        (*spectra, coef, *tables),
        (
            jax.ShapeDtypeStruct((sources, pairs_sub, wire_lanes), bf16),
            jax.ShapeDtypeStruct((8 * (-(-(fields // bands) // 8)), lane_width), f32),
        ),
        [
            pltpu.VMEM((wire_lanes // lane_width, sources * pairs_sub, lane_width), f32),
            pltpu.VMEM((pairs_sub, bands * cycle_band, round_up(4 * panel_rows, lane_width)), f32),
        ],
    )
    wire = lax.all_to_all(wire, group_axes, 0, 0, tiled=True)
    (sensitivity,) = call(
        synthesise_kernel,
        "synthesise",
        held_nodes,
        (coarse, fine, wire.reshape(half_lanes, wire_lanes)),
        (jax.ShapeDtypeStruct((share, fields, extent), bf16),),
        [],
    )
    return misfit[: fields // bands, 0], sensitivity


def solution(mesh):
    in_specs = (
        P(("groups", "band", "field", "wave"), None, None),
        P(("groups", "band", "field", "wave"), None, None),
        P(),
        P(("field", "wave"), "band", None),
    )
    out_specs = (P(("groups", "band")), P(("groups", "band", "field", "wave"), None, None))
    return jax.shard_map(
        per_device, mesh=mesh, in_specs=in_specs, out_specs=out_specs, check_vma=False
    )
```

```python
import functools
import math

import jax
import jax.numpy as jnp
import numpy as np
from jax import lax
from jax.experimental import pallas as pl
from jax.experimental.pallas import tpu as pltpu
from jax.sharding import PartitionSpec as P

spectrum_floor = 0.25
gradient_gain = 16.0
lane_width = 128
vmem_bytes = 40 * 1024 * 1024
owner_axes = ("field", "wave")
group_axes = ("band", "field", "wave")
bf16 = jnp.bfloat16
f32 = jnp.float32


def round_up(value, step):
    return -(-value // step) * step


def dot_nn(left, right):
    return lax.dot_general(left, right, (((1,), (0,)), ((), ())), preferred_element_type=f32)


def dot_nt(left, right):
    return lax.dot_general(left, right, (((1,), (1,)), ((), ())), preferred_element_type=f32)


def dot_tn(left, right):
    return lax.dot_general(left, right, (((0,), (0,)), ((), ())), preferred_element_type=f32)


def lane_wavenumbers(groups, bands, owners, pairs_held, pairs_part, degree_count):
    group, band, owner, part, pair = np.meshgrid(
        np.arange(groups),
        np.arange(bands),
        np.arange(owners),
        np.arange(groups),
        np.arange(pairs_part),
        indexing="ij",
    )
    within = (band * groups + (group ^ part)) * pairs_part + pair
    pair_index = owner * pairs_held + within
    low = np.where(within < pairs_held, pair_index, 4 * degree_count)
    mirrored = degree_count - 1 - pair_index
    high = np.where((within < pairs_held) & (mirrored != pair_index), mirrored, 4 * degree_count)
    both = np.concatenate([low.reshape(groups, 1, -1), high.reshape(groups, 1, -1)], axis=2)
    return both.astype(np.float32)


def cos_and_minus_sin(wavenum, points, columns, inverse):
    quarters = (4.0 * wavenum) * columns
    turns = jnp.floor(quarters * inverse + 0.5)
    angle = (quarters - turns * points) * (0.5 * math.pi * inverse)
    square = angle * angle
    sine = angle * (1.0 + square * (-1.0 / 6 + square * (1.0 / 120 + square * (-1.0 / 5040))))
    cosine = 1.0 + square * (
        -0.5 + square * (1.0 / 24 + square * (-1.0 / 720 + square * (1.0 / 40320)))
    )
    quadrant = turns.astype(jnp.int32)
    swap = (quadrant & 1) != 0
    new_cos = jnp.where(swap, sine, cosine)
    new_sin = jnp.where(swap, cosine, sine)
    new_cos = jnp.where(((quadrant + 1) & 2) != 0, -new_cos, new_cos)
    new_sin = jnp.where((quadrant & 2) != 0, new_sin, -new_sin)
    return new_cos, new_sin


def analyse_kernel(nodes_ref, waves_ref, fore_ref, targ_ref, wire_ref, coarse_ref, fine_ref, rows_scr):
    share, fields, extent = fore_ref.shape
    steps = extent // lane_width
    both = waves_ref.shape[2]
    half_lanes = both // 2
    panel_rows = 2 * fields
    coarse_rows = coarse_ref.shape[2]
    first_cycle = lax.axis_index(group_axes) * share
    wavenum = waves_ref[lax.axis_index("groups")]
    rows_scr[...] = jnp.zeros_like(rows_scr)
    for il in range(share):
        points_i = nodes_ref[first_cycle + il]
        points = jnp.full((1, both), points_i, jnp.int32).astype(f32)
        inverse = 1.0 / points
        resolved = 2.0 * wavenum < points

        def rows_of(count, scale):
            return (lax.broadcasted_iota(jnp.int32, (count, both), 0) * scale).astype(f32)

        coarse_c, coarse_s = cos_and_minus_sin(wavenum, points, rows_of(coarse_rows, lane_width), inverse)
        coarse_ref[il, 0] = jnp.where(resolved, coarse_c, 0.0)
        coarse_ref[il, 1] = jnp.where(resolved, coarse_s, 0.0)
        mid_c, mid_s = cos_and_minus_sin(wavenum, points, rows_of(lane_width // 8, 8), inverse)
        unit_c, unit_s = cos_and_minus_sin(wavenum, points, rows_of(8, 1), inverse)
        for g in range(lane_width // 16):
            pieces_c = []
            pieces_s = []
            for a in (2 * g, 2 * g + 1):
                step_c = mid_c[a : a + 1]
                step_s = mid_s[a : a + 1]
                pieces_c.append(step_c * unit_c - step_s * unit_s)
                pieces_s.append(step_c * unit_s + step_s * unit_c)
            fine_ref[il, 0, 16 * g : 16 * g + 16] = jnp.concatenate(pieces_c, 0).astype(bf16)
            fine_ref[il, 1, 16 * g : 16 * g + 16] = jnp.concatenate(pieces_s, 0).astype(bf16)
        panel = jnp.concatenate([fore_ref[il].astype(f32), targ_ref[il].astype(f32)], axis=0)
        column = lax.broadcasted_iota(jnp.int32, (panel_rows, extent), 1)
        panel = jnp.where(column < points_i, panel, 0.0)
        stacked = jnp.concatenate(
            [panel[:, lane_width * j : lane_width * (j + 1)] for j in range(steps)], axis=0
        ).astype(bf16)
        scale = 1.0 / jnp.sqrt(points[:, :half_lanes])
        for h in range(2):
            lanes = slice(h * half_lanes, (h + 1) * half_lanes)
            part_c = dot_nn(stacked, fine_ref[il, 0, :, lanes])
            part_s = dot_nn(stacked, fine_ref[il, 1, :, lanes])
            total_c = jnp.zeros((panel_rows, half_lanes), f32)
            total_s = jnp.zeros((panel_rows, half_lanes), f32)
            for j in range(steps):
                turn_c = coarse_ref[il, 0, j : j + 1, lanes]
                turn_s = coarse_ref[il, 1, j : j + 1, lanes]
                piece_c = part_c[j * panel_rows : (j + 1) * panel_rows]
                piece_s = part_s[j * panel_rows : (j + 1) * panel_rows]
                total_c = total_c + (turn_c * piece_c - turn_s * piece_s)
                total_s = total_s + (turn_c * piece_s + turn_s * piece_c)
            at = (il * 2 + h) * 2 * panel_rows
            rows_scr[at : at + panel_rows, :] = total_c * scale
            rows_scr[at + panel_rows : at + 2 * panel_rows, :] = total_s * scale
    wire_ref[...] = jnp.transpose(rows_scr[...]).astype(bf16)


def take_block(rows, index, width, lanes):
    if width % lane_width == 0:
        return rows[:, index * width : (index + 1) * width]
    total = rows.shape[1]
    if index > 0:
        rows = pltpu.roll(rows, total - index * width, 1)
    return rows[:, :lanes]


def join_blocks(blocks, width, total):
    if width % lane_width == 0:
        return jnp.concatenate(blocks, axis=1)
    joined = jnp.zeros((blocks[0].shape[0], total), f32)
    lane = lax.broadcasted_iota(jnp.int32, joined.shape, 1)
    for index, block in enumerate(blocks):
        wide = jnp.concatenate([block] * (total // block.shape[1]), axis=1)
        if index > 0:
            wide = pltpu.roll(wide, index * width, 1)
        here = (lane >= index * width) & (lane < (index + 1) * width)
        joined = jnp.where(here, wide, joined)
    return joined


def pair_tables(own, parts, row, q):
    return jnp.concatenate([own[row + q].astype(f32)] + [t[q].astype(f32) for t in parts], axis=0).astype(bf16)


def pair_sides(pair, slot, degree_count):
    low_side = slot < degree_count - pair
    low_weight = jnp.where(pair == 0, 1.0, 2.0)
    high_weight = jnp.where(2 * pair == degree_count - 1, 0.0, 2.0)
    return low_side, low_weight, high_weight


def project_kernel(groups, bands, owners, pairs_held, share, wire_ref, own_ref, *refs):
    remote = groups * (bands - 1)
    part_refs = refs[:remote]
    coef_ref, spectra_ref, flat_scr, left_scr, own_scr, own_sem = refs[remote:]
    sources, pairs_sub, _ = wire_ref.shape
    slot_count = own_ref.shape[2]
    degree_count = slot_count - 1
    panel_rows = coef_ref.shape[2]
    fields = panel_rows // 2
    block_rows = 4 * panel_rows
    pairs_part = pairs_sub // groups
    group = lax.axis_index("groups")
    band = lax.axis_index("band")
    first = lax.axis_index(owner_axes) * pairs_held + band * pairs_sub
    own_copy = pltpu.make_async_copy(own_ref.at[pl.ds(band * pairs_sub, pairs_sub)], own_scr, own_sem)
    own_copy.start()
    for k in range(bands):
        other = band ^ k
        for w in range(owners):
            at = (k * owners + w) * pairs_sub
            rows = wire_ref[other * owners + w].astype(f32)
            for c in range(flat_scr.shape[0]):
                flat_scr[c, at : at + pairs_sub, :] = rows[:, c * lane_width : (c + 1) * lane_width]
    own_copy.wait()
    slot = lax.broadcasted_iota(jnp.int32, (panel_rows, slot_count), 1)
    row = lax.broadcasted_iota(jnp.int32, (panel_rows, slot_count // 2), 0)
    zero = jnp.zeros((panel_rows, slot_count), f32)
    high_power, high_cross = zero, zero
    all_power, all_cross = zero, zero
    for j in range(groups):
        part_row = (group ^ j) * pairs_part
        low_power, low_cross = zero, zero
        for q in reversed(range(pairs_part)):
            place = j * pairs_part + q
            received = jnp.concatenate(
                [
                    flat_scr[c, pl.ds(place, sources, stride=pairs_sub), :]
                    for c in range(flat_scr.shape[0])
                ],
                axis=1,
            )
            for il in range(share):
                left_scr[place, pl.ds(il, sources, stride=share), :] = take_block(
                    received, il, block_rows, left_scr.shape[2]
                )
            left = left_scr[place, :, 0:block_rows].astype(bf16)
            both_halves = dot_tn(
                left, pair_tables(own_scr, part_refs[j * (bands - 1) : (j + 1) * (bands - 1)], part_row, q)
            )
            pair = first + part_row + q
            low_side, low_weight, high_weight = pair_sides(pair, slot, degree_count)
            cosines = jnp.where(
                low_side, both_halves[0:panel_rows], both_halves[2 * panel_rows : 3 * panel_rows]
            )
            sines = jnp.where(
                low_side, both_halves[panel_rows : 2 * panel_rows], both_halves[3 * panel_rows :]
            )
            coef_ref[place, 0] = cosines
            coef_ref[place, 1] = sines
            weight = jnp.where(low_side, low_weight, high_weight)
            power = (cosines * cosines + sines * sines) * weight
            cross = (
                cosines * pltpu.roll(cosines, fields, 0) + sines * pltpu.roll(sines, fields, 0)
            ) * weight
            low_power = pltpu.roll(low_power, 1, 1) + jnp.where(low_side, power, 0.0)
            low_cross = pltpu.roll(low_cross, 1, 1) + jnp.where(low_side, cross, 0.0)
            high_power = high_power + jnp.where(low_side, 0.0, power)
            high_cross = high_cross + jnp.where(low_side, 0.0, cross)
        all_power = all_power + pltpu.roll(low_power, first + part_row, 1)
        all_cross = all_cross + pltpu.roll(low_cross, first + part_row, 1)
    all_power = all_power + pltpu.roll(high_power, slot_count - 1, 1)
    all_cross = all_cross + pltpu.roll(high_cross, slot_count - 1, 1)
    spectra_ref[:, 0:slot_count] = all_power
    spectra_ref[:, slot_count:] = jnp.where(
        row < fields, all_cross[:, : slot_count // 2], all_cross[:, slot_count // 2 :]
    )


def tree_sum(parts):
    while len(parts) > 1:
        parts = [parts[i] + parts[i + 1] for i in range(0, len(parts), 2)]
    return parts[0]


def gradient_kernel(groups, bands, owners, pairs_held, share, spectra_parts, own_ref, coef_ref, *refs):
    remote = groups * (bands - 1)
    spectra_refs = refs[:spectra_parts]
    part_refs = refs[spectra_parts : spectra_parts + remote]
    wire_ref, misfit_ref, flat_scr, cycle_scr, own_scr, own_sem = refs[spectra_parts + remote :]
    sources, pairs_sub, _ = wire_ref.shape
    slot_count = own_ref.shape[2]
    degree_count = slot_count - 1
    panel_rows = coef_ref.shape[2]
    fields = panel_rows // 2
    block_rows = 4 * panel_rows
    fields_out = fields // bands
    pairs_part = pairs_sub // groups
    group = lax.axis_index("groups")
    band = lax.axis_index("band")
    first = lax.axis_index(owner_axes) * pairs_held + band * pairs_sub
    own_copy = pltpu.make_async_copy(own_ref.at[pl.ds(band * pairs_sub, pairs_sub)], own_scr, own_sem)
    own_copy.start()
    if block_rows < cycle_scr.shape[2]:
        cycle_scr[...] = jnp.zeros_like(cycle_scr)
    slot = lax.broadcasted_iota(jnp.int32, (panel_rows, slot_count), 1)
    row = lax.broadcasted_iota(jnp.int32, (panel_rows, slot_count), 0)
    spectra = tree_sum([s[...] for s in spectra_refs])
    power = spectra[:, :slot_count]
    packed = spectra[:, slot_count:]
    turned = pltpu.roll(packed, fields, 0)
    upper = row[:, : slot_count // 2] < fields
    cross = jnp.concatenate([jnp.where(upper, packed, turned), jnp.where(upper, turned, packed)], axis=1)
    odd_weight = (2 * slot + 1).astype(f32)
    power = power / odd_weight + spectrum_floor
    cross = cross / odd_weight
    root = jnp.sqrt(power)
    other_root = pltpu.roll(root, fields, 0)
    both_power = power + pltpu.roll(power, fields, 0)
    geo_mean = root * other_root
    coherence = cross / geo_mean
    term = (root - other_root) * (root - other_root) + both_power * (1.0 - coherence)
    term = jnp.where(slot < degree_count, term, 0.0)
    mean = jnp.sum(term, axis=1, keepdims=True) / degree_count
    field_row = lax.broadcasted_iota(jnp.int32, (panel_rows, 1), 0)
    misfit_ref[...] = jnp.zeros_like(misfit_ref)
    for i in range(fields_out):
        chosen = jnp.where(field_row == band * fields_out + i, mean, 0.0)
        misfit_ref[i : i + 1, :] = jnp.broadcast_to(
            jnp.sum(chosen, axis=0, keepdims=True), (1, lane_width)
        )
    grad_power = (
        gradient_gain
        * (
            1.0
            - other_root / root
            + (1.0 - coherence)
            + both_power * coherence / (2.0 * power)
        )
        / odd_weight
    )
    grad_cross = -gradient_gain * both_power / geo_mean / odd_weight
    by_degree = jnp.where(row < fields, 2.0 * grad_power, grad_cross)
    high_grad = pltpu.roll(by_degree, 1, 1)
    own_copy.wait()
    for j in range(groups):
        part_row = (group ^ j) * pairs_part
        low_grad = pltpu.roll(by_degree, slot_count - first - part_row, 1)
        for q in range(pairs_part):
            place = j * pairs_part + q
            pair = first + part_row + q
            low_side, low_weight, high_weight = pair_sides(pair, slot, degree_count)
            gain = jnp.where(low_side, low_grad * low_weight, high_grad * high_weight)
            cosines = coef_ref[place, 0] * gain
            sines = coef_ref[place, 1] * gain
            cosines = cosines + pltpu.roll(cosines, fields, 0)
            sines = sines + pltpu.roll(sines, fields, 0)
            masked = jnp.concatenate(
                [
                    jnp.where(low_side, cosines, 0.0),
                    jnp.where(low_side, sines, 0.0),
                    jnp.where(low_side, 0.0, cosines),
                    jnp.where(low_side, 0.0, sines),
                ],
                axis=0,
            ).astype(bf16)
            cycle_scr[place, :, 0:block_rows] = dot_nt(
                pair_tables(own_scr, part_refs[j * (bands - 1) : (j + 1) * (bands - 1)], part_row, q), masked
            )
            joined = join_blocks(
                [cycle_scr[place, pl.ds(il, sources, stride=share), :] for il in range(share)],
                block_rows,
                flat_scr.shape[0] * lane_width,
            )
            for c in range(flat_scr.shape[0]):
                flat_scr[c, pl.ds(place, sources, stride=pairs_sub), :] = joined[
                    :, c * lane_width : (c + 1) * lane_width
                ]
            low_grad = pltpu.roll(low_grad, slot_count - 1, 1)
    for k in range(bands):
        other = band ^ k
        for w in range(owners):
            at = (k * owners + w) * pairs_sub
            wire_ref[other * owners + w] = jnp.concatenate(
                [flat_scr[c, at : at + pairs_sub, :] for c in range(flat_scr.shape[0])], axis=1
            ).astype(bf16)


def synthesise_kernel(nodes_ref, coarse_ref, fine_ref, wire_ref, out_ref):
    share, fields, extent = out_ref.shape
    steps = extent // lane_width
    half_lanes = coarse_ref.shape[3] // 2
    panel_rows = 2 * fields
    first_cycle = lax.axis_index(group_axes) * share
    values = jnp.transpose(wire_ref[...].astype(f32))
    column = lax.broadcasted_iota(jnp.int32, (fields, lane_width), 1)
    for il in range(share):
        points_i = nodes_ref[first_cycle + il]
        total = jnp.zeros((steps * panel_rows, lane_width), f32)
        for h in range(2):
            lanes = slice(h * half_lanes, (h + 1) * half_lanes)
            at = (il * 2 + h) * 2 * panel_rows
            cosines = values[at : at + panel_rows]
            sines = values[at + panel_rows : at + 2 * panel_rows]
            turned_c = []
            turned_s = []
            for j in range(steps):
                turn_c = coarse_ref[il, 0, j : j + 1, lanes]
                turn_s = coarse_ref[il, 1, j : j + 1, lanes]
                turned_c.append(cosines * turn_c + sines * turn_s)
                turned_s.append(sines * turn_c - cosines * turn_s)
            total = total + dot_nt(
                jnp.concatenate(turned_c, 0).astype(bf16), fine_ref[il, 0, :, lanes]
            )
            total = total + dot_nt(
                jnp.concatenate(turned_s, 0).astype(bf16), fine_ref[il, 1, :, lanes]
            )
        points = jnp.full((1, lane_width), points_i, jnp.int32).astype(f32)
        scale = 1.0 / jnp.sqrt(points)
        for j in range(steps):
            piece = total[j * panel_rows : j * panel_rows + fields] * scale
            piece = jnp.where(column + j * lane_width < points_i, piece, 0.0)
            out_ref[il, :, lane_width * j : lane_width * (j + 1)] = piece.astype(bf16)


def call(body, name, arrays, spaces, out_shapes, scratch):
    return pl.pallas_call(
        body,
        name=name,
        in_specs=[pl.BlockSpec(memory_space=space) for space in spaces],
        out_specs=tuple(pl.BlockSpec(memory_space=pltpu.VMEM) for _ in out_shapes),
        out_shape=tuple(out_shapes),
        scratch_shapes=scratch,
        compiler_params=pltpu.CompilerParams(vmem_limit_bytes=vmem_bytes),
    )(*arrays)


def exchange(array, axes, count):
    return [array] + [
        lax.ppermute(array, axes, [(i, i ^ k) for i in range(count)]) for k in range(1, count)
    ]


def per_device(predicted_state, analysis_state, nodes_per_parallel, weighted_harmonic_table):
    share, fields, extent = predicted_state.shape
    pairs_held, cycle_band, slot_count = weighted_harmonic_table.shape
    groups = lax.axis_size("groups")
    bands = lax.axis_size("band")
    owners = lax.axis_size(owner_axes)
    group = lax.axis_index("groups")
    band = lax.axis_index("band")
    sources = bands * owners
    pairs_part = -(-pairs_held // (bands * groups))
    pairs_sub = groups * pairs_part
    panel_rows = 2 * fields
    wire_lanes = round_up(share * 4 * panel_rows, lane_width)
    block_lanes = round_up(4 * panel_rows, lane_width)
    half_lanes = sources * pairs_sub
    coarse_rows = round_up(extent // lane_width, 8)

    table = weighted_harmonic_table
    if pairs_sub * bands != pairs_held:
        table = jnp.pad(table, ((0, pairs_sub * bands - pairs_held), (0, 0), (0, 0)))
    pieces = [
        lax.dynamic_slice_in_dim(table, (band ^ k) * pairs_sub + group * pairs_part, pairs_part, 0)
        for k in range(1, bands)
    ]
    own_parts = [
        lax.ppermute(piece, "band", [(i, i ^ (k + 1)) for i in range(bands)])
        for k, piece in enumerate(pieces)
    ]
    parts = list(own_parts)
    for j in range(1, groups):
        parts += [lax.ppermute(p, "groups", [(i, i ^ j) for i in range(groups)]) for p in own_parts]

    waves = lane_wavenumbers(groups, bands, owners, pairs_held, pairs_part, slot_count - 1)
    wire, coarse, fine = call(
        analyse_kernel,
        "analyse",
        (nodes_per_parallel, jnp.asarray(waves), predicted_state, analysis_state),
        (pltpu.SMEM, pltpu.VMEM, pltpu.VMEM, pltpu.VMEM),
        (
            jax.ShapeDtypeStruct((half_lanes, wire_lanes), bf16),
            jax.ShapeDtypeStruct((share, 2, coarse_rows, 2 * half_lanes), f32),
            jax.ShapeDtypeStruct((share, 2, lane_width, 2 * half_lanes), bf16),
        ),
        [pltpu.VMEM((wire_lanes, half_lanes), f32)],
    )
    wire = lax.all_to_all(
        wire.reshape(sources, pairs_sub, wire_lanes), group_axes, 0, 0, tiled=True
    )
    scratch = [
        pltpu.VMEM((wire_lanes // lane_width, sources * pairs_sub, lane_width), f32),
        pltpu.VMEM((pairs_sub, bands * cycle_band, block_lanes), f32),
        pltpu.VMEM((pairs_sub, cycle_band, slot_count), bf16),
        pltpu.SemaphoreType.DMA,
    ]
    coef, spectra = call(
        functools.partial(project_kernel, groups, bands, owners, pairs_held, share),
        "project",
        (wire, table, *parts),
        (pltpu.VMEM, pl.ANY) + (pltpu.VMEM,) * len(parts),
        (
            jax.ShapeDtypeStruct((pairs_sub, 2, panel_rows, slot_count), f32),
            jax.ShapeDtypeStruct((panel_rows, slot_count + slot_count // 2), f32),
        ),
        scratch,
    )
    spectra = tree_sum(exchange(spectra, owner_axes, owners))
    spectra = exchange(spectra, "band", bands)
    wire, misfit = call(
        functools.partial(gradient_kernel, groups, bands, owners, pairs_held, share, len(spectra)),
        "gradient",
        (table, coef, *spectra, *parts),
        (pl.ANY,) + (pltpu.VMEM,) * (1 + len(spectra) + len(parts)),
        (
            jax.ShapeDtypeStruct((sources, pairs_sub, wire_lanes), bf16),
            jax.ShapeDtypeStruct((round_up(fields // bands, 8), lane_width), f32),
        ),
        scratch,
    )
    wire = lax.all_to_all(wire, group_axes, 0, 0, tiled=True)
    (sensitivity,) = call(
        synthesise_kernel,
        "synthesise",
        (nodes_per_parallel, coarse, fine, wire.reshape(half_lanes, wire_lanes)),
        (pltpu.SMEM, pltpu.VMEM, pltpu.VMEM, pltpu.VMEM),
        (jax.ShapeDtypeStruct((share, fields, extent), bf16),),
        [],
    )
    return misfit[: fields // bands, 0], sensitivity


def solution(mesh):
    in_specs = (
        P(("groups", "band", "field", "wave"), None, None),
        P(("groups", "band", "field", "wave"), None, None),
        P(),
        P(("field", "wave"), "band", None),
    )
    out_specs = (P(("groups", "band")), P(("groups", "band", "field", "wave"), None, None))
    return jax.shard_map(
        per_device, mesh=mesh, in_specs=in_specs, out_specs=out_specs, check_vma=False
    )
```

```python
import functools
import math

import jax
import jax.numpy as jnp
from jax import lax
from jax.experimental import pallas as pl
from jax.experimental.pallas import tpu as pltpu
from jax.sharding import PartitionSpec as P

spectrum_floor = 0.25
gradient_gain = 16.0
lane_width = 128
vmem_bytes = 40 * 1024 * 1024
owner_axes = ("field", "wave")
group_axes = ("band", "field", "wave")
bf16 = jnp.bfloat16
f32 = jnp.float32


def round_up(value, step):
    return -(-value // step) * step


def dot_nn(left, right):
    return lax.dot_general(left, right, (((1,), (0,)), ((), ())), preferred_element_type=f32)


def dot_nt(left, right):
    return lax.dot_general(left, right, (((1,), (1,)), ((), ())), preferred_element_type=f32)


def dot_tn(left, right):
    return lax.dot_general(left, right, (((0,), (0,)), ((), ())), preferred_element_type=f32)


def split_index(index, size):
    whole = jnp.floor((index + 0.5) * (1.0 / size))
    return whole, index - whole * size


def wavenumbers(owner, band, half, rest, pairs_held, pairs_part, groups, degree_count):
    part, pair = split_index(rest, pairs_part)
    part = (lax.axis_index("groups") ^ part.astype(jnp.int32)).astype(f32)
    within = (band * groups + part) * pairs_part + pair
    pair = owner * pairs_held + within
    mirrored = degree_count - 1.0 - pair
    wavenum = jnp.where(half > 0.0, mirrored, pair)
    void = (within >= pairs_held) | ((half > 0.0) & (mirrored == pair))
    return jnp.where(void, 4.0 * degree_count, wavenum)


def own_wavenumbers(lanes, owners, pairs_held, pairs_part, groups, degree_count):
    index = lax.broadcasted_iota(jnp.int32, (1, lanes), 1).astype(f32)
    half, index = split_index(index, lanes // 2)
    block, rest = split_index(index, groups * pairs_part)
    band, owner = split_index(block, owners)
    return wavenumbers(owner, band, half, rest, pairs_held, pairs_part, groups, degree_count)


def cos_and_minus_sin(wavenum, points, columns, inverse):
    quarters = (4.0 * wavenum) * columns
    turns = jnp.floor(quarters * inverse + 0.5)
    angle = (quarters - turns * points) * (0.5 * math.pi * inverse)
    square = angle * angle
    sine = angle * (1.0 + square * (-1.0 / 6 + square * (1.0 / 120 + square * (-1.0 / 5040))))
    cosine = 1.0 + square * (
        -0.5 + square * (1.0 / 24 + square * (-1.0 / 720 + square * (1.0 / 40320)))
    )
    quadrant = turns.astype(jnp.int32)
    swap = (quadrant & 1) != 0
    new_cos = jnp.where(swap, sine, cosine)
    new_sin = jnp.where(swap, cosine, sine)
    new_cos = jnp.where(((quadrant + 1) & 2) != 0, -new_cos, new_cos)
    new_sin = jnp.where((quadrant & 2) != 0, new_sin, -new_sin)
    return new_cos, new_sin


def fill_tables(points_i, wavenum, coarse_ref, fine_ref, at):
    lanes = wavenum.shape[1]
    points = jnp.full((1, lanes), points_i, jnp.int32).astype(f32)
    inverse = 1.0 / points
    scale = jnp.where(2.0 * wavenum < points, 1.0 / jnp.sqrt(points), 0.0)

    def rows_of(count, step):
        return (lax.broadcasted_iota(jnp.int32, (count, lanes), 0) * step).astype(f32)

    coarse_rows = coarse_ref.shape[2]
    coarse_c, coarse_s = cos_and_minus_sin(wavenum, points, rows_of(coarse_rows, lane_width), inverse)
    coarse_ref[at, 0] = coarse_c * scale
    coarse_ref[at, 1] = coarse_s * scale
    mid_c, mid_s = cos_and_minus_sin(wavenum, points, rows_of(lane_width // 8, 8), inverse)
    unit_c, unit_s = cos_and_minus_sin(wavenum, points, rows_of(8, 1), inverse)
    for g in range(lane_width // 16):
        pieces_c = []
        pieces_s = []
        for a in (2 * g, 2 * g + 1):
            step_c = mid_c[a : a + 1]
            step_s = mid_s[a : a + 1]
            pieces_c.append(step_c * unit_c - step_s * unit_s)
            pieces_s.append(step_c * unit_s + step_s * unit_c)
        fine_ref[at, 0, 16 * g : 16 * g + 16] = jnp.concatenate(pieces_c, 0).astype(bf16)
        fine_ref[at, 1, 16 * g : 16 * g + 16] = jnp.concatenate(pieces_s, 0).astype(bf16)


def analyse_kernel(
    groups,
    owners,
    pairs_held,
    pairs_part,
    degree_count,
    nodes_ref,
    states_ref,
    wire_ref,
    coarse_ref,
    fine_ref,
    mask_ref,
    rows_scr,
):
    share, panel_rows, extent = states_ref.shape
    steps = extent // lane_width
    half_lanes = coarse_ref.shape[3] // 2
    first_cycle = lax.axis_index(group_axes) * share
    column = lax.broadcasted_iota(jnp.int32, (1, extent), 1)
    wavenum = own_wavenumbers(
        2 * half_lanes, owners, pairs_held, pairs_part, groups, degree_count
    )
    if share * 4 * panel_rows < rows_scr.shape[0]:
        rows_scr[share * 4 * panel_rows :, :] = jnp.zeros_like(rows_scr[share * 4 * panel_rows :, :])
    for il in range(share):
        points_i = nodes_ref[first_cycle + il]
        fill_tables(points_i, wavenum, coarse_ref, fine_ref, il)
        held = column < points_i
        mask_ref[il : il + 1, :] = held.astype(f32)
        panel = jnp.where(held, states_ref[il].astype(f32), 0.0)
        stacked = jnp.concatenate(
            [panel[:, lane_width * j : lane_width * (j + 1)] for j in range(steps)], axis=0
        ).astype(bf16)
        for h in range(2):
            lanes = slice(h * half_lanes, (h + 1) * half_lanes)
            part_c = dot_nn(stacked, fine_ref[il, 0, :, lanes])
            part_s = dot_nn(stacked, fine_ref[il, 1, :, lanes])
            total_c = jnp.zeros((panel_rows, half_lanes), f32)
            total_s = jnp.zeros((panel_rows, half_lanes), f32)
            for j in range(steps):
                turn_c = coarse_ref[il, 0, j : j + 1, lanes]
                turn_s = coarse_ref[il, 1, j : j + 1, lanes]
                piece_c = part_c[j * panel_rows : (j + 1) * panel_rows]
                piece_s = part_s[j * panel_rows : (j + 1) * panel_rows]
                total_c = total_c + (turn_c * piece_c - turn_s * piece_s)
                total_s = total_s + (turn_c * piece_s + turn_s * piece_c)
            at = (il * 2 + h) * 2 * panel_rows
            rows_scr[at : at + panel_rows, :] = total_c
            rows_scr[at + panel_rows : at + 2 * panel_rows, :] = total_s
    wire_ref[...] = jnp.transpose(rows_scr[...]).astype(bf16)


def take_block(rows, index, width, lanes):
    if width % lane_width == 0:
        return rows[:, index * width : (index + 1) * width]
    total = rows.shape[1]
    if index > 0:
        rows = pltpu.roll(rows, total - index * width, 1)
    return rows[:, :lanes]


def join_blocks(blocks, width, total):
    if width % lane_width == 0:
        return jnp.concatenate(blocks, axis=1)
    joined = jnp.zeros((blocks[0].shape[0], total), f32)
    lane = lax.broadcasted_iota(jnp.int32, joined.shape, 1)
    for index, block in enumerate(blocks):
        wide = jnp.concatenate([block] * (total // block.shape[1]), axis=1)
        if index > 0:
            wide = pltpu.roll(wide, index * width, 1)
        here = (lane >= index * width) & (lane < (index + 1) * width)
        joined = jnp.where(here, wide, joined)
    return joined


def pair_tables(own, parts, groups, j, row, q):
    blocks = [own[row + q], parts[0][row + q]] + [t[q] for t in parts[1 + j :: groups]]
    return jnp.concatenate([b.astype(f32) for b in blocks], axis=0).astype(bf16)


def pair_sides(pair, slot, degree_count):
    low_side = slot < degree_count - pair
    low_weight = jnp.where(pair == 0, 1.0, 2.0)
    high_weight = jnp.where(2 * pair == degree_count - 1, 0.0, 2.0)
    return low_side, low_weight, high_weight


def project_kernel(groups, bands, owners, pairs_held, share, wire_ref, own_ref, *refs):
    remote = 1 + groups * (bands - 2)
    part_refs = refs[:remote]
    coef_ref, spectra_ref, flat_scr, left_scr = refs[remote:]
    sources, pairs_sub, _ = wire_ref.shape
    slot_count = own_ref.shape[2]
    degree_count = slot_count - 1
    panel_rows = coef_ref.shape[2]
    fields = panel_rows // 2
    block_rows = 4 * panel_rows
    pairs_part = pairs_sub // groups
    group = lax.axis_index("groups")
    band = lax.axis_index("band")
    first = lax.axis_index(owner_axes) * pairs_held + band * pairs_sub
    for k in range(bands):
        other = band ^ k
        for w in range(owners):
            at = (k * owners + w) * pairs_sub
            rows = wire_ref[other * owners + w].astype(f32)
            for c in range(flat_scr.shape[0]):
                flat_scr[c, at : at + pairs_sub, :] = rows[:, c * lane_width : (c + 1) * lane_width]
    slot = lax.broadcasted_iota(jnp.int32, (panel_rows, slot_count), 1)
    row = lax.broadcasted_iota(jnp.int32, (panel_rows, slot_count // 2), 0)
    zero = jnp.zeros((panel_rows, slot_count), f32)
    high_power, high_cross = zero, zero
    all_power, all_cross = zero, zero
    for j in range(groups):
        part_row = (group ^ j) * pairs_part
        low_power, low_cross = zero, zero
        for q in reversed(range(pairs_part)):
            place = j * pairs_part + q
            received = jnp.concatenate(
                [
                    flat_scr[c, pl.ds(place, sources, stride=pairs_sub), :]
                    for c in range(flat_scr.shape[0])
                ],
                axis=1,
            )
            for il in range(share):
                left_scr[place, pl.ds(il, sources, stride=share), :] = take_block(
                    received, il, block_rows, left_scr.shape[2]
                )
            left = left_scr[place, :, 0:block_rows].astype(bf16)
            both_halves = dot_tn(
                left, pair_tables(own_ref, part_refs, groups, j, part_row, q)
            )
            pair = first + part_row + q
            low_side, low_weight, high_weight = pair_sides(pair, slot, degree_count)
            cosines = jnp.where(
                low_side, both_halves[0:panel_rows], both_halves[2 * panel_rows : 3 * panel_rows]
            )
            sines = jnp.where(
                low_side, both_halves[panel_rows : 2 * panel_rows], both_halves[3 * panel_rows :]
            )
            coef_ref[place, 0] = cosines
            coef_ref[place, 1] = sines
            weight = jnp.where(low_side, low_weight, high_weight)
            power = (cosines * cosines + sines * sines) * weight
            cross = (
                cosines * pltpu.roll(cosines, fields, 0) + sines * pltpu.roll(sines, fields, 0)
            ) * weight
            low_power = pltpu.roll(low_power, 1, 1) + jnp.where(low_side, power, 0.0)
            low_cross = pltpu.roll(low_cross, 1, 1) + jnp.where(low_side, cross, 0.0)
            high_power = high_power + jnp.where(low_side, 0.0, power)
            high_cross = high_cross + jnp.where(low_side, 0.0, cross)
        all_power = all_power + pltpu.roll(low_power, first + part_row, 1)
        all_cross = all_cross + pltpu.roll(low_cross, first + part_row, 1)
    all_power = all_power + pltpu.roll(high_power, slot_count - 1, 1)
    all_cross = all_cross + pltpu.roll(high_cross, slot_count - 1, 1)
    spectra_ref[:, 0:slot_count] = all_power
    spectra_ref[:, slot_count:] = jnp.where(
        row < fields, all_cross[:, : slot_count // 2], all_cross[:, slot_count // 2 :]
    )


def tree_sum(parts):
    while len(parts) > 1:
        parts = [parts[i] + parts[i + 1] for i in range(0, len(parts), 2)]
    return parts[0]


def gradient_kernel(groups, bands, owners, pairs_held, share, spectra_parts, own_ref, coef_ref, *refs):
    remote = 1 + groups * (bands - 2)
    spectra_refs = refs[:spectra_parts]
    part_refs = refs[spectra_parts : spectra_parts + remote]
    wire_ref, misfit_ref, flat_scr, cycle_scr = refs[spectra_parts + remote :]
    sources, pairs_sub, _ = wire_ref.shape
    slot_count = own_ref.shape[2]
    degree_count = slot_count - 1
    panel_rows = coef_ref.shape[2]
    fields = panel_rows // 2
    block_rows = 4 * panel_rows
    fields_out = fields // bands
    pairs_part = pairs_sub // groups
    group = lax.axis_index("groups")
    band = lax.axis_index("band")
    first = lax.axis_index(owner_axes) * pairs_held + band * pairs_sub
    if block_rows < cycle_scr.shape[2]:
        cycle_scr[...] = jnp.zeros_like(cycle_scr)
    slot = lax.broadcasted_iota(jnp.int32, (panel_rows, slot_count), 1)
    row = lax.broadcasted_iota(jnp.int32, (panel_rows, slot_count), 0)
    spectra = tree_sum([s[...] for s in spectra_refs])
    power = spectra[:, :slot_count]
    packed = spectra[:, slot_count:]
    turned = pltpu.roll(packed, fields, 0)
    upper = row[:, : slot_count // 2] < fields
    cross = jnp.concatenate([jnp.where(upper, packed, turned), jnp.where(upper, turned, packed)], axis=1)
    odd_weight = (2 * slot + 1).astype(f32)
    power = power / odd_weight + spectrum_floor
    cross = cross / odd_weight
    root = jnp.sqrt(power)
    other_root = pltpu.roll(root, fields, 0)
    both_power = power + pltpu.roll(power, fields, 0)
    geo_mean = root * other_root
    coherence = cross / geo_mean
    term = (root - other_root) * (root - other_root) + both_power * (1.0 - coherence)
    term = jnp.where(slot < degree_count, term, 0.0)
    mean = jnp.sum(term, axis=1, keepdims=True) / degree_count
    field_row = lax.broadcasted_iota(jnp.int32, (panel_rows, 1), 0)
    misfit_ref[...] = jnp.zeros_like(misfit_ref)
    for i in range(fields_out):
        chosen = jnp.where(field_row == band * fields_out + i, mean, 0.0)
        misfit_ref[i : i + 1, :] = jnp.broadcast_to(
            jnp.sum(chosen, axis=0, keepdims=True), (1, lane_width)
        )
    grad_power = (
        gradient_gain
        * (
            1.0
            - other_root / root
            + (1.0 - coherence)
            + both_power * coherence / (2.0 * power)
        )
        / odd_weight
    )
    grad_cross = -gradient_gain * both_power / geo_mean / odd_weight
    by_degree = jnp.where(row < fields, 2.0 * grad_power, grad_cross)
    high_grad = pltpu.roll(by_degree, 1, 1)
    for j in range(groups):
        part_row = (group ^ j) * pairs_part
        low_grad = pltpu.roll(by_degree, slot_count - first - part_row, 1)
        for q in range(pairs_part):
            place = j * pairs_part + q
            pair = first + part_row + q
            low_side, low_weight, high_weight = pair_sides(pair, slot, degree_count)
            gain = jnp.where(low_side, low_grad * low_weight, high_grad * high_weight)
            cosines = coef_ref[place, 0] * gain
            sines = coef_ref[place, 1] * gain
            cosines = cosines + pltpu.roll(cosines, fields, 0)
            sines = sines + pltpu.roll(sines, fields, 0)
            masked = jnp.concatenate(
                [
                    jnp.where(low_side, cosines, 0.0),
                    jnp.where(low_side, sines, 0.0),
                    jnp.where(low_side, 0.0, cosines),
                    jnp.where(low_side, 0.0, sines),
                ],
                axis=0,
            ).astype(bf16)
            cycle_scr[place, :, 0:block_rows] = dot_nt(
                pair_tables(own_ref, part_refs, groups, j, part_row, q), masked
            )
            joined = join_blocks(
                [cycle_scr[place, pl.ds(il, sources, stride=share), :] for il in range(share)],
                block_rows,
                flat_scr.shape[0] * lane_width,
            )
            for c in range(flat_scr.shape[0]):
                flat_scr[c, pl.ds(place, sources, stride=pairs_sub), :] = joined[
                    :, c * lane_width : (c + 1) * lane_width
                ]
            low_grad = pltpu.roll(low_grad, slot_count - 1, 1)
    for k in range(bands):
        other = band ^ k
        for w in range(owners):
            at = (k * owners + w) * pairs_sub
            wire_ref[other * owners + w] = jnp.concatenate(
                [flat_scr[c, at : at + pairs_sub, :] for c in range(flat_scr.shape[0])], axis=1
            ).astype(bf16)


def synthesise_kernel(coarse_ref, fine_ref, mask_ref, wire_ref, out_ref):
    share, fields, extent = out_ref.shape
    steps = extent // lane_width
    half_lanes = coarse_ref.shape[3] // 2
    panel_rows = 2 * fields
    values = jnp.transpose(wire_ref[...].astype(f32))
    for il in range(share):
        total = jnp.zeros((steps * panel_rows, lane_width), f32)
        for h in range(2):
            lanes = slice(h * half_lanes, (h + 1) * half_lanes)
            at = (il * 2 + h) * 2 * panel_rows
            cosines = values[at : at + panel_rows]
            sines = values[at + panel_rows : at + 2 * panel_rows]
            turned_c = []
            turned_s = []
            for j in range(steps):
                turn_c = coarse_ref[il, 0, j : j + 1, lanes]
                turn_s = coarse_ref[il, 1, j : j + 1, lanes]
                turned_c.append(cosines * turn_c + sines * turn_s)
                turned_s.append(sines * turn_c - cosines * turn_s)
            total = total + dot_nt(
                jnp.concatenate(turned_c, 0).astype(bf16), fine_ref[il, 0, :, lanes]
            )
            total = total + dot_nt(
                jnp.concatenate(turned_s, 0).astype(bf16), fine_ref[il, 1, :, lanes]
            )
        mask = mask_ref[il : il + 1, :]
        for j in range(steps):
            lanes = slice(lane_width * j, lane_width * (j + 1))
            piece = total[j * panel_rows : j * panel_rows + fields] * mask[:, lanes]
            out_ref[il, :, lanes] = piece.astype(bf16)


def call(body, name, arrays, spaces, out_shapes, scratch, flops=1):
    return pl.pallas_call(
        body,
        name=name,
        cost_estimate=pl.CostEstimate(flops=flops, transcendentals=0, bytes_accessed=1),
        in_specs=[pl.BlockSpec(memory_space=space) for space in spaces],
        out_specs=tuple(pl.BlockSpec(memory_space=pltpu.VMEM) for _ in out_shapes),
        out_shape=tuple(out_shapes),
        scratch_shapes=scratch,
        compiler_params=pltpu.CompilerParams(vmem_limit_bytes=vmem_bytes),
    )(*arrays)


def exchange(array, axes, count):
    return [array] + [
        lax.ppermute(array, axes, [(i, i ^ k) for i in range(count)]) for k in range(1, count)
    ]


def per_device(predicted_state, analysis_state, nodes_per_parallel, weighted_harmonic_table):
    share, fields, extent = predicted_state.shape
    pairs_held, cycle_band, slot_count = weighted_harmonic_table.shape
    groups = lax.axis_size("groups")
    bands = lax.axis_size("band")
    owners = lax.axis_size(owner_axes)
    group = lax.axis_index("groups")
    band = lax.axis_index("band")
    sources = bands * owners
    pairs_part = -(-pairs_held // (bands * groups))
    pairs_sub = groups * pairs_part
    panel_rows = 2 * fields
    wire_lanes = round_up(share * 4 * panel_rows, lane_width)
    block_lanes = round_up(4 * panel_rows, lane_width)
    half_lanes = sources * pairs_sub
    coarse_rows = round_up(extent // lane_width, 8)

    table = weighted_harmonic_table
    if pairs_sub * bands != pairs_held:
        table = jnp.pad(table, ((0, pairs_sub * bands - pairs_held), (0, 0), (0, 0)))
    own_table = lax.dynamic_slice_in_dim(table, band * pairs_sub, pairs_sub, 0)

    def over_bands(array, k):
        return lax.ppermute(array, "band", [(i, i ^ k) for i in range(bands)])

    starts = [(band ^ k) * pairs_sub + group * pairs_part for k in range(bands)]
    far = [lax.dynamic_slice_in_dim(table, starts[k], pairs_part, 0) for k in range(2, bands)]
    near = lax.dynamic_slice_in_dim(table, (band ^ 1) * pairs_sub, pairs_sub, 0)
    near = over_bands(near, 1)
    far = [None, None] + [over_bands(piece, k + 2) for k, piece in enumerate(far)]
    states = jnp.concatenate([predicted_state, analysis_state], axis=1)
    wire, coarse, fine, mask = call(
        functools.partial(
            analyse_kernel, groups, owners, pairs_held, pairs_part, slot_count - 1
        ),
        "analyse",
        (nodes_per_parallel, states),
        (pltpu.SMEM, pltpu.VMEM),
        (
            jax.ShapeDtypeStruct((half_lanes, wire_lanes), bf16),
            jax.ShapeDtypeStruct((share, 2, coarse_rows, 2 * half_lanes), f32),
            jax.ShapeDtypeStruct((share, 2, lane_width, 2 * half_lanes), bf16),
            jax.ShapeDtypeStruct((share, extent), f32),
        ),
        [pltpu.VMEM((wire_lanes, half_lanes), f32)],
    )
    wire = lax.all_to_all(
        wire.reshape(sources, pairs_sub, wire_lanes), group_axes, 0, 0, tiled=True
    )
    parts = [near]
    for piece in far[2:]:
        parts.append(piece)
        for j in range(1, groups):
            parts.append(lax.ppermute(piece, "groups", [(i, i ^ j) for i in range(groups)]))
    scratch = [
        pltpu.VMEM((wire_lanes // lane_width, sources * pairs_sub, lane_width), f32),
        pltpu.VMEM((pairs_sub, bands * cycle_band, block_lanes), f32),
    ]
    coef, spectra = call(
        functools.partial(project_kernel, groups, bands, owners, pairs_held, share),
        "project",
        (wire, own_table, *parts),
        (pltpu.VMEM,) * (2 + len(parts)),
        (
            jax.ShapeDtypeStruct((pairs_sub, 2, panel_rows, slot_count), f32),
            jax.ShapeDtypeStruct((panel_rows, slot_count + slot_count // 2), f32),
        ),
        scratch,
    )
    spectra = tree_sum(exchange(spectra, owner_axes, owners))
    spectra = exchange(spectra, "band", bands)
    wire, misfit = call(
        functools.partial(gradient_kernel, groups, bands, owners, pairs_held, share, len(spectra)),
        "gradient",
        (own_table, coef, *spectra, *parts),
        (pltpu.VMEM,) * (2 + len(spectra) + len(parts)),
        (
            jax.ShapeDtypeStruct((sources, pairs_sub, wire_lanes), bf16),
            jax.ShapeDtypeStruct((round_up(fields // bands, 8), lane_width), f32),
        ),
        scratch,
    )
    wire = lax.all_to_all(wire, group_axes, 0, 0, tiled=True)
    (sensitivity,) = call(
        synthesise_kernel,
        "synthesise",
        (coarse, fine, mask, wire.reshape(half_lanes, wire_lanes)),
        (pltpu.VMEM,) * 4,
        (jax.ShapeDtypeStruct((share, fields, extent), bf16),),
        [],
    )
    return misfit[: fields // bands, 0], sensitivity


def solution(mesh):
    in_specs = (
        P(("groups", "band", "field", "wave"), None, None),
        P(("groups", "band", "field", "wave"), None, None),
        P(),
        P(("field", "wave"), "band", None),
    )
    out_specs = (P(("groups", "band")), P(("groups", "band", "field", "wave"), None, None))
    return jax.shard_map(
        per_device, mesh=mesh, in_specs=in_specs, out_specs=out_specs, check_vma=False
    )
```

```python
import functools
import math

import jax
import jax.numpy as jnp
from jax import lax
from jax.experimental import pallas as pl
from jax.experimental.pallas import tpu as pltpu
from jax.sharding import PartitionSpec as P

spectrum_floor = 0.25
gradient_gain = 16.0
lane_width = 128
vmem_bytes = 40 * 1024 * 1024
owner_axes = ("field", "wave")
group_axes = ("band", "field", "wave")
bf16 = jnp.bfloat16
f32 = jnp.float32


def round_up(value, step):
    return -(-value // step) * step


def dot_nn(left, right):
    return lax.dot_general(left, right, (((1,), (0,)), ((), ())), preferred_element_type=f32)


def dot_nt(left, right):
    return lax.dot_general(left, right, (((1,), (1,)), ((), ())), preferred_element_type=f32)


def dot_tn(left, right):
    return lax.dot_general(left, right, (((0,), (0,)), ((), ())), preferred_element_type=f32)


def split_index(index, size):
    whole = jnp.floor((index + 0.5) * (1.0 / size))
    return whole, index - whole * size


def wavenumbers(owner, band, half, rest, pairs_held, pairs_part, groups, degree_count):
    part, pair = split_index(rest, pairs_part)
    part = (lax.axis_index("groups") ^ part.astype(jnp.int32)).astype(f32)
    within = (band * groups + part) * pairs_part + pair
    pair = owner * pairs_held + within
    mirrored = degree_count - 1.0 - pair
    wavenum = jnp.where(half > 0.0, mirrored, pair)
    void = (within >= pairs_held) | ((half > 0.0) & (mirrored == pair))
    return jnp.where(void, 4.0 * degree_count, wavenum)


def own_wavenumbers(lanes, pack, bands, owners, pairs_held, pairs_part, groups, degree_count):
    index = lax.broadcasted_iota(jnp.int32, (1, lanes), 1).astype(f32)
    half, index = split_index(index, lanes // 2)
    rows = groups * pairs_part // pack
    low_place, index = split_index(index, bands * owners * rows)
    block, high_place = split_index(index, rows)
    band, owner = split_index(block, owners)
    rest = high_place * pack + low_place
    return wavenumbers(owner, band, half, rest, pairs_held, pairs_part, groups, degree_count)


def move_lanes(values, moves, lanes):
    total = values.shape[1]
    moved = jnp.zeros(values.shape, f32)
    lane = lax.broadcasted_iota(jnp.int32, values.shape, 1)
    for start, width, place in moves:
        shift = (place - start) % total
        turned = pltpu.roll(values, shift, 1) if shift else values
        moved = jnp.where((lane >= place) & (lane < place + width), turned, moved)
    return moved[:, :lanes]


def cos_and_minus_sin(wavenum, points, columns, inverse):
    quarters = (4.0 * wavenum) * columns
    turns = jnp.floor(quarters * inverse + 0.5)
    angle = (quarters - turns * points) * (0.5 * math.pi * inverse)
    square = angle * angle
    sine = angle * (1.0 + square * (-1.0 / 6 + square * (1.0 / 120 + square * (-1.0 / 5040))))
    cosine = 1.0 + square * (
        -0.5 + square * (1.0 / 24 + square * (-1.0 / 720 + square * (1.0 / 40320)))
    )
    quadrant = turns.astype(jnp.int32)
    swap = (quadrant & 1) != 0
    new_cos = jnp.where(swap, sine, cosine)
    new_sin = jnp.where(swap, cosine, sine)
    new_cos = jnp.where(((quadrant + 1) & 2) != 0, -new_cos, new_cos)
    new_sin = jnp.where((quadrant & 2) != 0, new_sin, -new_sin)
    return new_cos, new_sin


def fill_tables(points_i, wavenum, coarse_ref, fine_ref, at):
    lanes = wavenum.shape[1]
    points = jnp.full((1, lanes), points_i, jnp.int32).astype(f32)
    inverse = 1.0 / points
    scale = jnp.where(2.0 * wavenum < points, 1.0 / jnp.sqrt(points), 0.0)

    def rows_of(count, step):
        return (lax.broadcasted_iota(jnp.int32, (count, lanes), 0) * step).astype(f32)

    coarse_rows = coarse_ref.shape[2]
    coarse_c, coarse_s = cos_and_minus_sin(wavenum, points, rows_of(coarse_rows, lane_width), inverse)
    coarse_ref[at, 0] = coarse_c * scale
    coarse_ref[at, 1] = coarse_s * scale
    mid_c, mid_s = cos_and_minus_sin(wavenum, points, rows_of(lane_width // 8, 8), inverse)
    unit_c, unit_s = cos_and_minus_sin(wavenum, points, rows_of(8, 1), inverse)
    for g in range(lane_width // 16):
        pieces_c = []
        pieces_s = []
        for a in (2 * g, 2 * g + 1):
            step_c = mid_c[a : a + 1]
            step_s = mid_s[a : a + 1]
            pieces_c.append(step_c * unit_c - step_s * unit_s)
            pieces_s.append(step_c * unit_s + step_s * unit_c)
        fine_ref[at, 0, 16 * g : 16 * g + 16] = jnp.concatenate(pieces_c, 0).astype(bf16)
        fine_ref[at, 1, 16 * g : 16 * g + 16] = jnp.concatenate(pieces_s, 0).astype(bf16)


def analyse_kernel(
    pack,
    wire_pack,
    groups,
    bands,
    owners,
    pairs_held,
    pairs_part,
    degree_count,
    nodes_ref,
    states_ref,
    wire_ref,
    coarse_ref,
    fine_ref,
    mask_ref,
    rows_scr,
    wide_scr,
    flat_scr,
):
    share, panel_rows, extent = states_ref.shape
    steps = extent // lane_width
    half_lanes = coarse_ref.shape[3] // 2
    first_cycle = lax.axis_index(group_axes) * share
    column = lax.broadcasted_iota(jnp.int32, (1, extent), 1)
    wavenum = own_wavenumbers(
        2 * half_lanes, pack, bands, owners, pairs_held, pairs_part, groups, degree_count
    )
    for il in range(share):
        points_i = nodes_ref[first_cycle + il]
        fill_tables(points_i, wavenum, coarse_ref, fine_ref, il)
        held = column < points_i
        mask_ref[il : il + 1, :] = held.astype(f32)
        panel = jnp.where(held, states_ref[il].astype(f32), 0.0)
        stacked = jnp.concatenate(
            [panel[:, lane_width * j : lane_width * (j + 1)] for j in range(steps)], axis=0
        ).astype(bf16)
        for h in range(2):
            lanes = slice(h * half_lanes, (h + 1) * half_lanes)
            part_c = dot_nn(stacked, fine_ref[il, 0, :, lanes])
            part_s = dot_nn(stacked, fine_ref[il, 1, :, lanes])
            total_c = jnp.zeros((panel_rows, half_lanes), f32)
            total_s = jnp.zeros((panel_rows, half_lanes), f32)
            for j in range(steps):
                turn_c = coarse_ref[il, 0, j : j + 1, lanes]
                turn_s = coarse_ref[il, 1, j : j + 1, lanes]
                piece_c = part_c[j * panel_rows : (j + 1) * panel_rows]
                piece_s = part_s[j * panel_rows : (j + 1) * panel_rows]
                total_c = total_c + (turn_c * piece_c - turn_s * piece_s)
                total_s = total_s + (turn_c * piece_s + turn_s * piece_c)
            at = (il * 2 + h) * 2 * panel_rows
            rows_scr[at : at + panel_rows, :] = total_c
            rows_scr[at + panel_rows : at + 2 * panel_rows, :] = total_s
    sources = bands * owners
    rows = groups * pairs_part // pack
    width = sources * rows
    count = rows_scr.shape[0]
    parts = pack // wire_pack
    values = rows_scr[...]
    if wide_scr.shape[0] > wire_pack * count:
        wide_scr[wire_pack * count :, :] = jnp.zeros_like(wide_scr[wire_pack * count :, :])
    for d in range(wire_pack):
        moves = [((e * wire_pack + d) * width, width, e * width) for e in range(parts)]
        wide_scr[d * count : (d + 1) * count, :] = move_lanes(values, moves, wide_scr.shape[1])
    flat_scr[...] = jnp.transpose(wide_scr[...])
    for source in range(sources):
        starts = [(e * sources + source) * rows for e in range(parts)]
        wire_ref[source] = jnp.concatenate(
            [flat_scr[at : at + rows, :] for at in starts], axis=0
        ).astype(bf16)


def take_block(rows, index, width, lanes):
    if width % lane_width == 0:
        return rows[:, index * width : (index + 1) * width]
    total = rows.shape[1]
    if index > 0:
        rows = pltpu.roll(rows, total - index * width, 1)
    return rows[:, :lanes]


def join_blocks(blocks, width, total):
    if width % lane_width == 0:
        return jnp.concatenate(blocks, axis=1)
    joined = jnp.zeros((blocks[0].shape[0], total), f32)
    lane = lax.broadcasted_iota(jnp.int32, joined.shape, 1)
    for index, block in enumerate(blocks):
        wide = jnp.concatenate([block] * (total // block.shape[1]), axis=1)
        if index > 0:
            wide = pltpu.roll(wide, index * width, 1)
        here = (lane >= index * width) & (lane < (index + 1) * width)
        joined = jnp.where(here, wide, joined)
    return joined


def pair_tables(own, parts, groups, j, row, q):
    blocks = [own[row + q], parts[0][row + q]] + [t[q] for t in parts[1 + j :: groups]]
    return jnp.concatenate([b.astype(f32) for b in blocks], axis=0).astype(bf16)


def pair_sides(pair, slot, degree_count):
    low_side = slot < degree_count - pair
    low_weight = jnp.where(pair == 0, 1.0, 2.0)
    high_weight = jnp.where(2 * pair == degree_count - 1, 0.0, 2.0)
    return low_side, low_weight, high_weight


def project_kernel(pack, wire_pack, groups, bands, owners, pairs_held, share, wire_ref, own_ref, *refs):
    remote = 1 + groups * (bands - 2)
    part_refs = refs[:remote]
    coef_ref, spectra_ref, flat_scr, left_scr = refs[remote:]
    sources, wire_rows, _ = wire_ref.shape
    pairs_sub = own_ref.shape[0]
    high_places = pairs_sub // pack
    slot_count = own_ref.shape[2]
    degree_count = slot_count - 1
    panel_rows = coef_ref.shape[2]
    fields = panel_rows // 2
    block_rows = 4 * panel_rows
    pairs_part = pairs_sub // groups
    group = lax.axis_index("groups")
    band = lax.axis_index("band")
    first = lax.axis_index(owner_axes) * pairs_held + band * pairs_sub
    for k in range(bands):
        other = band ^ k
        for w in range(owners):
            at = (k * owners + w) * wire_rows
            rows = wire_ref[other * owners + w].astype(f32)
            for c in range(flat_scr.shape[0]):
                flat_scr[c, at : at + wire_rows, :] = rows[:, c * lane_width : (c + 1) * lane_width]
    slot = lax.broadcasted_iota(jnp.int32, (panel_rows, slot_count), 1)
    row = lax.broadcasted_iota(jnp.int32, (panel_rows, slot_count // 2), 0)
    zero = jnp.zeros((panel_rows, slot_count), f32)
    high_power, high_cross = zero, zero
    all_power, all_cross = zero, zero
    for j in range(groups):
        part_row = (group ^ j) * pairs_part
        low_power, low_cross = zero, zero
        for q in reversed(range(pairs_part)):
            place = j * pairs_part + q
            high_place, low_place = divmod(place, pack)
            wire_row = low_place // wire_pack * high_places + high_place
            received = jnp.concatenate(
                [
                    flat_scr[c, pl.ds(wire_row, sources, stride=wire_rows), :]
                    for c in range(flat_scr.shape[0])
                ],
                axis=1,
            )
            for il in range(share):
                left_scr[place, pl.ds(il, sources, stride=share), :] = take_block(
                    received, low_place % wire_pack * share + il, block_rows, left_scr.shape[2]
                )
            left = left_scr[place, :, 0:block_rows].astype(bf16)
            both_halves = dot_tn(
                left, pair_tables(own_ref, part_refs, groups, j, part_row, q)
            )
            pair = first + part_row + q
            low_side, low_weight, high_weight = pair_sides(pair, slot, degree_count)
            cosines = jnp.where(
                low_side, both_halves[0:panel_rows], both_halves[2 * panel_rows : 3 * panel_rows]
            )
            sines = jnp.where(
                low_side, both_halves[panel_rows : 2 * panel_rows], both_halves[3 * panel_rows :]
            )
            coef_ref[place, 0] = cosines
            coef_ref[place, 1] = sines
            weight = jnp.where(low_side, low_weight, high_weight)
            power = (cosines * cosines + sines * sines) * weight
            cross = (
                cosines * pltpu.roll(cosines, fields, 0) + sines * pltpu.roll(sines, fields, 0)
            ) * weight
            low_power = pltpu.roll(low_power, 1, 1) + jnp.where(low_side, power, 0.0)
            low_cross = pltpu.roll(low_cross, 1, 1) + jnp.where(low_side, cross, 0.0)
            high_power = high_power + jnp.where(low_side, 0.0, power)
            high_cross = high_cross + jnp.where(low_side, 0.0, cross)
        all_power = all_power + pltpu.roll(low_power, first + part_row, 1)
        all_cross = all_cross + pltpu.roll(low_cross, first + part_row, 1)
    all_power = all_power + pltpu.roll(high_power, slot_count - 1, 1)
    all_cross = all_cross + pltpu.roll(high_cross, slot_count - 1, 1)
    spectra_ref[:, 0:slot_count] = all_power
    spectra_ref[:, slot_count:] = jnp.where(
        row < fields, all_cross[:, : slot_count // 2], all_cross[:, slot_count // 2 :]
    )


def tree_sum(parts):
    while len(parts) > 1:
        parts = [parts[i] + parts[i + 1] for i in range(0, len(parts), 2)]
    return parts[0]


def gradient_kernel(pack, groups, bands, owners, pairs_held, share, spectra_parts, own_ref, coef_ref, *refs):
    remote = 1 + groups * (bands - 2)
    spectra_refs = refs[:spectra_parts]
    part_refs = refs[spectra_parts : spectra_parts + remote]
    wire_ref, misfit_ref, flat_scr, cycle_scr = refs[spectra_parts + remote :]
    sources, wire_rows, wire_lanes = wire_ref.shape
    pairs_sub = own_ref.shape[0]
    slot_count = own_ref.shape[2]
    degree_count = slot_count - 1
    panel_rows = coef_ref.shape[2]
    fields = panel_rows // 2
    block_rows = 4 * fields
    fields_out = fields // bands
    pairs_part = pairs_sub // groups
    group = lax.axis_index("groups")
    band = lax.axis_index("band")
    first = lax.axis_index(owner_axes) * pairs_held + band * pairs_sub
    slot = lax.broadcasted_iota(jnp.int32, (panel_rows, slot_count), 1)
    row = lax.broadcasted_iota(jnp.int32, (panel_rows, slot_count), 0)
    spectra = tree_sum([s[...] for s in spectra_refs])
    power = spectra[:, :slot_count]
    packed = spectra[:, slot_count:]
    turned = pltpu.roll(packed, fields, 0)
    upper = row[:, : slot_count // 2] < fields
    cross = jnp.concatenate([jnp.where(upper, packed, turned), jnp.where(upper, turned, packed)], axis=1)
    odd_weight = (2 * slot + 1).astype(f32)
    power = power / odd_weight + spectrum_floor
    cross = cross / odd_weight
    root = jnp.sqrt(power)
    other_root = pltpu.roll(root, fields, 0)
    both_power = power + pltpu.roll(power, fields, 0)
    geo_mean = root * other_root
    coherence = cross / geo_mean
    term = (root - other_root) * (root - other_root) + both_power * (1.0 - coherence)
    term = jnp.where(slot < degree_count, term, 0.0)
    mean = jnp.sum(term, axis=1, keepdims=True) / degree_count
    field_row = lax.broadcasted_iota(jnp.int32, (panel_rows, 1), 0)
    misfit_ref[...] = jnp.zeros_like(misfit_ref)
    for i in range(fields_out):
        chosen = jnp.where(field_row == band * fields_out + i, mean, 0.0)
        misfit_ref[i : i + 1, :] = jnp.broadcast_to(
            jnp.sum(chosen, axis=0, keepdims=True), (1, lane_width)
        )
    grad_power = (
        gradient_gain
        * (
            1.0
            - other_root / root
            + (1.0 - coherence)
            + both_power * coherence / (2.0 * power)
        )
        / odd_weight
    )
    grad_cross = -gradient_gain * both_power / geo_mean / odd_weight
    by_degree = jnp.where(row < fields, 2.0 * grad_power, grad_cross)
    high_grad = pltpu.roll(by_degree, 1, 1)
    blocks = []
    for j in range(groups):
        part_row = (group ^ j) * pairs_part
        low_grad = pltpu.roll(by_degree, slot_count - first - part_row, 1)
        for q in range(pairs_part):
            place = j * pairs_part + q
            pair = first + part_row + q
            low_side, low_weight, high_weight = pair_sides(pair, slot, degree_count)
            gain = jnp.where(low_side, low_grad * low_weight, high_grad * high_weight)
            cosines = coef_ref[place, 0] * gain
            sines = coef_ref[place, 1] * gain
            cosines = cosines + pltpu.roll(cosines, fields, 0)
            sines = sines + pltpu.roll(sines, fields, 0)
            grads = jnp.where(row < fields, cosines, sines)
            masked = jnp.concatenate(
                [jnp.where(low_side, grads, 0.0), jnp.where(low_side, 0.0, grads)], axis=0
            ).astype(bf16)
            cycle_scr[place, :, 0:block_rows] = dot_nt(
                pair_tables(own_ref, part_refs, groups, j, part_row, q), masked
            )
            high_place, low_place = divmod(place, pack)
            blocks = [] if low_place == 0 else blocks
            blocks += [cycle_scr[place, pl.ds(il, sources, stride=share), :] for il in range(share)]
            if low_place == pack - 1:
                joined = join_blocks(blocks, block_rows, wire_lanes)
                for c in range(flat_scr.shape[0]):
                    flat_scr[c, pl.ds(high_place, sources, stride=wire_rows), :] = joined[
                        :, c * lane_width : (c + 1) * lane_width
                    ]
            low_grad = pltpu.roll(low_grad, slot_count - 1, 1)
    for k in range(bands):
        other = band ^ k
        for w in range(owners):
            at = (k * owners + w) * wire_rows
            wire_ref[other * owners + w] = jnp.concatenate(
                [flat_scr[c, at : at + wire_rows, :] for c in range(flat_scr.shape[0])], axis=1
            ).astype(bf16)


def synthesise_kernel(pack, coarse_ref, fine_ref, mask_ref, wire_ref, out_ref, flat_scr):
    share, fields, extent = out_ref.shape
    sources, wire_rows, wire_lanes = wire_ref.shape
    steps = extent // lane_width
    half_lanes = coarse_ref.shape[3] // 2
    panel_rows = 2 * fields
    width = sources * wire_rows
    for source in range(sources):
        flat_scr[source * wire_rows : (source + 1) * wire_rows, :] = wire_ref[source].astype(f32)
    if flat_scr.shape[0] > width:
        flat_scr[width:, :] = jnp.zeros_like(flat_scr[width:, :])
    turned = jnp.transpose(flat_scr[...])
    count = wire_lanes // pack
    if pack > 1:
        spare = jnp.zeros((count, round_up(half_lanes, lane_width) - turned.shape[1]), f32)
        values = jnp.zeros((count, half_lanes), f32)
        for low_place in range(pack):
            block = jnp.concatenate([turned[low_place * count : (low_place + 1) * count], spare], axis=1)
            values = values + move_lanes(block, [(0, width, low_place * width)], half_lanes)
    else:
        values = turned[:, :half_lanes]
    row = lax.broadcasted_iota(jnp.int32, (panel_rows, half_lanes), 0)
    for il in range(share):
        total_c = jnp.zeros((steps * panel_rows, lane_width), f32)
        total_s = jnp.zeros((steps * panel_rows, lane_width), f32)
        for h in range(2):
            lanes = slice(h * half_lanes, (h + 1) * half_lanes)
            at = (il * 2 + h) * panel_rows
            direct = values[at : at + panel_rows]
            crossed = pltpu.roll(direct, fields, 0)
            crossed = jnp.where(row < fields, crossed, -crossed)
            pieces = [
                direct * coarse_ref[il, 0, j : j + 1, lanes] + crossed * coarse_ref[il, 1, j : j + 1, lanes]
                for j in range(steps)
            ]
            pieces = jnp.concatenate(pieces, 0).astype(bf16)
            total_c = total_c + dot_nt(pieces, fine_ref[il, 0, :, lanes])
            total_s = total_s + dot_nt(pieces, fine_ref[il, 1, :, lanes])
        mask = mask_ref[il : il + 1, :]
        for j in range(steps):
            lanes = slice(lane_width * j, lane_width * (j + 1))
            at = j * panel_rows
            piece = total_c[at : at + fields] + total_s[at + fields : at + panel_rows]
            out_ref[il, :, lanes] = (piece * mask[:, lanes]).astype(bf16)


def call(body, name, arrays, spaces, out_shapes, scratch, flops=1):
    return pl.pallas_call(
        body,
        name=name,
        cost_estimate=pl.CostEstimate(flops=flops, transcendentals=0, bytes_accessed=1),
        in_specs=[pl.BlockSpec(memory_space=space) for space in spaces],
        out_specs=tuple(pl.BlockSpec(memory_space=pltpu.VMEM) for _ in out_shapes),
        out_shape=tuple(out_shapes),
        scratch_shapes=scratch,
        compiler_params=pltpu.CompilerParams(vmem_limit_bytes=vmem_bytes),
    )(*arrays)


def exchange(array, axes, count):
    return [array] + [
        lax.ppermute(array, axes, [(i, i ^ k) for i in range(count)]) for k in range(1, count)
    ]


def per_device(predicted_state, analysis_state, nodes_per_parallel, weighted_harmonic_table):
    share, fields, extent = predicted_state.shape
    pairs_held, cycle_band, slot_count = weighted_harmonic_table.shape
    groups = lax.axis_size("groups")
    bands = lax.axis_size("band")
    owners = lax.axis_size(owner_axes)
    group = lax.axis_index("groups")
    band = lax.axis_index("band")
    sources = bands * owners
    pairs_part = -(-pairs_held // (bands * groups))
    pairs_sub = groups * pairs_part
    panel_rows = 2 * fields
    pack = max(1, lane_width // (share * 4 * fields))
    wire_pack = max(1, lane_width // (share * 4 * panel_rows))
    wire_lanes = round_up(wire_pack * share * 4 * panel_rows, lane_width)
    back_lanes = round_up(pack * share * 4 * fields, lane_width)
    block_lanes = round_up(4 * panel_rows, lane_width)
    half_lanes = sources * pairs_sub
    coarse_rows = round_up(extent // lane_width, 8)

    table = weighted_harmonic_table
    if pairs_sub * bands != pairs_held:
        table = jnp.pad(table, ((0, pairs_sub * bands - pairs_held), (0, 0), (0, 0)))
    own_table = lax.dynamic_slice_in_dim(table, band * pairs_sub, pairs_sub, 0)

    def over_bands(array, k):
        return lax.ppermute(array, "band", [(i, i ^ k) for i in range(bands)])

    starts = [(band ^ k) * pairs_sub + group * pairs_part for k in range(bands)]
    far = [lax.dynamic_slice_in_dim(table, starts[k], pairs_part, 0) for k in range(2, bands)]
    near = lax.dynamic_slice_in_dim(table, (band ^ 1) * pairs_sub, pairs_sub, 0)
    near, *far = lax.optimization_barrier((near, *far))
    near = over_bands(near, 1)
    far = [None, None] + [over_bands(piece, k + 2) for k, piece in enumerate(far)]
    states = jnp.concatenate([predicted_state, analysis_state], axis=1)
    wire, coarse, fine, mask = call(
        functools.partial(
            analyse_kernel,
            pack,
            wire_pack,
            groups,
            bands,
            owners,
            pairs_held,
            pairs_part,
            slot_count - 1,
        ),
        "analyse",
        (nodes_per_parallel, states),
        (pltpu.SMEM, pltpu.VMEM),
        (
            jax.ShapeDtypeStruct((sources, pairs_sub // wire_pack, wire_lanes), bf16),
            jax.ShapeDtypeStruct((share, 2, coarse_rows, 2 * half_lanes), f32),
            jax.ShapeDtypeStruct((share, 2, lane_width, 2 * half_lanes), bf16),
            jax.ShapeDtypeStruct((share, extent), f32),
        ),
        [
            pltpu.VMEM((share * 4 * panel_rows, half_lanes), f32),
            pltpu.VMEM((wire_lanes, round_up(half_lanes // wire_pack, lane_width)), f32),
            pltpu.VMEM((round_up(half_lanes // wire_pack, lane_width), wire_lanes), f32),
        ],
    )
    wire = lax.all_to_all(wire, group_axes, 0, 0, tiled=True)
    parts = [near]
    for piece in far[2:]:
        parts.append(piece)
        for j in range(1, groups):
            parts.append(lax.ppermute(piece, "groups", [(i, i ^ j) for i in range(groups)]))
    block_scratch = pltpu.VMEM((pairs_sub, bands * cycle_band, block_lanes), f32)
    coef, spectra = call(
        functools.partial(project_kernel, pack, wire_pack, groups, bands, owners, pairs_held, share),
        "project",
        (wire, own_table, *parts),
        (pltpu.VMEM,) * (2 + len(parts)),
        (
            jax.ShapeDtypeStruct((pairs_sub, 2, panel_rows, slot_count), f32),
            jax.ShapeDtypeStruct((panel_rows, slot_count + slot_count // 2), f32),
        ),
        [
            pltpu.VMEM((wire_lanes // lane_width, half_lanes // wire_pack, lane_width), f32),
            block_scratch,
        ],
    )
    spectra = tree_sum(exchange(spectra, owner_axes, owners))
    spectra = exchange(spectra, "band", bands)
    wire, misfit = call(
        functools.partial(gradient_kernel, pack, groups, bands, owners, pairs_held, share, len(spectra)),
        "gradient",
        (own_table, coef, *spectra, *parts),
        (pltpu.VMEM,) * (2 + len(spectra) + len(parts)),
        (
            jax.ShapeDtypeStruct((sources, pairs_sub // pack, back_lanes), bf16),
            jax.ShapeDtypeStruct((round_up(fields // bands, 8), lane_width), f32),
        ),
        [
            pltpu.VMEM((back_lanes // lane_width, half_lanes // pack, lane_width), f32),
            block_scratch,
        ],
    )
    wire = lax.all_to_all(wire, group_axes, 0, 0, tiled=True)
    (sensitivity,) = call(
        functools.partial(synthesise_kernel, pack),
        "synthesise",
        (coarse, fine, mask, wire),
        (pltpu.VMEM,) * 4,
        (jax.ShapeDtypeStruct((share, fields, extent), bf16),),
        [pltpu.VMEM((round_up(half_lanes // pack, lane_width), back_lanes), f32)],
    )
    return misfit[: fields // bands, 0], sensitivity


def solution(mesh):
    in_specs = (
        P(("groups", "band", "field", "wave"), None, None),
        P(("groups", "band", "field", "wave"), None, None),
        P(),
        P(("field", "wave"), "band", None),
    )
    out_specs = (P(("groups", "band")), P(("groups", "band", "field", "wave"), None, None))
    return jax.shard_map(
        per_device, mesh=mesh, in_specs=in_specs, out_specs=out_specs, check_vma=False
    )
```

```python
import functools
import math

import jax
import jax.numpy as jnp
from jax import lax
from jax.experimental import pallas as pl
from jax.experimental.pallas import tpu as pltpu
from jax.sharding import PartitionSpec as P

spectrum_floor = 0.25
gradient_gain = 16.0
lane_width = 128
vmem_bytes = 40 * 1024 * 1024
owner_axes = ("field", "wave")
group_axes = ("band", "field", "wave")
bf16 = jnp.bfloat16
f32 = jnp.float32


def round_up(value, step):
    return -(-value // step) * step


def dot_nn(left, right):
    return lax.dot_general(left, right, (((1,), (0,)), ((), ())), preferred_element_type=f32)


def dot_nt(left, right):
    return lax.dot_general(left, right, (((1,), (1,)), ((), ())), preferred_element_type=f32)


def dot_tn(left, right):
    return lax.dot_general(left, right, (((0,), (0,)), ((), ())), preferred_element_type=f32)


def split_index(index, size):
    whole = jnp.floor((index + 0.5) * (1.0 / size))
    return whole, index - whole * size


def wavenumbers(owner, band, half, rest, pairs_held, pairs_part, groups, degree_count):
    part, pair = split_index(rest, pairs_part)
    part = (lax.axis_index("groups") ^ part.astype(jnp.int32)).astype(f32)
    within = (band * groups + part) * pairs_part + pair
    pair = owner * pairs_held + within
    mirrored = degree_count - 1.0 - pair
    wavenum = jnp.where(half > 0.0, mirrored, pair)
    void = (within >= pairs_held) | ((half > 0.0) & (mirrored == pair))
    return jnp.where(void, 4.0 * degree_count, wavenum)


def own_wavenumbers(lanes, pack, bands, owners, pairs_held, pairs_part, groups, degree_count):
    index = lax.broadcasted_iota(jnp.int32, (1, lanes), 1).astype(f32)
    half, index = split_index(index, lanes // 2)
    rows = groups * pairs_part // pack
    low_place, index = split_index(index, bands * owners * rows)
    block, high_place = split_index(index, rows)
    band, owner = split_index(block, owners)
    rest = high_place * pack + low_place
    return wavenumbers(owner, band, half, rest, pairs_held, pairs_part, groups, degree_count)


def move_lanes(values, moves, lanes):
    total = values.shape[1]
    moved = jnp.zeros(values.shape, f32)
    lane = lax.broadcasted_iota(jnp.int32, values.shape, 1)
    for start, width, place in moves:
        shift = (place - start) % total
        turned = pltpu.roll(values, shift, 1) if shift else values
        moved = jnp.where((lane >= place) & (lane < place + width), turned, moved)
    return moved[:, :lanes]


def cos_and_minus_sin(wavenum, points, columns, inverse):
    quarters = (4.0 * wavenum) * columns
    turns = jnp.floor(quarters * inverse + 0.5)
    angle = (quarters - turns * points) * (0.5 * math.pi * inverse)
    square = angle * angle
    sine = angle * (1.0 + square * (-1.0 / 6 + square * (1.0 / 120 + square * (-1.0 / 5040))))
    cosine = 1.0 + square * (
        -0.5 + square * (1.0 / 24 + square * (-1.0 / 720 + square * (1.0 / 40320)))
    )
    quadrant = turns.astype(jnp.int32)
    swap = (quadrant & 1) != 0
    new_cos = jnp.where(swap, sine, cosine)
    new_sin = jnp.where(swap, cosine, sine)
    new_cos = jnp.where(((quadrant + 1) & 2) != 0, -new_cos, new_cos)
    new_sin = jnp.where((quadrant & 2) != 0, new_sin, -new_sin)
    return new_cos, new_sin


def fill_tables(points_i, wavenum, coarse_ref, fine_ref, at):
    lanes = wavenum.shape[1]
    points = jnp.full((1, lanes), points_i, jnp.int32).astype(f32)
    inverse = 1.0 / points
    scale = jnp.where(2.0 * wavenum < points, 1.0 / jnp.sqrt(points), 0.0)

    def rows_of(count, step):
        return (lax.broadcasted_iota(jnp.int32, (count, lanes), 0) * step).astype(f32)

    coarse_rows = coarse_ref.shape[2]
    coarse_c, coarse_s = cos_and_minus_sin(wavenum, points, rows_of(coarse_rows, lane_width), inverse)
    coarse_ref[at, 0] = coarse_c * scale
    coarse_ref[at, 1] = coarse_s * scale
    mid_c, mid_s = cos_and_minus_sin(wavenum, points, rows_of(lane_width // 8, 8), inverse)
    unit_c, unit_s = cos_and_minus_sin(wavenum, points, rows_of(8, 1), inverse)
    for g in range(lane_width // 16):
        pieces_c = []
        pieces_s = []
        for a in (2 * g, 2 * g + 1):
            step_c = mid_c[a : a + 1]
            step_s = mid_s[a : a + 1]
            pieces_c.append(step_c * unit_c - step_s * unit_s)
            pieces_s.append(step_c * unit_s + step_s * unit_c)
        fine_ref[at, 0, 16 * g : 16 * g + 16] = jnp.concatenate(pieces_c, 0).astype(bf16)
        fine_ref[at, 1, 16 * g : 16 * g + 16] = jnp.concatenate(pieces_s, 0).astype(bf16)


def analyse_kernel(
    pack,
    wire_pack,
    groups,
    bands,
    owners,
    pairs_held,
    pairs_part,
    degree_count,
    nodes_ref,
    states_ref,
    wire_ref,
    coarse_ref,
    fine_ref,
    mask_ref,
    rows_scr,
    wide_scr,
    flat_scr,
):
    share, panel_rows, extent = states_ref.shape
    steps = extent // lane_width
    half_lanes = coarse_ref.shape[3] // 2
    first_cycle = lax.axis_index(group_axes) * share
    column = lax.broadcasted_iota(jnp.int32, (1, extent), 1)
    wavenum = own_wavenumbers(
        2 * half_lanes, pack, bands, owners, pairs_held, pairs_part, groups, degree_count
    )
    for il in range(share):
        points_i = nodes_ref[first_cycle + il]
        fill_tables(points_i, wavenum, coarse_ref, fine_ref, il)
        held = column < points_i
        mask_ref[il : il + 1, :] = held.astype(f32)
        panel = jnp.where(held, states_ref[il].astype(f32), 0.0)
        stacked = jnp.concatenate(
            [panel[:, lane_width * j : lane_width * (j + 1)] for j in range(steps)], axis=0
        ).astype(bf16)
        for h in range(2):
            lanes = slice(h * half_lanes, (h + 1) * half_lanes)
            part_c = dot_nn(stacked, fine_ref[il, 0, :, lanes])
            part_s = dot_nn(stacked, fine_ref[il, 1, :, lanes])
            total_c = jnp.zeros((panel_rows, half_lanes), f32)
            total_s = jnp.zeros((panel_rows, half_lanes), f32)
            for j in range(steps):
                turn_c = coarse_ref[il, 0, j : j + 1, lanes]
                turn_s = coarse_ref[il, 1, j : j + 1, lanes]
                piece_c = part_c[j * panel_rows : (j + 1) * panel_rows]
                piece_s = part_s[j * panel_rows : (j + 1) * panel_rows]
                total_c = total_c + (turn_c * piece_c - turn_s * piece_s)
                total_s = total_s + (turn_c * piece_s + turn_s * piece_c)
            at = (il * 2 + h) * 2 * panel_rows
            rows_scr[at : at + panel_rows, :] = total_c
            rows_scr[at + panel_rows : at + 2 * panel_rows, :] = total_s
    sources = bands * owners
    rows = groups * pairs_part // pack
    width = sources * rows
    count = rows_scr.shape[0]
    parts = pack // wire_pack
    values = rows_scr[...]
    if wide_scr.shape[0] > wire_pack * count:
        wide_scr[wire_pack * count :, :] = jnp.zeros_like(wide_scr[wire_pack * count :, :])
    for d in range(wire_pack):
        moves = [((e * wire_pack + d) * width, width, e * width) for e in range(parts)]
        wide_scr[d * count : (d + 1) * count, :] = move_lanes(values, moves, wide_scr.shape[1])
    flat_scr[...] = jnp.transpose(wide_scr[...])
    for source in range(sources):
        starts = [(e * sources + source) * rows for e in range(parts)]
        wire_ref[source] = jnp.concatenate(
            [flat_scr[at : at + rows, :] for at in starts], axis=0
        ).astype(bf16)


def take_block(rows, index, width, lanes):
    if width % lane_width == 0:
        return rows[:, index * width : (index + 1) * width]
    total = rows.shape[1]
    if index > 0:
        rows = pltpu.roll(rows, total - index * width, 1)
    return rows[:, :lanes]


def join_blocks(blocks, width, total):
    if width % lane_width == 0:
        return jnp.concatenate(blocks, axis=1)
    joined = jnp.zeros((blocks[0].shape[0], total), f32)
    lane = lax.broadcasted_iota(jnp.int32, joined.shape, 1)
    for index, block in enumerate(blocks):
        wide = jnp.concatenate([block] * (total // block.shape[1]), axis=1)
        if index > 0:
            wide = pltpu.roll(wide, index * width, 1)
        here = (lane >= index * width) & (lane < (index + 1) * width)
        joined = jnp.where(here, wide, joined)
    return joined


def pair_tables(own, parts, groups, j, row, q):
    blocks = [own[row + q], parts[0][row + q]] + [t[q] for t in parts[1 + j :: groups]]
    return jnp.concatenate([b.astype(f32) for b in blocks], axis=0).astype(bf16)


def pair_sides(pair, slot, degree_count):
    low_side = slot < degree_count - pair
    low_weight = jnp.where(pair == 0, 1.0, 2.0)
    high_weight = jnp.where(2 * pair == degree_count - 1, 0.0, 2.0)
    return low_side, low_weight, high_weight


def project_kernel(pack, wire_pack, groups, bands, owners, pairs_held, share, wire_ref, own_ref, *refs):
    remote = 1 + groups * (bands - 2)
    part_refs = refs[:remote]
    coef_ref, spectra_ref, flat_scr, left_scr = refs[remote:]
    sources, wire_rows, _ = wire_ref.shape
    pairs_sub = own_ref.shape[0]
    high_places = pairs_sub // pack
    slot_count = own_ref.shape[2]
    degree_count = slot_count - 1
    panel_rows = coef_ref.shape[2]
    fields = panel_rows // 2
    block_rows = 4 * panel_rows
    pairs_part = pairs_sub // groups
    group = lax.axis_index("groups")
    band = lax.axis_index("band")
    first = lax.axis_index(owner_axes) * pairs_held + band * pairs_sub
    for k in range(bands):
        other = band ^ k
        for w in range(owners):
            at = (k * owners + w) * wire_rows
            rows = wire_ref[other * owners + w].astype(f32)
            for c in range(flat_scr.shape[0]):
                flat_scr[c, at : at + wire_rows, :] = rows[:, c * lane_width : (c + 1) * lane_width]
    slot = lax.broadcasted_iota(jnp.int32, (panel_rows, slot_count), 1)
    row = lax.broadcasted_iota(jnp.int32, (panel_rows, slot_count // 2), 0)
    zero = jnp.zeros((panel_rows, slot_count), f32)
    high_power, high_cross = zero, zero
    all_power, all_cross = zero, zero
    for j in range(groups):
        part_row = (group ^ j) * pairs_part
        low_power, low_cross = zero, zero
        for q in reversed(range(pairs_part)):
            place = j * pairs_part + q
            high_place, low_place = divmod(place, pack)
            wire_row = low_place // wire_pack * high_places + high_place
            received = jnp.concatenate(
                [
                    flat_scr[c, pl.ds(wire_row, sources, stride=wire_rows), :]
                    for c in range(flat_scr.shape[0])
                ],
                axis=1,
            )
            for il in range(share):
                left_scr[place, pl.ds(il, sources, stride=share), :] = take_block(
                    received, low_place % wire_pack * share + il, block_rows, left_scr.shape[2]
                )
            left = left_scr[place, :, 0:block_rows].astype(bf16)
            both_halves = dot_tn(
                left, pair_tables(own_ref, part_refs, groups, j, part_row, q)
            )
            pair = first + part_row + q
            low_side, low_weight, high_weight = pair_sides(pair, slot, degree_count)
            cosines = jnp.where(
                low_side, both_halves[0:panel_rows], both_halves[2 * panel_rows : 3 * panel_rows]
            )
            sines = jnp.where(
                low_side, both_halves[panel_rows : 2 * panel_rows], both_halves[3 * panel_rows :]
            )
            coef_ref[place, 0] = cosines
            coef_ref[place, 1] = sines
            weight = jnp.where(low_side, low_weight, high_weight)
            power = (cosines * cosines + sines * sines) * weight
            cross = (
                cosines * pltpu.roll(cosines, fields, 0) + sines * pltpu.roll(sines, fields, 0)
            ) * weight
            low_power = pltpu.roll(low_power, 1, 1) + jnp.where(low_side, power, 0.0)
            low_cross = pltpu.roll(low_cross, 1, 1) + jnp.where(low_side, cross, 0.0)
            high_power = high_power + jnp.where(low_side, 0.0, power)
            high_cross = high_cross + jnp.where(low_side, 0.0, cross)
        all_power = all_power + pltpu.roll(low_power, first + part_row, 1)
        all_cross = all_cross + pltpu.roll(low_cross, first + part_row, 1)
    all_power = all_power + pltpu.roll(high_power, slot_count - 1, 1)
    all_cross = all_cross + pltpu.roll(high_cross, slot_count - 1, 1)
    spectra_ref[:, 0:slot_count] = all_power
    spectra_ref[:, slot_count:] = jnp.where(
        row < fields, all_cross[:, : slot_count // 2], all_cross[:, slot_count // 2 :]
    )


def tree_sum(parts):
    while len(parts) > 1:
        parts = [parts[i] + parts[i + 1] for i in range(0, len(parts), 2)]
    return parts[0]


def gradient_kernel(pack, groups, bands, owners, pairs_held, share, spectra_parts, own_ref, coef_ref, *refs):
    remote = 1 + groups * (bands - 2)
    spectra_refs = refs[:spectra_parts]
    part_refs = refs[spectra_parts : spectra_parts + remote]
    wire_ref, misfit_ref, flat_scr, cycle_scr = refs[spectra_parts + remote :]
    sources, wire_rows, wire_lanes = wire_ref.shape
    pairs_sub = own_ref.shape[0]
    slot_count = own_ref.shape[2]
    degree_count = slot_count - 1
    panel_rows = coef_ref.shape[2]
    fields = panel_rows // 2
    block_rows = 4 * fields
    fields_out = fields // bands
    pairs_part = pairs_sub // groups
    group = lax.axis_index("groups")
    band = lax.axis_index("band")
    first = lax.axis_index(owner_axes) * pairs_held + band * pairs_sub
    slot = lax.broadcasted_iota(jnp.int32, (panel_rows, slot_count), 1)
    row = lax.broadcasted_iota(jnp.int32, (panel_rows, slot_count), 0)
    spectra = tree_sum([s[...] for s in spectra_refs])
    power = spectra[:, :slot_count]
    packed = spectra[:, slot_count:]
    turned = pltpu.roll(packed, fields, 0)
    upper = row[:, : slot_count // 2] < fields
    cross = jnp.concatenate([jnp.where(upper, packed, turned), jnp.where(upper, turned, packed)], axis=1)
    odd_weight = (2 * slot + 1).astype(f32)
    power = power / odd_weight + spectrum_floor
    cross = cross / odd_weight
    root = jnp.sqrt(power)
    other_root = pltpu.roll(root, fields, 0)
    both_power = power + pltpu.roll(power, fields, 0)
    geo_mean = root * other_root
    coherence = cross / geo_mean
    term = (root - other_root) * (root - other_root) + both_power * (1.0 - coherence)
    term = jnp.where(slot < degree_count, term, 0.0)
    mean = jnp.sum(term, axis=1, keepdims=True) / degree_count
    field_row = lax.broadcasted_iota(jnp.int32, (panel_rows, 1), 0)
    misfit_ref[...] = jnp.zeros_like(misfit_ref)
    for i in range(fields_out):
        chosen = jnp.where(field_row == band * fields_out + i, mean, 0.0)
        misfit_ref[i : i + 1, :] = jnp.broadcast_to(
            jnp.sum(chosen, axis=0, keepdims=True), (1, lane_width)
        )
    grad_power = (
        gradient_gain
        * (
            1.0
            - other_root / root
            + (1.0 - coherence)
            + both_power * coherence / (2.0 * power)
        )
        / odd_weight
    )
    grad_cross = -gradient_gain * both_power / geo_mean / odd_weight
    by_degree = jnp.where(row < fields, 2.0 * grad_power, grad_cross)
    high_grad = pltpu.roll(by_degree, 1, 1)
    blocks = []
    for j in range(groups):
        part_row = (group ^ j) * pairs_part
        low_grad = pltpu.roll(by_degree, slot_count - first - part_row, 1)
        for q in range(pairs_part):
            place = j * pairs_part + q
            pair = first + part_row + q
            low_side, low_weight, high_weight = pair_sides(pair, slot, degree_count)
            gain = jnp.where(low_side, low_grad * low_weight, high_grad * high_weight)
            cosines = coef_ref[place, 0] * gain
            sines = coef_ref[place, 1] * gain
            cosines = cosines + pltpu.roll(cosines, fields, 0)
            sines = sines + pltpu.roll(sines, fields, 0)
            grads = jnp.where(row < fields, cosines, sines)
            masked = jnp.concatenate(
                [jnp.where(low_side, grads, 0.0), jnp.where(low_side, 0.0, grads)], axis=0
            ).astype(bf16)
            cycle_scr[place, :, 0:block_rows] = dot_nt(
                pair_tables(own_ref, part_refs, groups, j, part_row, q), masked
            )
            high_place, low_place = divmod(place, pack)
            blocks = [] if low_place == 0 else blocks
            blocks += [cycle_scr[place, pl.ds(il, sources, stride=share), :] for il in range(share)]
            if low_place == pack - 1:
                joined = join_blocks(blocks, block_rows, wire_lanes)
                for c in range(flat_scr.shape[0]):
                    flat_scr[c, pl.ds(high_place, sources, stride=wire_rows), :] = joined[
                        :, c * lane_width : (c + 1) * lane_width
                    ]
            low_grad = pltpu.roll(low_grad, slot_count - 1, 1)
    for k in range(bands):
        other = band ^ k
        for w in range(owners):
            at = (k * owners + w) * wire_rows
            wire_ref[other * owners + w] = jnp.concatenate(
                [flat_scr[c, at : at + wire_rows, :] for c in range(flat_scr.shape[0])], axis=1
            ).astype(bf16)


def synthesise_kernel(pack, coarse_ref, fine_ref, mask_ref, wire_ref, out_ref, flat_scr):
    share, fields, extent = out_ref.shape
    sources, wire_rows, wire_lanes = wire_ref.shape
    steps = extent // lane_width
    half_lanes = coarse_ref.shape[3] // 2
    panel_rows = 2 * fields
    width = sources * wire_rows
    for source in range(sources):
        flat_scr[source * wire_rows : (source + 1) * wire_rows, :] = wire_ref[source].astype(f32)
    if flat_scr.shape[0] > width:
        flat_scr[width:, :] = jnp.zeros_like(flat_scr[width:, :])
    turned = jnp.transpose(flat_scr[...])
    count = wire_lanes // pack
    if pack > 1:
        spare = jnp.zeros((count, round_up(half_lanes, lane_width) - turned.shape[1]), f32)
        values = jnp.zeros((count, half_lanes), f32)
        for low_place in range(pack):
            block = jnp.concatenate([turned[low_place * count : (low_place + 1) * count], spare], axis=1)
            values = values + move_lanes(block, [(0, width, low_place * width)], half_lanes)
    else:
        values = turned[:, :half_lanes]
    row = lax.broadcasted_iota(jnp.int32, (panel_rows, half_lanes), 0)
    for il in range(share):
        total_c = jnp.zeros((steps * panel_rows, lane_width), f32)
        total_s = jnp.zeros((steps * panel_rows, lane_width), f32)
        for h in range(2):
            lanes = slice(h * half_lanes, (h + 1) * half_lanes)
            at = (il * 2 + h) * panel_rows
            direct = values[at : at + panel_rows]
            crossed = pltpu.roll(direct, fields, 0)
            crossed = jnp.where(row < fields, crossed, -crossed)
            pieces = [
                direct * coarse_ref[il, 0, j : j + 1, lanes] + crossed * coarse_ref[il, 1, j : j + 1, lanes]
                for j in range(steps)
            ]
            pieces = jnp.concatenate(pieces, 0).astype(bf16)
            total_c = total_c + dot_nt(pieces, fine_ref[il, 0, :, lanes])
            total_s = total_s + dot_nt(pieces, fine_ref[il, 1, :, lanes])
        mask = mask_ref[il : il + 1, :]
        for j in range(steps):
            lanes = slice(lane_width * j, lane_width * (j + 1))
            at = j * panel_rows
            piece = total_c[at : at + fields] + total_s[at + fields : at + panel_rows]
            out_ref[il, :, lanes] = (piece * mask[:, lanes]).astype(bf16)


def call(body, name, arrays, spaces, out_shapes, scratch, flops=1):
    return pl.pallas_call(
        body,
        name=name,
        cost_estimate=pl.CostEstimate(flops=flops, transcendentals=0, bytes_accessed=1),
        in_specs=[pl.BlockSpec(memory_space=space) for space in spaces],
        out_specs=tuple(pl.BlockSpec(memory_space=pltpu.VMEM) for _ in out_shapes),
        out_shape=tuple(out_shapes),
        scratch_shapes=scratch,
        compiler_params=pltpu.CompilerParams(vmem_limit_bytes=vmem_bytes),
    )(*arrays)


def exchange(array, axes, count):
    return [array] + [
        lax.ppermute(array, axes, [(i, i ^ k) for i in range(count)]) for k in range(1, count)
    ]


def per_device(predicted_state, analysis_state, nodes_per_parallel, weighted_harmonic_table):
    share, fields, extent = predicted_state.shape
    pairs_held, cycle_band, slot_count = weighted_harmonic_table.shape
    groups = lax.axis_size("groups")
    bands = lax.axis_size("band")
    owners = lax.axis_size(owner_axes)
    group = lax.axis_index("groups")
    band = lax.axis_index("band")
    sources = bands * owners
    pairs_part = -(-pairs_held // (bands * groups))
    pairs_sub = groups * pairs_part
    panel_rows = 2 * fields
    pack = max(1, lane_width // (share * 4 * fields))
    wire_pack = 1
    wire_lanes = round_up(wire_pack * share * 4 * panel_rows, lane_width)
    back_lanes = round_up(pack * share * 4 * fields, lane_width)
    block_lanes = round_up(4 * panel_rows, lane_width)
    half_lanes = sources * pairs_sub
    coarse_rows = round_up(extent // lane_width, 8)

    table = weighted_harmonic_table
    if pairs_sub * bands != pairs_held:
        table = jnp.pad(table, ((0, pairs_sub * bands - pairs_held), (0, 0), (0, 0)))
    own_table = lax.dynamic_slice_in_dim(table, band * pairs_sub, pairs_sub, 0)

    def over_bands(array, k):
        return lax.ppermute(array, "band", [(i, i ^ k) for i in range(bands)])

    starts = [(band ^ k) * pairs_sub + group * pairs_part for k in range(bands)]
    far = [lax.dynamic_slice_in_dim(table, starts[k], pairs_part, 0) for k in range(2, bands)]
    near = lax.dynamic_slice_in_dim(table, (band ^ 1) * pairs_sub, pairs_sub, 0)
    near, *far = lax.optimization_barrier((near, *far))
    near = over_bands(near, 1)
    far = [None, None] + [over_bands(piece, k + 2) for k, piece in enumerate(far)]
    states = jnp.concatenate([predicted_state, analysis_state], axis=1)
    wire, coarse, fine, mask = call(
        functools.partial(
            analyse_kernel,
            pack,
            wire_pack,
            groups,
            bands,
            owners,
            pairs_held,
            pairs_part,
            slot_count - 1,
        ),
        "analyse",
        (nodes_per_parallel, states),
        (pltpu.SMEM, pltpu.VMEM),
        (
            jax.ShapeDtypeStruct((sources, pairs_sub // wire_pack, wire_lanes), bf16),
            jax.ShapeDtypeStruct((share, 2, coarse_rows, 2 * half_lanes), f32),
            jax.ShapeDtypeStruct((share, 2, lane_width, 2 * half_lanes), bf16),
            jax.ShapeDtypeStruct((share, extent), f32),
        ),
        [
            pltpu.VMEM((share * 4 * panel_rows, half_lanes), f32),
            pltpu.VMEM((wire_lanes, round_up(half_lanes // wire_pack, lane_width)), f32),
            pltpu.VMEM((round_up(half_lanes // wire_pack, lane_width), wire_lanes), f32),
        ],
    )
    wire = lax.all_to_all(wire, group_axes, 0, 0, tiled=True)
    parts = [near]
    for piece in far[2:]:
        parts.append(piece)
        for j in range(1, groups):
            parts.append(lax.ppermute(piece, "groups", [(i, i ^ j) for i in range(groups)]))
    block_scratch = pltpu.VMEM((pairs_sub, bands * cycle_band, block_lanes), f32)
    coef, spectra = call(
        functools.partial(project_kernel, pack, wire_pack, groups, bands, owners, pairs_held, share),
        "project",
        (wire, own_table, *parts),
        (pltpu.VMEM,) * (2 + len(parts)),
        (
            jax.ShapeDtypeStruct((pairs_sub, 2, panel_rows, slot_count), f32),
            jax.ShapeDtypeStruct((panel_rows, slot_count + slot_count // 2), f32),
        ),
        [
            pltpu.VMEM((wire_lanes // lane_width, half_lanes // wire_pack, lane_width), f32),
            block_scratch,
        ],
    )
    spectra = tree_sum(exchange(spectra, owner_axes, owners))
    spectra = exchange(spectra, "band", bands)
    wire, misfit = call(
        functools.partial(gradient_kernel, pack, groups, bands, owners, pairs_held, share, len(spectra)),
        "gradient",
        (own_table, coef, *spectra, *parts),
        (pltpu.VMEM,) * (2 + len(spectra) + len(parts)),
        (
            jax.ShapeDtypeStruct((sources, pairs_sub // pack, back_lanes), bf16),
            jax.ShapeDtypeStruct((round_up(fields // bands, 8), lane_width), f32),
        ),
        [
            pltpu.VMEM((back_lanes // lane_width, half_lanes // pack, lane_width), f32),
            block_scratch,
        ],
    )
    wire = lax.all_to_all(wire, group_axes, 0, 0, tiled=True)
    (sensitivity,) = call(
        functools.partial(synthesise_kernel, pack),
        "synthesise",
        (coarse, fine, mask, wire),
        (pltpu.VMEM,) * 4,
        (jax.ShapeDtypeStruct((share, fields, extent), bf16),),
        [pltpu.VMEM((round_up(half_lanes // pack, lane_width), back_lanes), f32)],
    )
    return misfit[: fields // bands, 0], sensitivity


def solution(mesh):
    in_specs = (
        P(("groups", "band", "field", "wave"), None, None),
        P(("groups", "band", "field", "wave"), None, None),
        P(),
        P(("field", "wave"), "band", None),
    )
    out_specs = (P(("groups", "band")), P(("groups", "band", "field", "wave"), None, None))
    return jax.shard_map(
        per_device, mesh=mesh, in_specs=in_specs, out_specs=out_specs, check_vma=False
    )
```

```python
import functools
import math

import jax
import jax.numpy as jnp
from jax import lax
from jax.experimental import pallas as pl
from jax.experimental.pallas import tpu as pltpu
from jax.sharding import PartitionSpec as P

spectrum_floor = 0.25
gradient_gain = 16.0
lane_width = 128
vmem_bytes = 40 * 1024 * 1024
owner_axes = ("field", "wave")
group_axes = ("band", "field", "wave")
bf16 = jnp.bfloat16
f32 = jnp.float32


def round_up(value, step):
    return -(-value // step) * step


def dot_nn(left, right):
    return lax.dot_general(left, right, (((1,), (0,)), ((), ())), preferred_element_type=f32)


def dot_nt(left, right):
    return lax.dot_general(left, right, (((1,), (1,)), ((), ())), preferred_element_type=f32)


def dot_tn(left, right):
    return lax.dot_general(left, right, (((0,), (0,)), ((), ())), preferred_element_type=f32)


def split_index(index, size):
    whole = jnp.floor((index + 0.5) * (1.0 / size))
    return whole, index - whole * size


def wavenumbers(owner, band, half, rest, pairs_held, pairs_part, groups, degree_count):
    part, pair = split_index(rest, pairs_part)
    part = (lax.axis_index("groups") ^ part.astype(jnp.int32)).astype(f32)
    within = (band * groups + part) * pairs_part + pair
    pair = owner * pairs_held + within
    mirrored = degree_count - 1.0 - pair
    wavenum = jnp.where(half > 0.0, mirrored, pair)
    void = (within >= pairs_held) | ((half > 0.0) & (mirrored == pair))
    return jnp.where(void, 4.0 * degree_count, wavenum)


def own_wavenumbers(lanes, pack, bands, owners, pairs_held, pairs_part, groups, degree_count):
    index = lax.broadcasted_iota(jnp.int32, (1, lanes), 1).astype(f32)
    half, index = split_index(index, lanes // 2)
    rows = groups * pairs_part // pack
    low_place, index = split_index(index, bands * owners * rows)
    block, high_place = split_index(index, rows)
    band, owner = split_index(block, owners)
    rest = high_place * pack + low_place
    return wavenumbers(owner, band, half, rest, pairs_held, pairs_part, groups, degree_count)


def move_lanes(values, moves, lanes):
    total = values.shape[1]
    moved = jnp.zeros(values.shape, f32)
    lane = lax.broadcasted_iota(jnp.int32, values.shape, 1)
    for start, width, place in moves:
        shift = (place - start) % total
        turned = pltpu.roll(values, shift, 1) if shift else values
        moved = jnp.where((lane >= place) & (lane < place + width), turned, moved)
    return moved[:, :lanes]


def cos_and_minus_sin(wavenum, points, columns, inverse):
    quarters = (4.0 * wavenum) * columns
    turns = jnp.floor(quarters * inverse + 0.5)
    angle = (quarters - turns * points) * (0.5 * math.pi * inverse)
    square = angle * angle
    sine = angle * (1.0 + square * (-1.0 / 6 + square * (1.0 / 120 + square * (-1.0 / 5040))))
    cosine = 1.0 + square * (
        -0.5 + square * (1.0 / 24 + square * (-1.0 / 720 + square * (1.0 / 40320)))
    )
    quadrant = turns.astype(jnp.int32)
    swap = (quadrant & 1) != 0
    new_cos = jnp.where(swap, sine, cosine)
    new_sin = jnp.where(swap, cosine, sine)
    new_cos = jnp.where(((quadrant + 1) & 2) != 0, -new_cos, new_cos)
    new_sin = jnp.where((quadrant & 2) != 0, new_sin, -new_sin)
    return new_cos, new_sin


def fill_tables(points_i, wavenum, coarse_ref, fine_ref, at):
    lanes = wavenum.shape[1]
    points = jnp.full((1, lanes), points_i, jnp.int32).astype(f32)
    inverse = 1.0 / points
    scale = jnp.where(2.0 * wavenum < points, 1.0 / jnp.sqrt(points), 0.0)

    def rows_of(count, step):
        return (lax.broadcasted_iota(jnp.int32, (count, lanes), 0) * step).astype(f32)

    coarse_rows = coarse_ref.shape[2]
    coarse_c, coarse_s = cos_and_minus_sin(wavenum, points, rows_of(coarse_rows, lane_width), inverse)
    coarse_ref[at, 0] = coarse_c * scale
    coarse_ref[at, 1] = coarse_s * scale
    mid_c, mid_s = cos_and_minus_sin(wavenum, points, rows_of(lane_width // 8, 8), inverse)
    unit_c, unit_s = cos_and_minus_sin(wavenum, points, rows_of(8, 1), inverse)
    for g in range(lane_width // 16):
        pieces_c = []
        pieces_s = []
        for a in (2 * g, 2 * g + 1):
            step_c = mid_c[a : a + 1]
            step_s = mid_s[a : a + 1]
            pieces_c.append(step_c * unit_c - step_s * unit_s)
            pieces_s.append(step_c * unit_s + step_s * unit_c)
        fine_ref[at, 0, 16 * g : 16 * g + 16] = jnp.concatenate(pieces_c, 0).astype(bf16)
        fine_ref[at, 1, 16 * g : 16 * g + 16] = jnp.concatenate(pieces_s, 0).astype(bf16)


def analyse_kernel(
    pack,
    wire_pack,
    groups,
    bands,
    owners,
    pairs_held,
    pairs_part,
    degree_count,
    nodes_ref,
    states_ref,
    wire_ref,
    coarse_ref,
    fine_ref,
    mask_ref,
    rows_scr,
    wide_scr,
    flat_scr,
):
    share, panel_rows, extent = states_ref.shape
    steps = extent // lane_width
    half_lanes = coarse_ref.shape[3] // 2
    first_cycle = lax.axis_index(group_axes) * share
    column = lax.broadcasted_iota(jnp.int32, (1, extent), 1)
    wavenum = own_wavenumbers(
        2 * half_lanes, pack, bands, owners, pairs_held, pairs_part, groups, degree_count
    )
    for il in range(share):
        points_i = nodes_ref[first_cycle + il]
        fill_tables(points_i, wavenum, coarse_ref, fine_ref, il)
        held = column < points_i
        mask_ref[il : il + 1, :] = held.astype(f32)
        panel = jnp.where(held, states_ref[il].astype(f32), 0.0)
        stacked = jnp.concatenate(
            [panel[:, lane_width * j : lane_width * (j + 1)] for j in range(steps)], axis=0
        ).astype(bf16)
        for h in range(2):
            lanes = slice(h * half_lanes, (h + 1) * half_lanes)
            part_c = dot_nn(stacked, fine_ref[il, 0, :, lanes])
            part_s = dot_nn(stacked, fine_ref[il, 1, :, lanes])
            total_c = jnp.zeros((panel_rows, half_lanes), f32)
            total_s = jnp.zeros((panel_rows, half_lanes), f32)
            for j in range(steps):
                turn_c = coarse_ref[il, 0, j : j + 1, lanes]
                turn_s = coarse_ref[il, 1, j : j + 1, lanes]
                piece_c = part_c[j * panel_rows : (j + 1) * panel_rows]
                piece_s = part_s[j * panel_rows : (j + 1) * panel_rows]
                total_c = total_c + (turn_c * piece_c - turn_s * piece_s)
                total_s = total_s + (turn_c * piece_s + turn_s * piece_c)
            at = (il * 2 + h) * 2 * panel_rows
            rows_scr[at : at + panel_rows, :] = total_c
            rows_scr[at + panel_rows : at + 2 * panel_rows, :] = total_s
    sources = bands * owners
    rows = groups * pairs_part // pack
    width = sources * rows
    count = rows_scr.shape[0]
    parts = pack // wire_pack
    values = rows_scr[...]
    if wide_scr.shape[0] > wire_pack * count:
        wide_scr[wire_pack * count :, :] = jnp.zeros_like(wide_scr[wire_pack * count :, :])
    for d in range(wire_pack):
        moves = [((e * wire_pack + d) * width, width, e * width) for e in range(parts)]
        wide_scr[d * count : (d + 1) * count, :] = move_lanes(values, moves, wide_scr.shape[1])
    flat_scr[...] = jnp.transpose(wide_scr[...])
    for source in range(sources):
        starts = [(e * sources + source) * rows for e in range(parts)]
        wire_ref[source] = jnp.concatenate(
            [flat_scr[at : at + rows, :] for at in starts], axis=0
        ).astype(bf16)


def take_block(rows, index, width, lanes):
    if width % lane_width == 0:
        return rows[:, index * width : (index + 1) * width]
    total = rows.shape[1]
    if index > 0:
        rows = pltpu.roll(rows, total - index * width, 1)
    return rows[:, :lanes]


def join_blocks(blocks, width, total):
    if width % lane_width == 0:
        return jnp.concatenate(blocks, axis=1)
    joined = jnp.zeros((blocks[0].shape[0], total), f32)
    lane = lax.broadcasted_iota(jnp.int32, joined.shape, 1)
    for index, block in enumerate(blocks):
        wide = jnp.concatenate([block] * (total // block.shape[1]), axis=1)
        if index > 0:
            wide = pltpu.roll(wide, index * width, 1)
        here = (lane >= index * width) & (lane < (index + 1) * width)
        joined = jnp.where(here, wide, joined)
    return joined


def pair_tables(own, parts, groups, j, row, q):
    blocks = [own[row + q]] + [t[q] for t in parts[j::groups]]
    return jnp.concatenate([b.astype(f32) for b in blocks], axis=0).astype(bf16)


def pair_sides(pair, slot, degree_count):
    low_side = slot < degree_count - pair
    low_weight = jnp.where(pair == 0, 1.0, 2.0)
    high_weight = jnp.where(2 * pair == degree_count - 1, 0.0, 2.0)
    return low_side, low_weight, high_weight


def project_kernel(pack, wire_pack, groups, bands, owners, pairs_held, share, wire_ref, own_ref, *refs):
    remote = groups * (bands - 1)
    part_refs = refs[:remote]
    coef_ref, spectra_ref, flat_scr, left_scr = refs[remote:]
    sources, wire_rows, _ = wire_ref.shape
    pairs_sub = own_ref.shape[0]
    high_places = pairs_sub // pack
    slot_count = own_ref.shape[2]
    degree_count = slot_count - 1
    panel_rows = coef_ref.shape[2]
    fields = panel_rows // 2
    block_rows = 4 * panel_rows
    pairs_part = pairs_sub // groups
    group = lax.axis_index("groups")
    band = lax.axis_index("band")
    first = lax.axis_index(owner_axes) * pairs_held + band * pairs_sub
    for k in range(bands):
        other = band ^ k
        for w in range(owners):
            at = (k * owners + w) * wire_rows
            rows = wire_ref[other * owners + w].astype(f32)
            for c in range(flat_scr.shape[0]):
                flat_scr[c, at : at + wire_rows, :] = rows[:, c * lane_width : (c + 1) * lane_width]
    slot = lax.broadcasted_iota(jnp.int32, (panel_rows, slot_count), 1)
    row = lax.broadcasted_iota(jnp.int32, (panel_rows, slot_count // 2), 0)
    zero = jnp.zeros((panel_rows, slot_count), f32)
    high_power, high_cross = zero, zero
    all_power, all_cross = zero, zero
    for j in range(groups):
        part_row = (group ^ j) * pairs_part
        low_power, low_cross = zero, zero
        for q in reversed(range(pairs_part)):
            place = j * pairs_part + q
            high_place, low_place = divmod(place, pack)
            wire_row = low_place // wire_pack * high_places + high_place
            received = jnp.concatenate(
                [
                    flat_scr[c, pl.ds(wire_row, sources, stride=wire_rows), :]
                    for c in range(flat_scr.shape[0])
                ],
                axis=1,
            )
            for il in range(share):
                left_scr[place, pl.ds(il, sources, stride=share), :] = take_block(
                    received, low_place % wire_pack * share + il, block_rows, left_scr.shape[2]
                )
            left = left_scr[place, :, 0:block_rows].astype(bf16)
            both_halves = dot_tn(
                left, pair_tables(own_ref, part_refs, groups, j, part_row, q)
            )
            pair = first + part_row + q
            low_side, low_weight, high_weight = pair_sides(pair, slot, degree_count)
            cosines = jnp.where(
                low_side, both_halves[0:panel_rows], both_halves[2 * panel_rows : 3 * panel_rows]
            )
            sines = jnp.where(
                low_side, both_halves[panel_rows : 2 * panel_rows], both_halves[3 * panel_rows :]
            )
            coef_ref[place, 0] = cosines
            coef_ref[place, 1] = sines
            weight = jnp.where(low_side, low_weight, high_weight)
            power = (cosines * cosines + sines * sines) * weight
            cross = (
                cosines * pltpu.roll(cosines, fields, 0) + sines * pltpu.roll(sines, fields, 0)
            ) * weight
            low_power = pltpu.roll(low_power, 1, 1) + jnp.where(low_side, power, 0.0)
            low_cross = pltpu.roll(low_cross, 1, 1) + jnp.where(low_side, cross, 0.0)
            high_power = high_power + jnp.where(low_side, 0.0, power)
            high_cross = high_cross + jnp.where(low_side, 0.0, cross)
        all_power = all_power + pltpu.roll(low_power, first + part_row, 1)
        all_cross = all_cross + pltpu.roll(low_cross, first + part_row, 1)
    all_power = all_power + pltpu.roll(high_power, slot_count - 1, 1)
    all_cross = all_cross + pltpu.roll(high_cross, slot_count - 1, 1)
    spectra_ref[:, 0:slot_count] = all_power
    spectra_ref[:, slot_count:] = jnp.where(
        row < fields, all_cross[:, : slot_count // 2], all_cross[:, slot_count // 2 :]
    )


def tree_sum(parts):
    while len(parts) > 1:
        parts = [parts[i] + parts[i + 1] for i in range(0, len(parts), 2)]
    return parts[0]


def gradient_kernel(pack, groups, bands, owners, pairs_held, share, spectra_parts, own_ref, coef_ref, *refs):
    remote = groups * (bands - 1)
    spectra_refs = refs[:spectra_parts]
    part_refs = refs[spectra_parts : spectra_parts + remote]
    wire_ref, misfit_ref, flat_scr, cycle_scr = refs[spectra_parts + remote :]
    sources, wire_rows, wire_lanes = wire_ref.shape
    pairs_sub = own_ref.shape[0]
    slot_count = own_ref.shape[2]
    degree_count = slot_count - 1
    panel_rows = coef_ref.shape[2]
    fields = panel_rows // 2
    block_rows = 4 * fields
    fields_out = fields // bands
    pairs_part = pairs_sub // groups
    group = lax.axis_index("groups")
    band = lax.axis_index("band")
    first = lax.axis_index(owner_axes) * pairs_held + band * pairs_sub
    slot = lax.broadcasted_iota(jnp.int32, (panel_rows, slot_count), 1)
    row = lax.broadcasted_iota(jnp.int32, (panel_rows, slot_count), 0)
    spectra = tree_sum([s[...] for s in spectra_refs])
    power = spectra[:, :slot_count]
    packed = spectra[:, slot_count:]
    turned = pltpu.roll(packed, fields, 0)
    upper = row[:, : slot_count // 2] < fields
    cross = jnp.concatenate([jnp.where(upper, packed, turned), jnp.where(upper, turned, packed)], axis=1)
    odd_weight = (2 * slot + 1).astype(f32)
    power = power / odd_weight + spectrum_floor
    cross = cross / odd_weight
    root = jnp.sqrt(power)
    other_root = pltpu.roll(root, fields, 0)
    both_power = power + pltpu.roll(power, fields, 0)
    geo_mean = root * other_root
    coherence = cross / geo_mean
    term = (root - other_root) * (root - other_root) + both_power * (1.0 - coherence)
    term = jnp.where(slot < degree_count, term, 0.0)
    mean = jnp.sum(term, axis=1, keepdims=True) / degree_count
    field_row = lax.broadcasted_iota(jnp.int32, (panel_rows, 1), 0)
    misfit_ref[...] = jnp.zeros_like(misfit_ref)
    for i in range(fields_out):
        chosen = jnp.where(field_row == band * fields_out + i, mean, 0.0)
        misfit_ref[i : i + 1, :] = jnp.broadcast_to(
            jnp.sum(chosen, axis=0, keepdims=True), (1, lane_width)
        )
    grad_power = (
        gradient_gain
        * (
            1.0
            - other_root / root
            + (1.0 - coherence)
            + both_power * coherence / (2.0 * power)
        )
        / odd_weight
    )
    grad_cross = -gradient_gain * both_power / geo_mean / odd_weight
    by_degree = jnp.where(row < fields, 2.0 * grad_power, grad_cross)
    high_grad = pltpu.roll(by_degree, 1, 1)
    blocks = []
    for j in range(groups):
        part_row = (group ^ j) * pairs_part
        low_grad = pltpu.roll(by_degree, slot_count - first - part_row, 1)
        for q in range(pairs_part):
            place = j * pairs_part + q
            pair = first + part_row + q
            low_side, low_weight, high_weight = pair_sides(pair, slot, degree_count)
            gain = jnp.where(low_side, low_grad * low_weight, high_grad * high_weight)
            cosines = coef_ref[place, 0] * gain
            sines = coef_ref[place, 1] * gain
            cosines = cosines + pltpu.roll(cosines, fields, 0)
            sines = sines + pltpu.roll(sines, fields, 0)
            grads = jnp.where(row < fields, cosines, sines)
            masked = jnp.concatenate(
                [jnp.where(low_side, grads, 0.0), jnp.where(low_side, 0.0, grads)], axis=0
            ).astype(bf16)
            cycle_scr[place, :, 0:block_rows] = dot_nt(
                pair_tables(own_ref, part_refs, groups, j, part_row, q), masked
            )
            high_place, low_place = divmod(place, pack)
            blocks = [] if low_place == 0 else blocks
            blocks += [cycle_scr[place, pl.ds(il, sources, stride=share), :] for il in range(share)]
            if low_place == pack - 1:
                joined = join_blocks(blocks, block_rows, wire_lanes)
                for c in range(flat_scr.shape[0]):
                    flat_scr[c, pl.ds(high_place, sources, stride=wire_rows), :] = joined[
                        :, c * lane_width : (c + 1) * lane_width
                    ]
            low_grad = pltpu.roll(low_grad, slot_count - 1, 1)
    for k in range(bands):
        other = band ^ k
        for w in range(owners):
            at = (k * owners + w) * wire_rows
            wire_ref[other * owners + w] = jnp.concatenate(
                [flat_scr[c, at : at + wire_rows, :] for c in range(flat_scr.shape[0])], axis=1
            ).astype(bf16)


def synthesise_kernel(pack, coarse_ref, fine_ref, mask_ref, wire_ref, out_ref, flat_scr):
    share, fields, extent = out_ref.shape
    sources, wire_rows, wire_lanes = wire_ref.shape
    steps = extent // lane_width
    half_lanes = coarse_ref.shape[3] // 2
    panel_rows = 2 * fields
    width = sources * wire_rows
    for source in range(sources):
        flat_scr[source * wire_rows : (source + 1) * wire_rows, :] = wire_ref[source].astype(f32)
    if flat_scr.shape[0] > width:
        flat_scr[width:, :] = jnp.zeros_like(flat_scr[width:, :])
    turned = jnp.transpose(flat_scr[...])
    count = wire_lanes // pack
    if pack > 1:
        spare = jnp.zeros((count, round_up(half_lanes, lane_width) - turned.shape[1]), f32)
        values = jnp.zeros((count, half_lanes), f32)
        for low_place in range(pack):
            block = jnp.concatenate([turned[low_place * count : (low_place + 1) * count], spare], axis=1)
            values = values + move_lanes(block, [(0, width, low_place * width)], half_lanes)
    else:
        values = turned[:, :half_lanes]
    row = lax.broadcasted_iota(jnp.int32, (panel_rows, half_lanes), 0)
    for il in range(share):
        total_c = jnp.zeros((steps * panel_rows, lane_width), f32)
        total_s = jnp.zeros((steps * panel_rows, lane_width), f32)
        for h in range(2):
            lanes = slice(h * half_lanes, (h + 1) * half_lanes)
            at = (il * 2 + h) * panel_rows
            direct = values[at : at + panel_rows]
            crossed = pltpu.roll(direct, fields, 0)
            crossed = jnp.where(row < fields, crossed, -crossed)
            pieces = [
                direct * coarse_ref[il, 0, j : j + 1, lanes] + crossed * coarse_ref[il, 1, j : j + 1, lanes]
                for j in range(steps)
            ]
            pieces = jnp.concatenate(pieces, 0).astype(bf16)
            total_c = total_c + dot_nt(pieces, fine_ref[il, 0, :, lanes])
            total_s = total_s + dot_nt(pieces, fine_ref[il, 1, :, lanes])
        mask = mask_ref[il : il + 1, :]
        for j in range(steps):
            lanes = slice(lane_width * j, lane_width * (j + 1))
            at = j * panel_rows
            piece = total_c[at : at + fields] + total_s[at + fields : at + panel_rows]
            out_ref[il, :, lanes] = (piece * mask[:, lanes]).astype(bf16)


def call(body, name, arrays, spaces, out_shapes, scratch, flops=1):
    return pl.pallas_call(
        body,
        name=name,
        cost_estimate=pl.CostEstimate(flops=flops, transcendentals=0, bytes_accessed=1),
        in_specs=[pl.BlockSpec(memory_space=space) for space in spaces],
        out_specs=tuple(pl.BlockSpec(memory_space=pltpu.VMEM) for _ in out_shapes),
        out_shape=tuple(out_shapes),
        scratch_shapes=scratch,
        compiler_params=pltpu.CompilerParams(vmem_limit_bytes=vmem_bytes),
    )(*arrays)


def exchange(array, axes, count):
    return [array] + [
        lax.ppermute(array, axes, [(i, i ^ k) for i in range(count)]) for k in range(1, count)
    ]


def per_device(predicted_state, analysis_state, nodes_per_parallel, weighted_harmonic_table):
    share, fields, extent = predicted_state.shape
    pairs_held, cycle_band, slot_count = weighted_harmonic_table.shape
    groups = lax.axis_size("groups")
    bands = lax.axis_size("band")
    owners = lax.axis_size(owner_axes)
    group = lax.axis_index("groups")
    band = lax.axis_index("band")
    sources = bands * owners
    pairs_part = -(-pairs_held // (bands * groups))
    pairs_sub = groups * pairs_part
    panel_rows = 2 * fields
    pack = max(1, lane_width // (share * 4 * fields))
    wire_pack = 1
    wire_lanes = round_up(wire_pack * share * 4 * panel_rows, lane_width)
    back_lanes = round_up(pack * share * 4 * fields, lane_width)
    block_lanes = round_up(4 * panel_rows, lane_width)
    half_lanes = sources * pairs_sub
    coarse_rows = round_up(extent // lane_width, 8)

    table = weighted_harmonic_table
    if pairs_sub * bands != pairs_held:
        table = jnp.pad(table, ((0, pairs_sub * bands - pairs_held), (0, 0), (0, 0)))
    own_table = lax.dynamic_slice_in_dim(table, band * pairs_sub, pairs_sub, 0)

    def over_bands(array, k):
        return lax.ppermute(array, "band", [(i, i ^ k) for i in range(bands)])

    starts = [((band ^ k) * groups + (group ^ j)) * pairs_part for k in range(1, bands) for j in range(groups)]
    pieces = [
        lax.dynamic_slice_in_dim(table, start, pairs_part, 0)
        for n, start in enumerate(starts)
        if n < groups or n % groups == 0
    ]
    pieces = lax.optimization_barrier(pieces)
    near = [over_bands(piece, 1) for piece in pieces[:groups]]
    far = [over_bands(piece, n + 2) for n, piece in enumerate(pieces[groups:])]
    states = jnp.concatenate([predicted_state, analysis_state], axis=1)
    wire, coarse, fine, mask = call(
        functools.partial(
            analyse_kernel,
            pack,
            wire_pack,
            groups,
            bands,
            owners,
            pairs_held,
            pairs_part,
            slot_count - 1,
        ),
        "analyse",
        (nodes_per_parallel, states),
        (pltpu.SMEM, pltpu.VMEM),
        (
            jax.ShapeDtypeStruct((sources, pairs_sub // wire_pack, wire_lanes), bf16),
            jax.ShapeDtypeStruct((share, 2, coarse_rows, 2 * half_lanes), f32),
            jax.ShapeDtypeStruct((share, 2, lane_width, 2 * half_lanes), bf16),
            jax.ShapeDtypeStruct((share, extent), f32),
        ),
        [
            pltpu.VMEM((share * 4 * panel_rows, half_lanes), f32),
            pltpu.VMEM((wire_lanes, round_up(half_lanes // wire_pack, lane_width)), f32),
            pltpu.VMEM((round_up(half_lanes // wire_pack, lane_width), wire_lanes), f32),
        ],
    )
    wire = lax.all_to_all(wire, group_axes, 0, 0, tiled=True)
    parts = list(near)
    for piece in far:
        parts.append(piece)
        for j in range(1, groups):
            parts.append(lax.ppermute(piece, "groups", [(i, i ^ j) for i in range(groups)]))
    block_scratch = pltpu.VMEM((pairs_sub, bands * cycle_band, block_lanes), f32)
    coef, spectra = call(
        functools.partial(project_kernel, pack, wire_pack, groups, bands, owners, pairs_held, share),
        "project",
        (wire, own_table, *parts),
        (pltpu.VMEM,) * (2 + len(parts)),
        (
            jax.ShapeDtypeStruct((pairs_sub, 2, panel_rows, slot_count), f32),
            jax.ShapeDtypeStruct((panel_rows, slot_count + slot_count // 2), f32),
        ),
        [
            pltpu.VMEM((wire_lanes // lane_width, half_lanes // wire_pack, lane_width), f32),
            block_scratch,
        ],
    )
    spectra = tree_sum(exchange(spectra, owner_axes, owners))
    spectra = exchange(spectra, "band", bands)
    wire, misfit = call(
        functools.partial(gradient_kernel, pack, groups, bands, owners, pairs_held, share, len(spectra)),
        "gradient",
        (own_table, coef, *spectra, *parts),
        (pltpu.VMEM,) * (2 + len(spectra) + len(parts)),
        (
            jax.ShapeDtypeStruct((sources, pairs_sub // pack, back_lanes), bf16),
            jax.ShapeDtypeStruct((round_up(fields // bands, 8), lane_width), f32),
        ),
        [
            pltpu.VMEM((back_lanes // lane_width, half_lanes // pack, lane_width), f32),
            block_scratch,
        ],
    )
    wire = lax.all_to_all(wire, group_axes, 0, 0, tiled=True)
    (sensitivity,) = call(
        functools.partial(synthesise_kernel, pack),
        "synthesise",
        (coarse, fine, mask, wire),
        (pltpu.VMEM,) * 4,
        (jax.ShapeDtypeStruct((share, fields, extent), bf16),),
        [pltpu.VMEM((round_up(half_lanes // pack, lane_width), back_lanes), f32)],
    )
    return misfit[: fields // bands, 0], sensitivity


def solution(mesh):
    in_specs = (
        P(("groups", "band", "field", "wave"), None, None),
        P(("groups", "band", "field", "wave"), None, None),
        P(),
        P(("field", "wave"), "band", None),
    )
    out_specs = (P(("groups", "band")), P(("groups", "band", "field", "wave"), None, None))
    return jax.shard_map(
        per_device, mesh=mesh, in_specs=in_specs, out_specs=out_specs, check_vma=False
    )
```

```python
import functools
import math

import jax
import jax.numpy as jnp
from jax import lax
from jax.experimental import pallas as pl
from jax.experimental.pallas import tpu as pltpu
from jax.sharding import PartitionSpec as P

spectrum_floor = 0.25
gradient_gain = 16.0
lane_width = 128
vmem_bytes = 40 * 1024 * 1024
owner_axes = ("field", "wave")
group_axes = ("band", "field", "wave")
bf16 = jnp.bfloat16
f32 = jnp.float32


def round_up(value, step):
    return -(-value // step) * step


def dot_nn(left, right):
    return lax.dot_general(left, right, (((1,), (0,)), ((), ())), preferred_element_type=f32)


def dot_nt(left, right):
    return lax.dot_general(left, right, (((1,), (1,)), ((), ())), preferred_element_type=f32)


def dot_tn(left, right):
    return lax.dot_general(left, right, (((0,), (0,)), ((), ())), preferred_element_type=f32)


def split_index(index, size):
    whole = jnp.floor((index + 0.5) * (1.0 / size))
    return whole, index - whole * size


def wavenumbers(owner, band, half, rest, pairs_held, pairs_part, groups, degree_count):
    part, pair = split_index(rest, pairs_part)
    part = (lax.axis_index("groups") ^ part.astype(jnp.int32)).astype(f32)
    within = (band * groups + part) * pairs_part + pair
    pair = owner * pairs_held + within
    mirrored = degree_count - 1.0 - pair
    wavenum = jnp.where(half > 0.0, mirrored, pair)
    void = (within >= pairs_held) | ((half > 0.0) & (mirrored == pair))
    return jnp.where(void, 4.0 * degree_count, wavenum)


def own_wavenumbers(lanes, pack, bands, owners, pairs_held, pairs_part, groups, degree_count):
    index = lax.broadcasted_iota(jnp.int32, (1, lanes), 1).astype(f32)
    half, index = split_index(index, lanes // 2)
    rows = groups * pairs_part // pack
    low_place, index = split_index(index, bands * owners * rows)
    block, high_place = split_index(index, rows)
    band, owner = split_index(block, owners)
    rest = high_place * pack + low_place
    return wavenumbers(owner, band, half, rest, pairs_held, pairs_part, groups, degree_count)


def move_lanes(values, moves, lanes):
    total = values.shape[1]
    moved = jnp.zeros(values.shape, f32)
    lane = lax.broadcasted_iota(jnp.int32, values.shape, 1)
    for start, width, place in moves:
        shift = (place - start) % total
        turned = pltpu.roll(values, shift, 1) if shift else values
        moved = jnp.where((lane >= place) & (lane < place + width), turned, moved)
    return moved[:, :lanes]


def cos_and_minus_sin(wavenum, points, columns, inverse):
    quarters = (4.0 * wavenum) * columns
    turns = jnp.floor(quarters * inverse + 0.5)
    angle = (quarters - turns * points) * (0.5 * math.pi * inverse)
    square = angle * angle
    sine = angle * (1.0 + square * (-1.0 / 6 + square * (1.0 / 120 + square * (-1.0 / 5040))))
    cosine = 1.0 + square * (
        -0.5 + square * (1.0 / 24 + square * (-1.0 / 720 + square * (1.0 / 40320)))
    )
    quadrant = turns.astype(jnp.int32)
    swap = (quadrant & 1) != 0
    new_cos = jnp.where(swap, sine, cosine)
    new_sin = jnp.where(swap, cosine, sine)
    new_cos = jnp.where(((quadrant + 1) & 2) != 0, -new_cos, new_cos)
    new_sin = jnp.where((quadrant & 2) != 0, new_sin, -new_sin)
    return new_cos, new_sin


def fill_tables(points_i, wavenum, coarse_ref, fine_ref, at):
    lanes = wavenum.shape[1]
    points = jnp.full((1, lanes), points_i, jnp.int32).astype(f32)
    inverse = 1.0 / points
    scale = jnp.where(2.0 * wavenum < points, 1.0 / jnp.sqrt(points), 0.0)

    def rows_of(count, step):
        return (lax.broadcasted_iota(jnp.int32, (count, lanes), 0) * step).astype(f32)

    coarse_rows = coarse_ref.shape[2]
    coarse_c, coarse_s = cos_and_minus_sin(wavenum, points, rows_of(coarse_rows, lane_width), inverse)
    coarse_ref[at, 0] = coarse_c * scale
    coarse_ref[at, 1] = coarse_s * scale
    mid_c, mid_s = cos_and_minus_sin(wavenum, points, rows_of(lane_width // 8, 8), inverse)
    unit_c, unit_s = cos_and_minus_sin(wavenum, points, rows_of(8, 1), inverse)
    for g in range(lane_width // 16):
        pieces_c = []
        pieces_s = []
        for a in (2 * g, 2 * g + 1):
            step_c = mid_c[a : a + 1]
            step_s = mid_s[a : a + 1]
            pieces_c.append(step_c * unit_c - step_s * unit_s)
            pieces_s.append(step_c * unit_s + step_s * unit_c)
        fine_ref[at, 0, 16 * g : 16 * g + 16] = jnp.concatenate(pieces_c, 0).astype(bf16)
        fine_ref[at, 1, 16 * g : 16 * g + 16] = jnp.concatenate(pieces_s, 0).astype(bf16)


def analyse_kernel(
    pack,
    wire_pack,
    groups,
    bands,
    owners,
    pairs_held,
    pairs_part,
    degree_count,
    nodes_ref,
    states_ref,
    wire_ref,
    coarse_ref,
    fine_ref,
    mask_ref,
    rows_scr,
    wide_scr,
    flat_scr,
):
    share, panel_rows, extent = states_ref.shape
    steps = extent // lane_width
    half_lanes = coarse_ref.shape[3] // 2
    first_cycle = lax.axis_index(group_axes) * share
    column = lax.broadcasted_iota(jnp.int32, (1, extent), 1)
    wavenum = own_wavenumbers(
        2 * half_lanes, pack, bands, owners, pairs_held, pairs_part, groups, degree_count
    )
    for il in range(share):
        points_i = nodes_ref[first_cycle + il]
        fill_tables(points_i, wavenum, coarse_ref, fine_ref, il)
        held = column < points_i
        mask_ref[il : il + 1, :] = held.astype(f32)
        panel = jnp.where(held, states_ref[il].astype(f32), 0.0)
        stacked = jnp.concatenate(
            [panel[:, lane_width * j : lane_width * (j + 1)] for j in range(steps)], axis=0
        ).astype(bf16)
        for h in range(2):
            lanes = slice(h * half_lanes, (h + 1) * half_lanes)
            part_c = dot_nn(stacked, fine_ref[il, 0, :, lanes])
            part_s = dot_nn(stacked, fine_ref[il, 1, :, lanes])
            total_c = jnp.zeros((panel_rows, half_lanes), f32)
            total_s = jnp.zeros((panel_rows, half_lanes), f32)
            for j in range(steps):
                turn_c = coarse_ref[il, 0, j : j + 1, lanes]
                turn_s = coarse_ref[il, 1, j : j + 1, lanes]
                piece_c = part_c[j * panel_rows : (j + 1) * panel_rows]
                piece_s = part_s[j * panel_rows : (j + 1) * panel_rows]
                total_c = total_c + (turn_c * piece_c - turn_s * piece_s)
                total_s = total_s + (turn_c * piece_s + turn_s * piece_c)
            at = (il * 2 + h) * 2 * panel_rows
            rows_scr[at : at + panel_rows, :] = total_c
            rows_scr[at + panel_rows : at + 2 * panel_rows, :] = total_s
    sources = bands * owners
    rows = groups * pairs_part // pack
    width = sources * rows
    count = rows_scr.shape[0]
    parts = pack // wire_pack
    values = rows_scr[...]
    if wide_scr.shape[0] > wire_pack * count:
        wide_scr[wire_pack * count :, :] = jnp.zeros_like(wide_scr[wire_pack * count :, :])
    for d in range(wire_pack):
        moves = [((e * wire_pack + d) * width, width, e * width) for e in range(parts)]
        wide_scr[d * count : (d + 1) * count, :] = move_lanes(values, moves, wide_scr.shape[1])
    flat_scr[...] = jnp.transpose(wide_scr[...])
    for source in range(sources):
        starts = [(e * sources + source) * rows for e in range(parts)]
        wire_ref[source] = jnp.concatenate(
            [flat_scr[at : at + rows, :] for at in starts], axis=0
        ).astype(bf16)


def take_block(rows, index, width, lanes):
    if width % lane_width == 0:
        return rows[:, index * width : (index + 1) * width]
    total = rows.shape[1]
    if index > 0:
        rows = pltpu.roll(rows, total - index * width, 1)
    return rows[:, :lanes]


def join_blocks(blocks, width, total):
    if width % lane_width == 0:
        return jnp.concatenate(blocks, axis=1)
    joined = jnp.zeros((blocks[0].shape[0], total), f32)
    lane = lax.broadcasted_iota(jnp.int32, joined.shape, 1)
    for index, block in enumerate(blocks):
        wide = jnp.concatenate([block] * (total // block.shape[1]), axis=1)
        if index > 0:
            wide = pltpu.roll(wide, index * width, 1)
        here = (lane >= index * width) & (lane < (index + 1) * width)
        joined = jnp.where(here, wide, joined)
    return joined


def pair_sides(pair, slot, degree_count):
    low_side = slot < degree_count - pair
    low_weight = jnp.where(pair == 0, 1.0, 2.0)
    high_weight = jnp.where(2 * pair == degree_count - 1, 0.0, 2.0)
    return low_side, low_weight, high_weight


def project_kernel(
    pack,
    wire_pack,
    groups,
    bands,
    owners,
    pairs_held,
    share,
    first_part,
    last_part,
    source_ref,
    own_ref,
    *refs,
):
    is_first = first_part == 0
    remote = (last_part - first_part) * (bands - 1)
    part_refs = refs[:remote]
    if is_first:
        coef_ref, table_ref, sums_ref, left_ref, flat_scr, left_scr = refs[remote:]
    else:
        earlier_ref, coef_ref, table_ref, spectra_ref = refs[remote:]
    pairs_sub, cycle_band, slot_count = own_ref.shape
    high_places = pairs_sub // pack
    degree_count = slot_count - 1
    panel_rows = coef_ref.shape[2]
    fields = panel_rows // 2
    block_rows = 4 * panel_rows
    pairs_part = pairs_sub // groups
    group = lax.axis_index("groups")
    band = lax.axis_index("band")
    first = lax.axis_index(owner_axes) * pairs_held + band * pairs_sub
    slot = lax.broadcasted_iota(jnp.int32, (panel_rows, slot_count), 1)
    row = lax.broadcasted_iota(jnp.int32, (panel_rows, slot_count // 2), 0)
    zero = jnp.zeros((panel_rows, slot_count), f32)
    high_power, high_cross = zero, zero
    all_power, all_cross = zero, zero
    if is_first:
        sources, wire_rows, _ = source_ref.shape
        for k in range(bands):
            other = band ^ k
            for w in range(owners):
                at = (k * owners + w) * wire_rows
                rows = source_ref[other * owners + w].astype(f32)
                for c in range(flat_scr.shape[0]):
                    flat_scr[c, at : at + wire_rows, :] = rows[:, c * lane_width : (c + 1) * lane_width]
        for place in range(pairs_sub):
            high_place, low_place = divmod(place, pack)
            wire_row = low_place // wire_pack * high_places + high_place
            received = jnp.concatenate(
                [
                    flat_scr[c, pl.ds(wire_row, sources, stride=wire_rows), :]
                    for c in range(flat_scr.shape[0])
                ],
                axis=1,
            )
            target, at = (left_scr, place) if place < pairs_part else (left_ref, place - pairs_part)
            for il in range(share):
                target[at, pl.ds(il, sources, stride=share), :] = take_block(
                    received, low_place % wire_pack * share + il, block_rows, left_scr.shape[2]
                )
        left_ref = left_scr
    else:
        left_ref = source_ref
        all_power, all_cross = earlier_ref[0], earlier_ref[1]
    for j in range(first_part, last_part):
        part_row = (group ^ j) * pairs_part
        low_power, low_cross = zero, zero
        for q in reversed(range(pairs_part)):
            at = (j - first_part) * pairs_part + q
            left = left_ref[at, :, 0:block_rows].astype(bf16)
            blocks = [own_ref[part_row + q]] + [t[q] for t in part_refs[j - first_part :: last_part - first_part]]
            table = jnp.concatenate([b.astype(f32) for b in blocks], axis=0).astype(bf16)
            table_ref[at] = table
            both_halves = dot_tn(left, table)
            pair = first + part_row + q
            low_side, low_weight, high_weight = pair_sides(pair, slot, degree_count)
            cosines = jnp.where(
                low_side, both_halves[0:panel_rows], both_halves[2 * panel_rows : 3 * panel_rows]
            )
            sines = jnp.where(
                low_side, both_halves[panel_rows : 2 * panel_rows], both_halves[3 * panel_rows :]
            )
            coef_ref[at, 0] = cosines
            coef_ref[at, 1] = sines
            weight = jnp.where(low_side, low_weight, high_weight)
            power = (cosines * cosines + sines * sines) * weight
            cross = (
                cosines * pltpu.roll(cosines, fields, 0) + sines * pltpu.roll(sines, fields, 0)
            ) * weight
            low_power = pltpu.roll(low_power, 1, 1) + jnp.where(low_side, power, 0.0)
            low_cross = pltpu.roll(low_cross, 1, 1) + jnp.where(low_side, cross, 0.0)
            high_power = high_power + jnp.where(low_side, 0.0, power)
            high_cross = high_cross + jnp.where(low_side, 0.0, cross)
        all_power = all_power + pltpu.roll(low_power, first + part_row, 1)
        all_cross = all_cross + pltpu.roll(low_cross, first + part_row, 1)
    all_power = all_power + pltpu.roll(high_power, slot_count - 1, 1)
    all_cross = all_cross + pltpu.roll(high_cross, slot_count - 1, 1)
    if is_first:
        sums_ref[0] = all_power
        sums_ref[1] = all_cross
    else:
        spectra_ref[:, 0:slot_count] = all_power
        spectra_ref[:, slot_count:] = jnp.where(
            row < fields, all_cross[:, : slot_count // 2], all_cross[:, slot_count // 2 :]
        )


def tree_sum(parts):
    while len(parts) > 1:
        parts = [parts[i] + parts[i + 1] for i in range(0, len(parts), 2)]
    return parts[0]


def gradient_kernel(pack, groups, bands, owners, pairs_held, share, spectra_parts, *refs):
    spectra_refs = refs[:spectra_parts]
    coef_refs = refs[spectra_parts : spectra_parts + 2]
    table_refs = refs[spectra_parts + 2 : spectra_parts + 4]
    wire_ref, misfit_ref, flat_scr, cycle_scr = refs[spectra_parts + 4 :]
    sources, wire_rows, wire_lanes = wire_ref.shape
    pairs_part = coef_refs[0].shape[0]
    pairs_sub = groups * pairs_part
    slot_count = table_refs[0].shape[2]
    degree_count = slot_count - 1
    panel_rows = coef_refs[0].shape[2]
    fields = panel_rows // 2
    block_rows = 4 * fields
    fields_out = fields // bands
    group = lax.axis_index("groups")
    band = lax.axis_index("band")
    first = lax.axis_index(owner_axes) * pairs_held + band * pairs_sub
    slot = lax.broadcasted_iota(jnp.int32, (panel_rows, slot_count), 1)
    row = lax.broadcasted_iota(jnp.int32, (panel_rows, slot_count), 0)
    spectra = tree_sum([s[...] for s in spectra_refs])
    power = spectra[:, :slot_count]
    packed = spectra[:, slot_count:]
    turned = pltpu.roll(packed, fields, 0)
    upper = row[:, : slot_count // 2] < fields
    cross = jnp.concatenate([jnp.where(upper, packed, turned), jnp.where(upper, turned, packed)], axis=1)
    odd_weight = (2 * slot + 1).astype(f32)
    power = power / odd_weight + spectrum_floor
    cross = cross / odd_weight
    root = jnp.sqrt(power)
    other_root = pltpu.roll(root, fields, 0)
    both_power = power + pltpu.roll(power, fields, 0)
    geo_mean = root * other_root
    coherence = cross / geo_mean
    term = (root - other_root) * (root - other_root) + both_power * (1.0 - coherence)
    term = jnp.where(slot < degree_count, term, 0.0)
    mean = jnp.sum(term, axis=1, keepdims=True) / degree_count
    field_row = lax.broadcasted_iota(jnp.int32, (panel_rows, 1), 0)
    misfit_ref[...] = jnp.zeros_like(misfit_ref)
    for i in range(fields_out):
        chosen = jnp.where(field_row == band * fields_out + i, mean, 0.0)
        misfit_ref[i : i + 1, :] = jnp.broadcast_to(
            jnp.sum(chosen, axis=0, keepdims=True), (1, lane_width)
        )
    grad_power = (
        gradient_gain
        * (
            1.0
            - other_root / root
            + (1.0 - coherence)
            + both_power * coherence / (2.0 * power)
        )
        / odd_weight
    )
    grad_cross = -gradient_gain * both_power / geo_mean / odd_weight
    by_degree = jnp.where(row < fields, 2.0 * grad_power, grad_cross)
    high_grad = pltpu.roll(by_degree, 1, 1)
    blocks = []
    for j in range(groups):
        part_row = (group ^ j) * pairs_part
        low_grad = pltpu.roll(by_degree, slot_count - first - part_row, 1)
        for q in range(pairs_part):
            place = j * pairs_part + q
            at_part = (0, q) if j == 0 else (1, place - pairs_part)
            pair = first + part_row + q
            low_side, low_weight, high_weight = pair_sides(pair, slot, degree_count)
            gain = jnp.where(low_side, low_grad * low_weight, high_grad * high_weight)
            cosines = coef_refs[at_part[0]][at_part[1], 0] * gain
            sines = coef_refs[at_part[0]][at_part[1], 1] * gain
            cosines = cosines + pltpu.roll(cosines, fields, 0)
            sines = sines + pltpu.roll(sines, fields, 0)
            grads = jnp.where(row < fields, cosines, sines)
            masked = jnp.concatenate(
                [jnp.where(low_side, grads, 0.0), jnp.where(low_side, 0.0, grads)], axis=0
            ).astype(bf16)
            cycle_scr[place, :, 0:block_rows] = dot_nt(
                table_refs[at_part[0]][at_part[1]], masked
            )
            high_place, low_place = divmod(place, pack)
            blocks = [] if low_place == 0 else blocks
            blocks += [cycle_scr[place, pl.ds(il, sources, stride=share), :] for il in range(share)]
            if low_place == pack - 1:
                joined = join_blocks(blocks, block_rows, wire_lanes)
                for c in range(flat_scr.shape[0]):
                    flat_scr[c, pl.ds(high_place, sources, stride=wire_rows), :] = joined[
                        :, c * lane_width : (c + 1) * lane_width
                    ]
            low_grad = pltpu.roll(low_grad, slot_count - 1, 1)
    for k in range(bands):
        other = band ^ k
        for w in range(owners):
            at = (k * owners + w) * wire_rows
            wire_ref[other * owners + w] = jnp.concatenate(
                [flat_scr[c, at : at + wire_rows, :] for c in range(flat_scr.shape[0])], axis=1
            ).astype(bf16)


def synthesise_kernel(pack, coarse_ref, fine_ref, mask_ref, wire_ref, out_ref, flat_scr):
    share, fields, extent = out_ref.shape
    sources, wire_rows, wire_lanes = wire_ref.shape
    steps = extent // lane_width
    half_lanes = coarse_ref.shape[3] // 2
    panel_rows = 2 * fields
    width = sources * wire_rows
    for source in range(sources):
        flat_scr[source * wire_rows : (source + 1) * wire_rows, :] = wire_ref[source].astype(f32)
    if flat_scr.shape[0] > width:
        flat_scr[width:, :] = jnp.zeros_like(flat_scr[width:, :])
    turned = jnp.transpose(flat_scr[...])
    count = wire_lanes // pack
    if pack > 1:
        spare = jnp.zeros((count, round_up(half_lanes, lane_width) - turned.shape[1]), f32)
        values = jnp.zeros((count, half_lanes), f32)
        for low_place in range(pack):
            block = jnp.concatenate([turned[low_place * count : (low_place + 1) * count], spare], axis=1)
            values = values + move_lanes(block, [(0, width, low_place * width)], half_lanes)
    else:
        values = turned[:, :half_lanes]
    row = lax.broadcasted_iota(jnp.int32, (panel_rows, half_lanes), 0)
    for il in range(share):
        total_c = jnp.zeros((steps * panel_rows, lane_width), f32)
        total_s = jnp.zeros((steps * panel_rows, lane_width), f32)
        for h in range(2):
            lanes = slice(h * half_lanes, (h + 1) * half_lanes)
            at = (il * 2 + h) * panel_rows
            direct = values[at : at + panel_rows]
            crossed = pltpu.roll(direct, fields, 0)
            crossed = jnp.where(row < fields, crossed, -crossed)
            pieces = [
                direct * coarse_ref[il, 0, j : j + 1, lanes] + crossed * coarse_ref[il, 1, j : j + 1, lanes]
                for j in range(steps)
            ]
            pieces = jnp.concatenate(pieces, 0).astype(bf16)
            total_c = total_c + dot_nt(pieces, fine_ref[il, 0, :, lanes])
            total_s = total_s + dot_nt(pieces, fine_ref[il, 1, :, lanes])
        mask = mask_ref[il : il + 1, :]
        for j in range(steps):
            lanes = slice(lane_width * j, lane_width * (j + 1))
            at = j * panel_rows
            piece = total_c[at : at + fields] + total_s[at + fields : at + panel_rows]
            out_ref[il, :, lanes] = (piece * mask[:, lanes]).astype(bf16)


def call(body, name, arrays, spaces, out_shapes, scratch, flops=1):
    return pl.pallas_call(
        body,
        name=name,
        cost_estimate=pl.CostEstimate(flops=flops, transcendentals=0, bytes_accessed=1),
        in_specs=[pl.BlockSpec(memory_space=space) for space in spaces],
        out_specs=tuple(pl.BlockSpec(memory_space=pltpu.VMEM) for _ in out_shapes),
        out_shape=tuple(out_shapes),
        scratch_shapes=scratch,
        compiler_params=pltpu.CompilerParams(vmem_limit_bytes=vmem_bytes),
    )(*arrays)


def exchange(array, axes, count):
    return [array] + [
        lax.ppermute(array, axes, [(i, i ^ k) for i in range(count)]) for k in range(1, count)
    ]


def per_device(predicted_state, analysis_state, nodes_per_parallel, weighted_harmonic_table):
    share, fields, extent = predicted_state.shape
    pairs_held, cycle_band, slot_count = weighted_harmonic_table.shape
    groups = lax.axis_size("groups")
    bands = lax.axis_size("band")
    owners = lax.axis_size(owner_axes)
    group = lax.axis_index("groups")
    band = lax.axis_index("band")
    sources = bands * owners
    pairs_part = -(-pairs_held // (bands * groups))
    pairs_sub = groups * pairs_part
    panel_rows = 2 * fields
    pack = max(1, lane_width // (share * 4 * fields))
    wire_pack = 1
    wire_lanes = round_up(wire_pack * share * 4 * panel_rows, lane_width)
    back_lanes = round_up(pack * share * 4 * fields, lane_width)
    block_lanes = round_up(4 * panel_rows, lane_width)
    half_lanes = sources * pairs_sub
    coarse_rows = round_up(extent // lane_width, 8)

    table = weighted_harmonic_table
    if pairs_sub * bands != pairs_held:
        table = jnp.pad(table, ((0, pairs_sub * bands - pairs_held), (0, 0), (0, 0)))
    own_table = lax.dynamic_slice_in_dim(table, band * pairs_sub, pairs_sub, 0)

    def over_bands(array, k):
        return lax.ppermute(array, "band", [(i, i ^ k) for i in range(bands)])

    starts = [((band ^ k) * groups + (group ^ j)) * pairs_part for k in range(1, bands) for j in range(groups)]
    pieces = [
        lax.dynamic_slice_in_dim(table, start, pairs_part, 0)
        for n, start in enumerate(starts)
        if n < groups or n % groups == 0
    ]
    pieces = lax.optimization_barrier(pieces)
    near = [over_bands(piece, 1) for piece in pieces[:groups]]
    far = [over_bands(piece, n + 2) for n, piece in enumerate(pieces[groups:])]
    states = jnp.concatenate([predicted_state, analysis_state], axis=1)
    wire, coarse, fine, mask = call(
        functools.partial(
            analyse_kernel,
            pack,
            wire_pack,
            groups,
            bands,
            owners,
            pairs_held,
            pairs_part,
            slot_count - 1,
        ),
        "analyse",
        (nodes_per_parallel, states),
        (pltpu.SMEM, pltpu.VMEM),
        (
            jax.ShapeDtypeStruct((sources, pairs_sub // wire_pack, wire_lanes), bf16),
            jax.ShapeDtypeStruct((share, 2, coarse_rows, 2 * half_lanes), f32),
            jax.ShapeDtypeStruct((share, 2, lane_width, 2 * half_lanes), bf16),
            jax.ShapeDtypeStruct((share, extent), f32),
        ),
        [
            pltpu.VMEM((share * 4 * panel_rows, half_lanes), f32),
            pltpu.VMEM((wire_lanes, round_up(half_lanes // wire_pack, lane_width)), f32),
            pltpu.VMEM((round_up(half_lanes // wire_pack, lane_width), wire_lanes), f32),
        ],
    )
    wire = lax.all_to_all(wire, group_axes, 0, 0, tiled=True)
    parts = list(near)
    for piece in far:
        parts.append(piece)
        for j in range(1, groups):
            parts.append(lax.ppermute(piece, "groups", [(i, i ^ j) for i in range(groups)]))
    sizes = (pack, wire_pack, groups, bands, owners, pairs_held, share)
    other_pairs = pairs_sub - pairs_part
    left_shape = (bands * cycle_band, block_lanes)

    def pair_shapes(count):
        return (
            jax.ShapeDtypeStruct((count, 2, panel_rows, slot_count), f32),
            jax.ShapeDtypeStruct((count, bands * cycle_band, slot_count), bf16),
        )

    own_coef, own_rows, sums, left = call(
        functools.partial(project_kernel, *sizes, 0, 1),
        "project_own",
        (wire, own_table, *parts[0::groups]),
        (pltpu.VMEM,) * (1 + bands),
        (
            *pair_shapes(pairs_part),
            jax.ShapeDtypeStruct((2, panel_rows, slot_count), f32),
            jax.ShapeDtypeStruct((other_pairs, *left_shape), f32),
        ),
        [
            pltpu.VMEM((wire_lanes // lane_width, half_lanes // wire_pack, lane_width), f32),
            pltpu.VMEM((pairs_part, *left_shape), f32),
        ],
    )
    others = [p for n, p in enumerate(parts) if n % groups > 0]
    other_coef, other_rows, spectra = call(
        functools.partial(project_kernel, *sizes, 1, groups),
        "project",
        (left, own_table, *others, sums),
        (pltpu.VMEM,) * (3 + len(others)),
        (
            *pair_shapes(other_pairs),
            jax.ShapeDtypeStruct((panel_rows, slot_count + slot_count // 2), f32),
        ),
        [],
    )
    spectra = tree_sum(exchange(spectra, owner_axes, owners))
    spectra = exchange(spectra, "band", bands)
    wire, misfit = call(
        functools.partial(gradient_kernel, pack, groups, bands, owners, pairs_held, share, len(spectra)),
        "gradient",
        (*spectra, own_coef, other_coef, own_rows, other_rows),
        (pltpu.VMEM,) * (4 + len(spectra)),
        (
            jax.ShapeDtypeStruct((sources, pairs_sub // pack, back_lanes), bf16),
            jax.ShapeDtypeStruct((round_up(fields // bands, 8), lane_width), f32),
        ),
        [
            pltpu.VMEM((back_lanes // lane_width, half_lanes // pack, lane_width), f32),
            pltpu.VMEM((pairs_sub, *left_shape), f32),
        ],
    )
    wire = lax.all_to_all(wire, group_axes, 0, 0, tiled=True)
    (sensitivity,) = call(
        functools.partial(synthesise_kernel, pack),
        "synthesise",
        (coarse, fine, mask, wire),
        (pltpu.VMEM,) * 4,
        (jax.ShapeDtypeStruct((share, fields, extent), bf16),),
        [pltpu.VMEM((round_up(half_lanes // pack, lane_width), back_lanes), f32)],
    )
    return misfit[: fields // bands, 0], sensitivity


def solution(mesh):
    in_specs = (
        P(("groups", "band", "field", "wave"), None, None),
        P(("groups", "band", "field", "wave"), None, None),
        P(),
        P(("field", "wave"), "band", None),
    )
    out_specs = (P(("groups", "band")), P(("groups", "band", "field", "wave"), None, None))
    return jax.shard_map(
        per_device, mesh=mesh, in_specs=in_specs, out_specs=out_specs, check_vma=False
    )
```

```python
import functools
import math

import jax
import jax.numpy as jnp
from jax import lax
from jax.experimental import pallas as pl
from jax.experimental.pallas import tpu as pltpu
from jax.sharding import PartitionSpec as P

spectrum_floor = 0.25
gradient_gain = 16.0
lane_width = 128
vmem_bytes = 40 * 1024 * 1024
owner_axes = ("field", "wave")
group_axes = ("band", "field", "wave")
bf16 = jnp.bfloat16
f32 = jnp.float32


def round_up(value, step):
    return -(-value // step) * step


def dot_nn(left, right):
    return lax.dot_general(left, right, (((1,), (0,)), ((), ())), preferred_element_type=f32)


def dot_nt(left, right):
    return lax.dot_general(left, right, (((1,), (1,)), ((), ())), preferred_element_type=f32)


def dot_tn(left, right):
    return lax.dot_general(left, right, (((0,), (0,)), ((), ())), preferred_element_type=f32)


def split_index(index, size):
    whole = jnp.floor((index + 0.5) * (1.0 / size))
    return whole, index - whole * size


def wavenumbers(owner, band, half, rest, pairs_held, pairs_part, groups, degree_count):
    part, pair = split_index(rest, pairs_part)
    part = (lax.axis_index("groups") ^ part.astype(jnp.int32)).astype(f32)
    within = (band * groups + part) * pairs_part + pair
    pair = owner * pairs_held + within
    mirrored = degree_count - 1.0 - pair
    wavenum = jnp.where(half > 0.0, mirrored, pair)
    void = (within >= pairs_held) | ((half > 0.0) & (mirrored == pair))
    return jnp.where(void, 4.0 * degree_count, wavenum)


def own_wavenumbers(lanes, pack, bands, owners, pairs_held, pairs_part, groups, degree_count):
    index = lax.broadcasted_iota(jnp.int32, (1, lanes), 1).astype(f32)
    half, index = split_index(index, lanes // 2)
    rows = groups * pairs_part // pack
    low_place, index = split_index(index, bands * owners * rows)
    block, high_place = split_index(index, rows)
    band, owner = split_index(block, owners)
    rest = high_place * pack + low_place
    return wavenumbers(owner, band, half, rest, pairs_held, pairs_part, groups, degree_count)


def move_lanes(values, moves, lanes):
    total = values.shape[1]
    moved = jnp.zeros(values.shape, f32)
    lane = lax.broadcasted_iota(jnp.int32, values.shape, 1)
    for start, width, place in moves:
        shift = (place - start) % total
        turned = pltpu.roll(values, shift, 1) if shift else values
        moved = jnp.where((lane >= place) & (lane < place + width), turned, moved)
    return moved[:, :lanes]


def cos_and_minus_sin(wavenum, points, columns, inverse):
    quarters = (4.0 * wavenum) * columns
    turns = jnp.floor(quarters * inverse + 0.5)
    angle = (quarters - turns * points) * (0.5 * math.pi * inverse)
    square = angle * angle
    sine = angle * (1.0 + square * (-1.0 / 6 + square * (1.0 / 120 + square * (-1.0 / 5040))))
    cosine = 1.0 + square * (
        -0.5 + square * (1.0 / 24 + square * (-1.0 / 720 + square * (1.0 / 40320)))
    )
    quadrant = turns.astype(jnp.int32)
    swap = (quadrant & 1) != 0
    new_cos = jnp.where(swap, sine, cosine)
    new_sin = jnp.where(swap, cosine, sine)
    new_cos = jnp.where(((quadrant + 1) & 2) != 0, -new_cos, new_cos)
    new_sin = jnp.where((quadrant & 2) != 0, new_sin, -new_sin)
    return new_cos, new_sin


def fill_tables(points_i, wavenum, coarse_ref, fine_ref, at):
    lanes = wavenum.shape[1]
    points = jnp.full((1, lanes), points_i, jnp.int32).astype(f32)
    inverse = 1.0 / points
    scale = jnp.where(2.0 * wavenum < points, 1.0 / jnp.sqrt(points), 0.0)

    def rows_of(count, step):
        return (lax.broadcasted_iota(jnp.int32, (count, lanes), 0) * step).astype(f32)

    coarse_rows = coarse_ref.shape[2]
    coarse_c, coarse_s = cos_and_minus_sin(wavenum, points, rows_of(coarse_rows, lane_width), inverse)
    coarse_ref[at, 0] = coarse_c * scale
    coarse_ref[at, 1] = coarse_s * scale
    mid_c, mid_s = cos_and_minus_sin(wavenum, points, rows_of(lane_width // 8, 8), inverse)
    unit_c, unit_s = cos_and_minus_sin(wavenum, points, rows_of(8, 1), inverse)
    for g in range(lane_width // 16):
        pieces_c = []
        pieces_s = []
        for a in (2 * g, 2 * g + 1):
            step_c = mid_c[a : a + 1]
            step_s = mid_s[a : a + 1]
            pieces_c.append(step_c * unit_c - step_s * unit_s)
            pieces_s.append(step_c * unit_s + step_s * unit_c)
        fine_ref[at, 0, 16 * g : 16 * g + 16] = jnp.concatenate(pieces_c, 0).astype(bf16)
        fine_ref[at, 1, 16 * g : 16 * g + 16] = jnp.concatenate(pieces_s, 0).astype(bf16)


def analyse_kernel(
    pack,
    wire_pack,
    groups,
    bands,
    owners,
    pairs_held,
    pairs_part,
    degree_count,
    nodes_ref,
    states_ref,
    wire_ref,
    coarse_ref,
    fine_ref,
    mask_ref,
    rows_scr,
    wide_scr,
    flat_scr,
):
    share, panel_rows, extent = states_ref.shape
    steps = extent // lane_width
    half_lanes = coarse_ref.shape[3] // 2
    first_cycle = lax.axis_index(group_axes) * share
    column = lax.broadcasted_iota(jnp.int32, (1, extent), 1)
    wavenum = own_wavenumbers(
        2 * half_lanes, pack, bands, owners, pairs_held, pairs_part, groups, degree_count
    )
    for il in range(share):
        points_i = nodes_ref[first_cycle + il]
        fill_tables(points_i, wavenum, coarse_ref, fine_ref, il)
        held = column < points_i
        mask_ref[il : il + 1, :] = held.astype(f32)
        panel = jnp.where(held, states_ref[il].astype(f32), 0.0)
        stacked = jnp.concatenate(
            [panel[:, lane_width * j : lane_width * (j + 1)] for j in range(steps)], axis=0
        ).astype(bf16)
        for h in range(2):
            lanes = slice(h * half_lanes, (h + 1) * half_lanes)
            part_c = dot_nn(stacked, fine_ref[il, 0, :, lanes])
            part_s = dot_nn(stacked, fine_ref[il, 1, :, lanes])
            total_c = jnp.zeros((panel_rows, half_lanes), f32)
            total_s = jnp.zeros((panel_rows, half_lanes), f32)
            for j in range(steps):
                turn_c = coarse_ref[il, 0, j : j + 1, lanes]
                turn_s = coarse_ref[il, 1, j : j + 1, lanes]
                piece_c = part_c[j * panel_rows : (j + 1) * panel_rows]
                piece_s = part_s[j * panel_rows : (j + 1) * panel_rows]
                total_c = total_c + (turn_c * piece_c - turn_s * piece_s)
                total_s = total_s + (turn_c * piece_s + turn_s * piece_c)
            at = (il * 2 + h) * 2 * panel_rows
            rows_scr[at : at + panel_rows, :] = total_c
            rows_scr[at + panel_rows : at + 2 * panel_rows, :] = total_s
    sources = bands * owners
    rows = groups * pairs_part // pack
    width = sources * rows
    count = rows_scr.shape[0]
    parts = pack // wire_pack
    values = rows_scr[...]
    if wide_scr.shape[0] > wire_pack * count:
        wide_scr[wire_pack * count :, :] = jnp.zeros_like(wide_scr[wire_pack * count :, :])
    for d in range(wire_pack):
        moves = [((e * wire_pack + d) * width, width, e * width) for e in range(parts)]
        wide_scr[d * count : (d + 1) * count, :] = move_lanes(values, moves, wide_scr.shape[1])
    flat_scr[...] = jnp.transpose(wide_scr[...])
    for source in range(sources):
        starts = [(e * sources + source) * rows for e in range(parts)]
        wire_ref[source] = jnp.concatenate(
            [flat_scr[at : at + rows, :] for at in starts], axis=0
        ).astype(bf16)


def take_block(rows, index, width, lanes):
    if width % lane_width == 0:
        return rows[:, index * width : (index + 1) * width]
    total = rows.shape[1]
    if index > 0:
        rows = pltpu.roll(rows, total - index * width, 1)
    return rows[:, :lanes]


def join_blocks(blocks, width, total):
    if width % lane_width == 0:
        return jnp.concatenate(blocks, axis=1)
    joined = jnp.zeros((blocks[0].shape[0], total), f32)
    lane = lax.broadcasted_iota(jnp.int32, joined.shape, 1)
    for index, block in enumerate(blocks):
        wide = jnp.concatenate([block] * (total // block.shape[1]), axis=1)
        if index > 0:
            wide = pltpu.roll(wide, index * width, 1)
        here = (lane >= index * width) & (lane < (index + 1) * width)
        joined = jnp.where(here, wide, joined)
    return joined


def roll_lanes(values, shift):
    shift = shift % values.shape[1]
    return pltpu.roll(values, shift, 1) if shift else values


def pair_sides(pair, slot, degree_count):
    low_side = slot < degree_count - pair
    low_weight = jnp.where(pair == 0, 1.0, 2.0)
    high_weight = jnp.where(2 * pair == degree_count - 1, 0.0, 2.0)
    return low_side, low_weight, high_weight


def project_kernel(
    pack,
    wire_pack,
    groups,
    bands,
    owners,
    pairs_held,
    share,
    first_part,
    last_part,
    source_ref,
    own_ref,
    *refs,
):
    is_first = first_part == 0
    remote = (last_part - first_part) * (bands - 1)
    part_refs = refs[:remote]
    if is_first:
        coef_ref, table_ref, sums_ref, left_ref, flat_scr, left_scr = refs[remote:]
    else:
        earlier_ref, coef_ref, table_ref, spectra_ref = refs[remote:]
    pairs_sub, cycle_band, slot_count = own_ref.shape
    high_places = pairs_sub // pack
    degree_count = slot_count - 1
    panel_rows = coef_ref.shape[2]
    fields = panel_rows // 2
    block_rows = 4 * panel_rows
    pairs_part = pairs_sub // groups
    group = lax.axis_index("groups")
    band = lax.axis_index("band")
    first = lax.axis_index(owner_axes) * pairs_held + band * pairs_sub
    slot = lax.broadcasted_iota(jnp.int32, (panel_rows, slot_count), 1)
    row = lax.broadcasted_iota(jnp.int32, (panel_rows, slot_count // 2), 0)
    upper = lax.broadcasted_iota(jnp.int32, (panel_rows, slot_count), 0) < fields
    zero = jnp.zeros((panel_rows, slot_count), f32)
    high_power, high_cross = zero, zero
    all_power, all_cross = zero, zero
    if is_first:
        sources, wire_rows, _ = source_ref.shape
        for k in range(bands):
            other = band ^ k
            for w in range(owners):
                at = (k * owners + w) * wire_rows
                rows = source_ref[other * owners + w].astype(f32)
                for c in range(flat_scr.shape[0]):
                    flat_scr[c, at : at + wire_rows, :] = rows[:, c * lane_width : (c + 1) * lane_width]
        for place in range(pairs_sub):
            high_place, low_place = divmod(place, pack)
            wire_row = low_place // wire_pack * high_places + high_place
            received = jnp.concatenate(
                [
                    flat_scr[c, pl.ds(wire_row, sources, stride=wire_rows), :]
                    for c in range(flat_scr.shape[0])
                ],
                axis=1,
            )
            target, at = (left_scr, place) if place < pairs_part else (left_ref, place - pairs_part)
            for il in range(share):
                target[at, pl.ds(il, sources, stride=share), :] = take_block(
                    received, low_place % wire_pack * share + il, block_rows, left_scr.shape[2]
                )
        left_ref = left_scr
    else:
        left_ref = source_ref
        all_power, all_cross = earlier_ref[0], earlier_ref[1]
    for j in range(first_part, last_part):
        part_row = (group ^ j) * pairs_part
        low_power, low_cross = zero, zero
        for q in range(pairs_part):
            at = (j - first_part) * pairs_part + q
            left = left_ref[at, :, 0:block_rows].astype(bf16)
            blocks = [own_ref[part_row + q]] + [t[q] for t in part_refs[j - first_part :: last_part - first_part]]
            table = jnp.concatenate([b.astype(f32) for b in blocks], axis=0).astype(bf16)
            table_ref[at] = table
            both_halves = dot_tn(left, table)
            pair = first + part_row + q
            low_side, low_weight, high_weight = pair_sides(pair, slot, degree_count)
            cosines = jnp.where(
                low_side, both_halves[0:panel_rows], both_halves[2 * panel_rows : 3 * panel_rows]
            )
            sines = jnp.where(
                low_side, both_halves[panel_rows : 2 * panel_rows], both_halves[3 * panel_rows :]
            )
            coef_ref[at, 0] = cosines
            coef_ref[at, 1] = sines
            weight = jnp.where(low_side, low_weight, high_weight)
            power = (cosines * cosines + sines * sines) * weight
            straight = jnp.where(upper, cosines, sines)
            swapped = pltpu.roll(jnp.where(upper, sines, cosines), fields, 0)
            cross = straight * swapped * weight
            low_power = low_power + roll_lanes(jnp.where(low_side, power, 0.0), q)
            low_cross = low_cross + roll_lanes(jnp.where(low_side, cross, 0.0), q)
            high_power = high_power + jnp.where(low_side, 0.0, power)
            high_cross = high_cross + jnp.where(low_side, 0.0, cross)
        all_power = all_power + pltpu.roll(low_power, first + part_row, 1)
        all_cross = all_cross + pltpu.roll(low_cross, first + part_row, 1)
    all_power = all_power + pltpu.roll(high_power, slot_count - 1, 1)
    all_cross = all_cross + pltpu.roll(high_cross, slot_count - 1, 1)
    if is_first:
        sums_ref[0] = all_power
        sums_ref[1] = all_cross
    else:
        all_cross = all_cross + pltpu.roll(all_cross, fields, 0)
        spectra_ref[:, 0:slot_count] = all_power
        spectra_ref[:, slot_count:] = jnp.where(
            row < fields, all_cross[:, : slot_count // 2], all_cross[:, slot_count // 2 :]
        )


def tree_sum(parts):
    while len(parts) > 1:
        parts = [parts[i] + parts[i + 1] for i in range(0, len(parts), 2)]
    return parts[0]


def gradient_kernel(pack, groups, bands, owners, pairs_held, share, spectra_parts, *refs):
    spectra_refs = refs[:spectra_parts]
    coef_refs = refs[spectra_parts : spectra_parts + 2]
    table_refs = refs[spectra_parts + 2 : spectra_parts + 4]
    wire_ref, misfit_ref, flat_scr, cycle_scr = refs[spectra_parts + 4 :]
    sources, wire_rows, wire_lanes = wire_ref.shape
    pairs_part = coef_refs[0].shape[0]
    pairs_sub = groups * pairs_part
    slot_count = table_refs[0].shape[2]
    degree_count = slot_count - 1
    panel_rows = coef_refs[0].shape[2]
    fields = panel_rows // 2
    block_rows = 4 * fields
    fields_out = fields // bands
    group = lax.axis_index("groups")
    band = lax.axis_index("band")
    first = lax.axis_index(owner_axes) * pairs_held + band * pairs_sub
    slot = lax.broadcasted_iota(jnp.int32, (panel_rows, slot_count), 1)
    row = lax.broadcasted_iota(jnp.int32, (panel_rows, slot_count), 0)
    spectra = tree_sum([s[...] for s in spectra_refs])
    power = spectra[:, :slot_count]
    packed = spectra[:, slot_count:]
    turned = pltpu.roll(packed, fields, 0)
    upper = row[:, : slot_count // 2] < fields
    cross = jnp.concatenate([jnp.where(upper, packed, turned), jnp.where(upper, turned, packed)], axis=1)
    odd_weight = (2 * slot + 1).astype(f32)
    power = power / odd_weight + spectrum_floor
    cross = cross / odd_weight
    root = jnp.sqrt(power)
    other_root = pltpu.roll(root, fields, 0)
    both_power = power + pltpu.roll(power, fields, 0)
    geo_mean = root * other_root
    coherence = cross / geo_mean
    term = (root - other_root) * (root - other_root) + both_power * (1.0 - coherence)
    term = jnp.where(slot < degree_count, term, 0.0)
    mean = jnp.sum(term, axis=1, keepdims=True) / degree_count
    field_row = lax.broadcasted_iota(jnp.int32, (panel_rows, 1), 0)
    misfit_ref[...] = jnp.zeros_like(misfit_ref)
    for i in range(fields_out):
        chosen = jnp.where(field_row == band * fields_out + i, mean, 0.0)
        misfit_ref[i : i + 1, :] = jnp.broadcast_to(
            jnp.sum(chosen, axis=0, keepdims=True), (1, lane_width)
        )
    grad_power = (
        gradient_gain
        * (
            1.0
            - other_root / root
            + (1.0 - coherence)
            + both_power * coherence / (2.0 * power)
        )
        / odd_weight
    )
    grad_cross = -gradient_gain * both_power / geo_mean / odd_weight
    by_degree = jnp.where(row < fields, 2.0 * grad_power, grad_cross)
    high_grad = pltpu.roll(by_degree, 1, 1)
    blocks = []
    for j in range(groups):
        part_row = (group ^ j) * pairs_part
        low_grad = pltpu.roll(by_degree, slot_count - first - part_row, 1)
        for q in range(pairs_part):
            place = j * pairs_part + q
            at_part = (0, q) if j == 0 else (1, place - pairs_part)
            pair = first + part_row + q
            low_side, low_weight, high_weight = pair_sides(pair, slot, degree_count)
            shifted = roll_lanes(low_grad, slot_count - q)
            gain = jnp.where(low_side, shifted * low_weight, high_grad * high_weight)
            cosines = coef_refs[at_part[0]][at_part[1], 0] * gain
            sines = coef_refs[at_part[0]][at_part[1], 1] * gain
            swapped = pltpu.roll(jnp.where(row < fields, sines, cosines), fields, 0)
            grads = jnp.where(row < fields, cosines, sines) + swapped
            masked = jnp.concatenate(
                [jnp.where(low_side, grads, 0.0), jnp.where(low_side, 0.0, grads)], axis=0
            ).astype(bf16)
            cycle_scr[place, :, 0:block_rows] = dot_nt(
                table_refs[at_part[0]][at_part[1]], masked
            )
            high_place, low_place = divmod(place, pack)
            blocks = [] if low_place == 0 else blocks
            blocks += [cycle_scr[place, pl.ds(il, sources, stride=share), :] for il in range(share)]
            if low_place == pack - 1:
                joined = join_blocks(blocks, block_rows, wire_lanes)
                for c in range(flat_scr.shape[0]):
                    flat_scr[c, pl.ds(high_place, sources, stride=wire_rows), :] = joined[
                        :, c * lane_width : (c + 1) * lane_width
                    ]
    for k in range(bands):
        other = band ^ k
        for w in range(owners):
            at = (k * owners + w) * wire_rows
            wire_ref[other * owners + w] = jnp.concatenate(
                [flat_scr[c, at : at + wire_rows, :] for c in range(flat_scr.shape[0])], axis=1
            ).astype(bf16)


def synthesise_kernel(pack, coarse_ref, fine_ref, mask_ref, wire_ref, out_ref, flat_scr):
    share, fields, extent = out_ref.shape
    sources, wire_rows, wire_lanes = wire_ref.shape
    steps = extent // lane_width
    half_lanes = coarse_ref.shape[3] // 2
    panel_rows = 2 * fields
    width = sources * wire_rows
    for source in range(sources):
        flat_scr[source * wire_rows : (source + 1) * wire_rows, :] = wire_ref[source].astype(f32)
    if flat_scr.shape[0] > width:
        flat_scr[width:, :] = jnp.zeros_like(flat_scr[width:, :])
    turned = jnp.transpose(flat_scr[...])
    count = wire_lanes // pack
    if pack > 1:
        spare = jnp.zeros((count, round_up(half_lanes, lane_width) - turned.shape[1]), f32)
        values = jnp.zeros((count, half_lanes), f32)
        for low_place in range(pack):
            block = jnp.concatenate([turned[low_place * count : (low_place + 1) * count], spare], axis=1)
            values = values + move_lanes(block, [(0, width, low_place * width)], half_lanes)
    else:
        values = turned[:, :half_lanes]
    row = lax.broadcasted_iota(jnp.int32, (panel_rows, 2 * half_lanes), 0)
    for il in range(share):
        at = il * 2 * panel_rows
        direct = jnp.concatenate(
            [values[at : at + panel_rows], values[at + panel_rows : at + 2 * panel_rows]], axis=1
        )
        crossed = pltpu.roll(direct, fields, 0)
        crossed = jnp.where(row < fields, crossed, -crossed)
        pieces = [
            direct * coarse_ref[il, 0, j : j + 1, :] + crossed * coarse_ref[il, 1, j : j + 1, :]
            for j in range(steps)
        ]
        pieces = jnp.concatenate(pieces, 0).astype(bf16)
        fine = jnp.concatenate([fine_ref[il, 0], fine_ref[il, 1]], axis=0)
        total = dot_nt(pieces, fine)
        total_c, total_s = total[:, :lane_width], total[:, lane_width:]
        mask = mask_ref[il : il + 1, :]
        for j in range(steps):
            lanes = slice(lane_width * j, lane_width * (j + 1))
            at = j * panel_rows
            piece = total_c[at : at + fields] + total_s[at + fields : at + panel_rows]
            out_ref[il, :, lanes] = (piece * mask[:, lanes]).astype(bf16)


def call(body, name, arrays, spaces, out_shapes, scratch, flops=1):
    return pl.pallas_call(
        body,
        name=name,
        cost_estimate=pl.CostEstimate(flops=flops, transcendentals=0, bytes_accessed=1),
        in_specs=[pl.BlockSpec(memory_space=space) for space in spaces],
        out_specs=tuple(pl.BlockSpec(memory_space=pltpu.VMEM) for _ in out_shapes),
        out_shape=tuple(out_shapes),
        scratch_shapes=scratch,
        compiler_params=pltpu.CompilerParams(vmem_limit_bytes=vmem_bytes),
    )(*arrays)


def exchange(array, axes, count):
    return [array] + [
        lax.ppermute(array, axes, [(i, i ^ k) for i in range(count)]) for k in range(1, count)
    ]


def per_device(predicted_state, analysis_state, nodes_per_parallel, weighted_harmonic_table):
    share, fields, extent = predicted_state.shape
    pairs_held, cycle_band, slot_count = weighted_harmonic_table.shape
    groups = lax.axis_size("groups")
    bands = lax.axis_size("band")
    owners = lax.axis_size(owner_axes)
    group = lax.axis_index("groups")
    band = lax.axis_index("band")
    sources = bands * owners
    pairs_part = -(-pairs_held // (bands * groups))
    pairs_sub = groups * pairs_part
    panel_rows = 2 * fields
    pack = max(1, lane_width // (share * 4 * fields))
    wire_pack = 1
    wire_lanes = round_up(wire_pack * share * 4 * panel_rows, lane_width)
    back_lanes = round_up(pack * share * 4 * fields, lane_width)
    block_lanes = round_up(4 * panel_rows, lane_width)
    half_lanes = sources * pairs_sub
    coarse_rows = round_up(extent // lane_width, 8)

    table = weighted_harmonic_table
    if pairs_sub * bands != pairs_held:
        table = jnp.pad(table, ((0, pairs_sub * bands - pairs_held), (0, 0), (0, 0)))
    own_table = lax.dynamic_slice_in_dim(table, band * pairs_sub, pairs_sub, 0)

    def over_bands(array, k):
        return lax.ppermute(array, "band", [(i, i ^ k) for i in range(bands)])

    starts = [((band ^ k) * groups + (group ^ j)) * pairs_part for k in range(1, bands) for j in range(groups)]
    pieces = [
        lax.dynamic_slice_in_dim(table, start, pairs_part, 0)
        for n, start in enumerate(starts)
        if n < groups or n % groups == 0
    ]
    pieces = lax.optimization_barrier(pieces)
    near = [over_bands(piece, 1) for piece in pieces[:groups]]
    far = [over_bands(piece, n + 2) for n, piece in enumerate(pieces[groups:])]
    states = jnp.concatenate([predicted_state, analysis_state], axis=1)
    wire, coarse, fine, mask = call(
        functools.partial(
            analyse_kernel,
            pack,
            wire_pack,
            groups,
            bands,
            owners,
            pairs_held,
            pairs_part,
            slot_count - 1,
        ),
        "analyse",
        (nodes_per_parallel, states),
        (pltpu.SMEM, pltpu.VMEM),
        (
            jax.ShapeDtypeStruct((sources, pairs_sub // wire_pack, wire_lanes), bf16),
            jax.ShapeDtypeStruct((share, 2, coarse_rows, 2 * half_lanes), f32),
            jax.ShapeDtypeStruct((share, 2, lane_width, 2 * half_lanes), bf16),
            jax.ShapeDtypeStruct((share, extent), f32),
        ),
        [
            pltpu.VMEM((share * 4 * panel_rows, half_lanes), f32),
            pltpu.VMEM((wire_lanes, round_up(half_lanes // wire_pack, lane_width)), f32),
            pltpu.VMEM((round_up(half_lanes // wire_pack, lane_width), wire_lanes), f32),
        ],
    )
    wire = lax.all_to_all(wire, group_axes, 0, 0, tiled=True)
    parts = list(near)
    for piece in far:
        parts.append(piece)
        for j in range(1, groups):
            parts.append(lax.ppermute(piece, "groups", [(i, i ^ j) for i in range(groups)]))
    sizes = (pack, wire_pack, groups, bands, owners, pairs_held, share)
    other_pairs = pairs_sub - pairs_part
    left_shape = (bands * cycle_band, block_lanes)

    def pair_shapes(count):
        return (
            jax.ShapeDtypeStruct((count, 2, panel_rows, slot_count), f32),
            jax.ShapeDtypeStruct((count, bands * cycle_band, slot_count), bf16),
        )

    own_coef, own_rows, sums, left = call(
        functools.partial(project_kernel, *sizes, 0, 1),
        "project_own",
        (wire, own_table, *parts[0::groups]),
        (pltpu.VMEM,) * (1 + bands),
        (
            *pair_shapes(pairs_part),
            jax.ShapeDtypeStruct((2, panel_rows, slot_count), f32),
            jax.ShapeDtypeStruct((other_pairs, *left_shape), f32),
        ),
        [
            pltpu.VMEM((wire_lanes // lane_width, half_lanes // wire_pack, lane_width), f32),
            pltpu.VMEM((pairs_part, *left_shape), f32),
        ],
    )
    others = [p for n, p in enumerate(parts) if n % groups > 0]
    other_coef, other_rows, spectra = call(
        functools.partial(project_kernel, *sizes, 1, groups),
        "project",
        (left, own_table, *others, sums),
        (pltpu.VMEM,) * (3 + len(others)),
        (
            *pair_shapes(other_pairs),
            jax.ShapeDtypeStruct((panel_rows, slot_count + slot_count // 2), f32),
        ),
        [],
    )
    spectra = tree_sum(exchange(spectra, owner_axes, owners))
    spectra = exchange(spectra, "band", bands)
    wire, misfit = call(
        functools.partial(gradient_kernel, pack, groups, bands, owners, pairs_held, share, len(spectra)),
        "gradient",
        (*spectra, own_coef, other_coef, own_rows, other_rows),
        (pltpu.VMEM,) * (4 + len(spectra)),
        (
            jax.ShapeDtypeStruct((sources, pairs_sub // pack, back_lanes), bf16),
            jax.ShapeDtypeStruct((round_up(fields // bands, 8), lane_width), f32),
        ),
        [
            pltpu.VMEM((back_lanes // lane_width, half_lanes // pack, lane_width), f32),
            pltpu.VMEM((pairs_sub, *left_shape), f32),
        ],
    )
    wire = lax.all_to_all(wire, group_axes, 0, 0, tiled=True)
    (sensitivity,) = call(
        functools.partial(synthesise_kernel, pack),
        "synthesise",
        (coarse, fine, mask, wire),
        (pltpu.VMEM,) * 4,
        (jax.ShapeDtypeStruct((share, fields, extent), bf16),),
        [pltpu.VMEM((round_up(half_lanes // pack, lane_width), back_lanes), f32)],
    )
    return misfit[: fields // bands, 0], sensitivity


def solution(mesh):
    in_specs = (
        P(("groups", "band", "field", "wave"), None, None),
        P(("groups", "band", "field", "wave"), None, None),
        P(),
        P(("field", "wave"), "band", None),
    )
    out_specs = (P(("groups", "band")), P(("groups", "band", "field", "wave"), None, None))
    return jax.shard_map(
        per_device, mesh=mesh, in_specs=in_specs, out_specs=out_specs, check_vma=False
    )
```

```python
import functools
import math

import jax
import jax.numpy as jnp
from jax import lax
from jax.experimental import pallas as pl
from jax.experimental.pallas import tpu as pltpu
from jax.sharding import PartitionSpec as P

spectrum_floor = 0.25
gradient_gain = 16.0
lane_width = 128
vmem_bytes = 40 * 1024 * 1024
owner_axes = ("field", "wave")
group_axes = ("band", "field", "wave")
bf16 = jnp.bfloat16
f32 = jnp.float32


def round_up(value, step):
    return -(-value // step) * step


def dot_nn(left, right):
    return lax.dot_general(left, right, (((1,), (0,)), ((), ())), preferred_element_type=f32)


def dot_nt(left, right):
    return lax.dot_general(left, right, (((1,), (1,)), ((), ())), preferred_element_type=f32)


def dot_tn(left, right):
    return lax.dot_general(left, right, (((0,), (0,)), ((), ())), preferred_element_type=f32)


def split_index(index, size):
    whole = jnp.floor((index + 0.5) * (1.0 / size))
    return whole, index - whole * size


def wavenumbers(owner, band, half, rest, pairs_held, pairs_part, groups, degree_count):
    part, pair = split_index(rest, pairs_part)
    part = (lax.axis_index("groups") ^ part.astype(jnp.int32)).astype(f32)
    within = (band * groups + part) * pairs_part + pair
    pair = owner * pairs_held + within
    mirrored = degree_count - 1.0 - pair
    wavenum = jnp.where(half > 0.0, mirrored, pair)
    void = (within >= pairs_held) | ((half > 0.0) & (mirrored == pair))
    return jnp.where(void, 4.0 * degree_count, wavenum)


def own_wavenumbers(lanes, pack, bands, owners, pairs_held, pairs_part, groups, degree_count):
    index = lax.broadcasted_iota(jnp.int32, (1, lanes), 1).astype(f32)
    half, index = split_index(index, lanes // 2)
    rows = groups * pairs_part // pack
    low_place, index = split_index(index, bands * owners * rows)
    block, high_place = split_index(index, rows)
    band, owner = split_index(block, owners)
    rest = high_place * pack + low_place
    return wavenumbers(owner, band, half, rest, pairs_held, pairs_part, groups, degree_count)


def move_lanes(values, moves, lanes):
    total = values.shape[1]
    moved = jnp.zeros(values.shape, f32)
    lane = lax.broadcasted_iota(jnp.int32, values.shape, 1)
    for start, width, place in moves:
        shift = (place - start) % total
        turned = pltpu.roll(values, shift, 1) if shift else values
        moved = jnp.where((lane >= place) & (lane < place + width), turned, moved)
    return moved[:, :lanes]


def cos_and_minus_sin(wavenum, points, columns, inverse):
    quarters = (4.0 * wavenum) * columns
    turns = jnp.floor(quarters * inverse + 0.5)
    angle = (quarters - turns * points) * (0.5 * math.pi * inverse)
    square = angle * angle
    sine = angle * (1.0 + square * (-1.0 / 6 + square * (1.0 / 120 + square * (-1.0 / 5040))))
    cosine = 1.0 + square * (
        -0.5 + square * (1.0 / 24 + square * (-1.0 / 720 + square * (1.0 / 40320)))
    )
    quadrant = turns.astype(jnp.int32)
    swap = (quadrant & 1) != 0
    new_cos = jnp.where(swap, sine, cosine)
    new_sin = jnp.where(swap, cosine, sine)
    new_cos = jnp.where(((quadrant + 1) & 2) != 0, -new_cos, new_cos)
    new_sin = jnp.where((quadrant & 2) != 0, new_sin, -new_sin)
    return new_cos, new_sin


def fill_tables(points_i, wavenum, coarse_ref, fine_ref, at):
    lanes = wavenum.shape[1]
    points = jnp.full((1, lanes), points_i, jnp.int32).astype(f32)
    inverse = 1.0 / points
    scale = jnp.where(2.0 * wavenum < points, 1.0 / jnp.sqrt(points), 0.0)

    def rows_of(count, step):
        return (lax.broadcasted_iota(jnp.int32, (count, lanes), 0) * step).astype(f32)

    coarse_rows = coarse_ref.shape[2]
    coarse_c, coarse_s = cos_and_minus_sin(wavenum, points, rows_of(coarse_rows, lane_width), inverse)
    coarse_ref[at, 0] = coarse_c * scale
    coarse_ref[at, 1] = coarse_s * scale
    mid_c, mid_s = cos_and_minus_sin(wavenum, points, rows_of(lane_width // 8, 8), inverse)
    unit_c, unit_s = cos_and_minus_sin(wavenum, points, rows_of(8, 1), inverse)
    for g in range(lane_width // 16):
        pieces_c = []
        pieces_s = []
        for a in (2 * g, 2 * g + 1):
            step_c = mid_c[a : a + 1]
            step_s = mid_s[a : a + 1]
            pieces_c.append(step_c * unit_c - step_s * unit_s)
            pieces_s.append(step_c * unit_s + step_s * unit_c)
        fine_ref[at, 0, 16 * g : 16 * g + 16] = jnp.concatenate(pieces_c, 0).astype(bf16)
        fine_ref[at, 1, 16 * g : 16 * g + 16] = jnp.concatenate(pieces_s, 0).astype(bf16)


def analyse_kernel(
    pack,
    wire_pack,
    groups,
    bands,
    owners,
    pairs_held,
    pairs_part,
    degree_count,
    nodes_ref,
    states_ref,
    wire_ref,
    coarse_ref,
    fine_ref,
    mask_ref,
    rows_scr,
    wide_scr,
    flat_scr,
):
    share, panel_rows, extent = states_ref.shape
    steps = extent // lane_width
    half_lanes = coarse_ref.shape[3] // 2
    first_cycle = lax.axis_index(group_axes) * share
    column = lax.broadcasted_iota(jnp.int32, (1, extent), 1)
    wavenum = own_wavenumbers(
        2 * half_lanes, pack, bands, owners, pairs_held, pairs_part, groups, degree_count
    )
    for il in range(share):
        points_i = nodes_ref[first_cycle + il]
        fill_tables(points_i, wavenum, coarse_ref, fine_ref, il)
        held = column < points_i
        mask_ref[il : il + 1, :] = held.astype(f32)
        panel = jnp.where(held, states_ref[il].astype(f32), 0.0)
        stacked = jnp.concatenate(
            [panel[:, lane_width * j : lane_width * (j + 1)] for j in range(steps)], axis=0
        ).astype(bf16)
        for h in range(2):
            lanes = slice(h * half_lanes, (h + 1) * half_lanes)
            part_c = dot_nn(stacked, fine_ref[il, 0, :, lanes])
            part_s = dot_nn(stacked, fine_ref[il, 1, :, lanes])
            total_c = jnp.zeros((panel_rows, half_lanes), f32)
            total_s = jnp.zeros((panel_rows, half_lanes), f32)
            for j in range(steps):
                turn_c = coarse_ref[il, 0, j : j + 1, lanes]
                turn_s = coarse_ref[il, 1, j : j + 1, lanes]
                piece_c = part_c[j * panel_rows : (j + 1) * panel_rows]
                piece_s = part_s[j * panel_rows : (j + 1) * panel_rows]
                total_c = total_c + (turn_c * piece_c - turn_s * piece_s)
                total_s = total_s + (turn_c * piece_s + turn_s * piece_c)
            at = (il * 2 + h) * 2 * panel_rows
            rows_scr[at : at + panel_rows, :] = total_c
            rows_scr[at + panel_rows : at + 2 * panel_rows, :] = total_s
    sources = bands * owners
    rows = groups * pairs_part // pack
    width = sources * rows
    count = rows_scr.shape[0]
    parts = pack // wire_pack
    values = rows_scr[...]
    if wide_scr.shape[0] > wire_pack * count:
        wide_scr[wire_pack * count :, :] = jnp.zeros_like(wide_scr[wire_pack * count :, :])
    for d in range(wire_pack):
        moves = [((e * wire_pack + d) * width, width, e * width) for e in range(parts)]
        wide_scr[d * count : (d + 1) * count, :] = move_lanes(values, moves, wide_scr.shape[1])
    flat_scr[...] = jnp.transpose(wide_scr[...])
    for source in range(sources):
        starts = [(e * sources + source) * rows for e in range(parts)]
        wire_ref[source] = jnp.concatenate(
            [flat_scr[at : at + rows, :] for at in starts], axis=0
        ).astype(bf16)


def take_block(rows, index, width, lanes):
    if width % lane_width == 0:
        return rows[:, index * width : (index + 1) * width]
    total = rows.shape[1]
    if index > 0:
        rows = pltpu.roll(rows, total - index * width, 1)
    return rows[:, :lanes]


def join_blocks(blocks, width, total):
    if width % lane_width == 0:
        return jnp.concatenate(blocks, axis=1)
    joined = jnp.zeros((blocks[0].shape[0], total), f32)
    lane = lax.broadcasted_iota(jnp.int32, joined.shape, 1)
    for index, block in enumerate(blocks):
        wide = jnp.concatenate([block] * (total // block.shape[1]), axis=1)
        if index > 0:
            wide = pltpu.roll(wide, index * width, 1)
        here = (lane >= index * width) & (lane < (index + 1) * width)
        joined = jnp.where(here, wide, joined)
    return joined


def roll_lanes(values, shift):
    shift = shift % values.shape[1]
    return pltpu.roll(values, shift, 1) if shift else values


def pair_sides(pair, slot, degree_count):
    low_side = slot < degree_count - pair
    low_weight = jnp.where(pair == 0, 1.0, 2.0)
    high_weight = jnp.where(2 * pair == degree_count - 1, 0.0, 2.0)
    return low_side, low_weight, high_weight


def project_kernel(
    pack,
    wire_pack,
    groups,
    bands,
    owners,
    pairs_held,
    share,
    first_part,
    last_part,
    source_ref,
    own_ref,
    *refs,
):
    is_first = first_part == 0
    remote = (last_part - first_part) * (bands - 1)
    part_refs = refs[:remote]
    if is_first:
        coef_ref, table_ref, sums_ref, left_ref, flat_scr, left_scr = refs[remote:]
    else:
        earlier_ref, coef_ref, table_ref, spectra_ref = refs[remote:]
    pairs_sub, cycle_band, slot_count = own_ref.shape
    high_places = pairs_sub // pack
    degree_count = slot_count - 1
    panel_rows = coef_ref.shape[2]
    fields = panel_rows // 2
    block_rows = 4 * panel_rows
    pairs_part = pairs_sub // groups
    group = lax.axis_index("groups")
    band = lax.axis_index("band")
    first = lax.axis_index(owner_axes) * pairs_held + band * pairs_sub
    slot = lax.broadcasted_iota(jnp.int32, (panel_rows, slot_count), 1)
    row = lax.broadcasted_iota(jnp.int32, (panel_rows, slot_count // 2), 0)
    upper = lax.broadcasted_iota(jnp.int32, (panel_rows, slot_count), 0) < fields
    zero = jnp.zeros((panel_rows, slot_count), f32)
    high_power, high_cross = zero, zero
    all_power, all_cross = zero, zero
    if is_first:
        sources, wire_rows, _ = source_ref.shape
        for k in range(bands):
            other = band ^ k
            for w in range(owners):
                at = (k * owners + w) * wire_rows
                rows = source_ref[other * owners + w].astype(f32)
                for c in range(flat_scr.shape[0]):
                    flat_scr[c, at : at + wire_rows, :] = rows[:, c * lane_width : (c + 1) * lane_width]
        for place in range(pairs_sub):
            high_place, low_place = divmod(place, pack)
            wire_row = low_place // wire_pack * high_places + high_place
            received = jnp.concatenate(
                [
                    flat_scr[c, pl.ds(wire_row, sources, stride=wire_rows), :]
                    for c in range(flat_scr.shape[0])
                ],
                axis=1,
            )
            target, at = (left_scr, place) if place < pairs_part else (left_ref, place - pairs_part)
            for il in range(share):
                target[at, pl.ds(il, sources, stride=share), :] = take_block(
                    received, low_place % wire_pack * share + il, block_rows, left_scr.shape[2]
                )
        left_ref = left_scr
    else:
        left_ref = source_ref
        all_power, all_cross = earlier_ref[0], earlier_ref[1]
    for j in range(first_part, last_part):
        part_row = (group ^ j) * pairs_part
        low_power, low_cross = zero, zero
        for q in range(pairs_part):
            at = (j - first_part) * pairs_part + q
            left = left_ref[at, :, 0:block_rows].astype(bf16)
            blocks = [own_ref[part_row + q]] + [t[q] for t in part_refs[j - first_part :: last_part - first_part]]
            table = jnp.concatenate([b.astype(f32) for b in blocks], axis=0).astype(bf16)
            table_ref[at] = table
            both_halves = dot_tn(left, table)
            pair = first + part_row + q
            low_side, low_weight, high_weight = pair_sides(pair, slot, degree_count)
            cosines = jnp.where(
                low_side, both_halves[0:panel_rows], both_halves[2 * panel_rows : 3 * panel_rows]
            )
            sines = jnp.where(
                low_side, both_halves[panel_rows : 2 * panel_rows], both_halves[3 * panel_rows :]
            )
            coef_ref[at, 0] = cosines
            coef_ref[at, 1] = sines
            weight = jnp.where(low_side, low_weight, high_weight)
            power = (cosines * cosines + sines * sines) * weight
            straight = jnp.where(upper, cosines, sines)
            swapped = pltpu.roll(jnp.where(upper, sines, cosines), fields, 0)
            cross = straight * swapped * weight
            low_power = low_power + roll_lanes(jnp.where(low_side, power, 0.0), q)
            low_cross = low_cross + roll_lanes(jnp.where(low_side, cross, 0.0), q)
            high_power = high_power + jnp.where(low_side, 0.0, power)
            high_cross = high_cross + jnp.where(low_side, 0.0, cross)
        all_power = all_power + pltpu.roll(low_power, first + part_row, 1)
        all_cross = all_cross + pltpu.roll(low_cross, first + part_row, 1)
    all_power = all_power + pltpu.roll(high_power, slot_count - 1, 1)
    all_cross = all_cross + pltpu.roll(high_cross, slot_count - 1, 1)
    if is_first:
        sums_ref[0] = all_power
        sums_ref[1] = all_cross
    else:
        all_cross = all_cross + pltpu.roll(all_cross, fields, 0)
        spectra_ref[:, 0:slot_count] = all_power
        spectra_ref[:, slot_count:] = jnp.where(
            row < fields, all_cross[:, : slot_count // 2], all_cross[:, slot_count // 2 :]
        )


def tree_sum(parts):
    while len(parts) > 1:
        parts = [parts[i] + parts[i + 1] for i in range(0, len(parts), 2)]
    return parts[0]


def gradient_kernel(pack, groups, bands, owners, pairs_held, share, spectra_parts, *refs):
    spectra_refs = refs[:spectra_parts]
    coef_refs = refs[spectra_parts : spectra_parts + 2]
    table_refs = refs[spectra_parts + 2 : spectra_parts + 4]
    wire_ref, misfit_ref, flat_scr, cycle_scr = refs[spectra_parts + 4 :]
    sources, wire_rows, wire_lanes = wire_ref.shape
    pairs_part = coef_refs[0].shape[0]
    pairs_sub = groups * pairs_part
    slot_count = table_refs[0].shape[2]
    degree_count = slot_count - 1
    panel_rows = coef_refs[0].shape[2]
    fields = panel_rows // 2
    block_rows = 4 * fields
    fields_out = fields // bands
    group = lax.axis_index("groups")
    band = lax.axis_index("band")
    first = lax.axis_index(owner_axes) * pairs_held + band * pairs_sub
    slot = lax.broadcasted_iota(jnp.int32, (panel_rows, slot_count), 1)
    row = lax.broadcasted_iota(jnp.int32, (panel_rows, slot_count), 0)
    spectra = tree_sum([s[...] for s in spectra_refs])
    power = spectra[:, :slot_count]
    packed = spectra[:, slot_count:]
    turned = pltpu.roll(packed, fields, 0)
    upper = row[:, : slot_count // 2] < fields
    cross = jnp.concatenate([jnp.where(upper, packed, turned), jnp.where(upper, turned, packed)], axis=1)
    odd_weight = (2 * slot + 1).astype(f32)
    power = power / odd_weight + spectrum_floor
    cross = cross / odd_weight
    root = jnp.sqrt(power)
    other_root = pltpu.roll(root, fields, 0)
    both_power = power + pltpu.roll(power, fields, 0)
    geo_mean = root * other_root
    coherence = cross / geo_mean
    term = (root - other_root) * (root - other_root) + both_power * (1.0 - coherence)
    term = jnp.where(slot < degree_count, term, 0.0)
    mean = jnp.sum(term, axis=1, keepdims=True) / degree_count
    field_row = lax.broadcasted_iota(jnp.int32, (panel_rows, 1), 0)
    misfit_ref[...] = jnp.zeros_like(misfit_ref)
    for i in range(fields_out):
        chosen = jnp.where(field_row == band * fields_out + i, mean, 0.0)
        misfit_ref[i : i + 1, :] = jnp.broadcast_to(
            jnp.sum(chosen, axis=0, keepdims=True), (1, lane_width)
        )
    grad_power = (
        gradient_gain
        * (
            1.0
            - other_root / root
            + (1.0 - coherence)
            + both_power * coherence / (2.0 * power)
        )
        / odd_weight
    )
    grad_cross = -gradient_gain * both_power / geo_mean / odd_weight
    by_degree = jnp.where(row < fields, 2.0 * grad_power, grad_cross)
    high_grad = pltpu.roll(by_degree, 1, 1)
    blocks = []
    for j in range(groups):
        part_row = (group ^ j) * pairs_part
        low_grad = pltpu.roll(by_degree, slot_count - first - part_row, 1)
        for q in range(pairs_part):
            place = j * pairs_part + q
            at_part = (0, q) if j == 0 else (1, place - pairs_part)
            pair = first + part_row + q
            low_side, low_weight, high_weight = pair_sides(pair, slot, degree_count)
            shifted = roll_lanes(low_grad, slot_count - q)
            gain = jnp.where(low_side, shifted * low_weight, high_grad * high_weight)
            cosines = coef_refs[at_part[0]][at_part[1], 0] * gain
            sines = coef_refs[at_part[0]][at_part[1], 1] * gain
            swapped = pltpu.roll(jnp.where(row < fields, sines, cosines), fields, 0)
            grads = jnp.where(row < fields, cosines, sines) + swapped
            masked = jnp.concatenate(
                [jnp.where(low_side, grads, 0.0), jnp.where(low_side, 0.0, grads)], axis=0
            ).astype(bf16)
            cycle_scr[place, :, 0:block_rows] = dot_nt(
                table_refs[at_part[0]][at_part[1]], masked
            )
            high_place, low_place = divmod(place, pack)
            blocks = [] if low_place == 0 else blocks
            blocks += [cycle_scr[place, pl.ds(il, sources, stride=share), :] for il in range(share)]
            if low_place == pack - 1:
                joined = join_blocks(blocks, block_rows, wire_lanes)
                for c in range(flat_scr.shape[0]):
                    flat_scr[c, pl.ds(high_place, sources, stride=wire_rows), :] = joined[
                        :, c * lane_width : (c + 1) * lane_width
                    ]
    for k in range(bands):
        other = band ^ k
        for w in range(owners):
            at = (k * owners + w) * wire_rows
            wire_ref[other * owners + w] = jnp.concatenate(
                [flat_scr[c, at : at + wire_rows, :] for c in range(flat_scr.shape[0])], axis=1
            ).astype(bf16)


def synthesise_kernel(pack, coarse_ref, fine_ref, mask_ref, wire_ref, out_ref, flat_scr):
    share, fields, extent = out_ref.shape
    sources, wire_rows, wire_lanes = wire_ref.shape
    steps = extent // lane_width
    half_lanes = coarse_ref.shape[3] // 2
    panel_rows = 2 * fields
    width = sources * wire_rows
    for source in range(sources):
        flat_scr[source * wire_rows : (source + 1) * wire_rows, :] = wire_ref[source].astype(f32)
    if flat_scr.shape[0] > width:
        flat_scr[width:, :] = jnp.zeros_like(flat_scr[width:, :])
    turned = jnp.transpose(flat_scr[...])
    count = wire_lanes // pack
    if pack > 1:
        spare = jnp.zeros((count, round_up(half_lanes, lane_width) - turned.shape[1]), f32)
        values = jnp.zeros((count, half_lanes), f32)
        for low_place in range(pack):
            block = jnp.concatenate([turned[low_place * count : (low_place + 1) * count], spare], axis=1)
            values = values + move_lanes(block, [(0, width, low_place * width)], half_lanes)
    else:
        values = turned[:, :half_lanes]
    row = lax.broadcasted_iota(jnp.int32, (panel_rows, 2 * half_lanes), 0)
    for il in range(share):
        at = il * 2 * panel_rows
        direct = jnp.concatenate(
            [values[at : at + panel_rows], values[at + panel_rows : at + 2 * panel_rows]], axis=1
        )
        crossed = pltpu.roll(direct, fields, 0)
        crossed = jnp.where(row < fields, crossed, -crossed)
        pieces = [
            direct * coarse_ref[il, 0, j : j + 1, :] + crossed * coarse_ref[il, 1, j : j + 1, :]
            for j in range(steps)
        ]
        pieces = jnp.concatenate(pieces, 0).astype(bf16)
        fine = jnp.concatenate([fine_ref[il, 0], fine_ref[il, 1]], axis=0)
        total = dot_nt(pieces, fine)
        total_c, total_s = total[:, :lane_width], total[:, lane_width:]
        mask = mask_ref[il : il + 1, :]
        for j in range(steps):
            lanes = slice(lane_width * j, lane_width * (j + 1))
            at = j * panel_rows
            piece = total_c[at : at + fields] + total_s[at + fields : at + panel_rows]
            out_ref[il, :, lanes] = (piece * mask[:, lanes]).astype(bf16)


def call(body, name, arrays, spaces, out_shapes, scratch, flops=1):
    return pl.pallas_call(
        body,
        name=name,
        cost_estimate=pl.CostEstimate(flops=flops, transcendentals=0, bytes_accessed=1),
        in_specs=[pl.BlockSpec(memory_space=space) for space in spaces],
        out_specs=tuple(pl.BlockSpec(memory_space=pltpu.VMEM) for _ in out_shapes),
        out_shape=tuple(out_shapes),
        scratch_shapes=scratch,
        compiler_params=pltpu.CompilerParams(vmem_limit_bytes=vmem_bytes),
    )(*arrays)


def exchange(array, axes, count):
    return [array] + [
        lax.ppermute(array, axes, [(i, i ^ k) for i in range(count)]) for k in range(1, count)
    ]


def per_device(predicted_state, analysis_state, nodes_per_parallel, weighted_harmonic_table):
    share, fields, extent = predicted_state.shape
    pairs_held, cycle_band, slot_count = weighted_harmonic_table.shape
    groups = lax.axis_size("groups")
    bands = lax.axis_size("band")
    owners = lax.axis_size(owner_axes)
    group = lax.axis_index("groups")
    band = lax.axis_index("band")
    sources = bands * owners
    pairs_part = -(-pairs_held // (bands * groups))
    pairs_sub = groups * pairs_part
    panel_rows = 2 * fields
    pack = max(1, lane_width // (share * 4 * fields))
    wire_pack = 1
    wire_lanes = round_up(wire_pack * share * 4 * panel_rows, lane_width)
    back_lanes = round_up(pack * share * 4 * fields, lane_width)
    block_lanes = round_up(4 * panel_rows, lane_width)
    half_lanes = sources * pairs_sub
    coarse_rows = round_up(extent // lane_width, 8)

    table = weighted_harmonic_table
    if pairs_sub * bands != pairs_held:
        table = jnp.pad(table, ((0, pairs_sub * bands - pairs_held), (0, 0), (0, 0)))

    def over_bands(array, k):
        return lax.ppermute(array, "band", [(i, i ^ k) for i in range(bands)])

    starts = [((band ^ k) * groups + (group ^ j)) * pairs_part for k in range(1, bands) for j in range(groups)]
    pieces = [
        lax.dynamic_slice_in_dim(table, start, pairs_part, 0)
        for n, start in enumerate(starts)
        if n < groups or n % groups == 0
    ]
    pieces = lax.optimization_barrier(pieces)
    near = over_bands(jnp.stack(pieces[:groups]), 1)
    near = [near[j] for j in range(groups)]
    far = [over_bands(piece, n + 2) for n, piece in enumerate(pieces[groups:])]
    states = jnp.concatenate([predicted_state, analysis_state], axis=1)
    wire, coarse, fine, mask = call(
        functools.partial(
            analyse_kernel,
            pack,
            wire_pack,
            groups,
            bands,
            owners,
            pairs_held,
            pairs_part,
            slot_count - 1,
        ),
        "analyse",
        (nodes_per_parallel, states),
        (pltpu.SMEM, pltpu.VMEM),
        (
            jax.ShapeDtypeStruct((sources, pairs_sub // wire_pack, wire_lanes), bf16),
            jax.ShapeDtypeStruct((share, 2, coarse_rows, 2 * half_lanes), f32),
            jax.ShapeDtypeStruct((share, 2, lane_width, 2 * half_lanes), bf16),
            jax.ShapeDtypeStruct((share, extent), f32),
        ),
        [
            pltpu.VMEM((share * 4 * panel_rows, half_lanes), f32),
            pltpu.VMEM((wire_lanes, round_up(half_lanes // wire_pack, lane_width)), f32),
            pltpu.VMEM((round_up(half_lanes // wire_pack, lane_width), wire_lanes), f32),
        ],
    )
    wire = lax.all_to_all(wire, group_axes, 0, 0, tiled=True)
    parts = list(near)
    for piece in far:
        parts.append(piece)
        for j in range(1, groups):
            parts.append(lax.ppermute(piece, "groups", [(i, i ^ j) for i in range(groups)]))
    far[0], own_start = lax.optimization_barrier((far[0], band * pairs_sub))
    own_table = lax.dynamic_slice_in_dim(table, own_start, pairs_sub, 0)
    sizes = (pack, wire_pack, groups, bands, owners, pairs_held, share)
    other_pairs = pairs_sub - pairs_part
    left_shape = (bands * cycle_band, block_lanes)

    def pair_shapes(count):
        return (
            jax.ShapeDtypeStruct((count, 2, panel_rows, slot_count), f32),
            jax.ShapeDtypeStruct((count, bands * cycle_band, slot_count), bf16),
        )

    own_coef, own_rows, sums, left = call(
        functools.partial(project_kernel, *sizes, 0, 1),
        "project_own",
        (wire, own_table, *parts[0::groups]),
        (pltpu.VMEM,) * (1 + bands),
        (
            *pair_shapes(pairs_part),
            jax.ShapeDtypeStruct((2, panel_rows, slot_count), f32),
            jax.ShapeDtypeStruct((other_pairs, *left_shape), f32),
        ),
        [
            pltpu.VMEM((wire_lanes // lane_width, half_lanes // wire_pack, lane_width), f32),
            pltpu.VMEM((pairs_part, *left_shape), f32),
        ],
    )
    others = [p for n, p in enumerate(parts) if n % groups > 0]
    other_coef, other_rows, spectra = call(
        functools.partial(project_kernel, *sizes, 1, groups),
        "project",
        (left, own_table, *others, sums),
        (pltpu.VMEM,) * (3 + len(others)),
        (
            *pair_shapes(other_pairs),
            jax.ShapeDtypeStruct((panel_rows, slot_count + slot_count // 2), f32),
        ),
        [],
    )
    spectra = tree_sum(exchange(spectra, owner_axes, owners))
    spectra = exchange(spectra, "band", bands)
    wire, misfit = call(
        functools.partial(gradient_kernel, pack, groups, bands, owners, pairs_held, share, len(spectra)),
        "gradient",
        (*spectra, own_coef, other_coef, own_rows, other_rows),
        (pltpu.VMEM,) * (4 + len(spectra)),
        (
            jax.ShapeDtypeStruct((sources, pairs_sub // pack, back_lanes), bf16),
            jax.ShapeDtypeStruct((round_up(fields // bands, 8), lane_width), f32),
        ),
        [
            pltpu.VMEM((back_lanes // lane_width, half_lanes // pack, lane_width), f32),
            pltpu.VMEM((pairs_sub, *left_shape), f32),
        ],
    )
    wire = lax.all_to_all(wire, group_axes, 0, 0, tiled=True)
    (sensitivity,) = call(
        functools.partial(synthesise_kernel, pack),
        "synthesise",
        (coarse, fine, mask, wire),
        (pltpu.VMEM,) * 4,
        (jax.ShapeDtypeStruct((share, fields, extent), bf16),),
        [pltpu.VMEM((round_up(half_lanes // pack, lane_width), back_lanes), f32)],
    )
    return misfit[: fields // bands, 0], sensitivity


def solution(mesh):
    in_specs = (
        P(("groups", "band", "field", "wave"), None, None),
        P(("groups", "band", "field", "wave"), None, None),
        P(),
        P(("field", "wave"), "band", None),
    )
    out_specs = (P(("groups", "band")), P(("groups", "band", "field", "wave"), None, None))
    return jax.shard_map(
        per_device, mesh=mesh, in_specs=in_specs, out_specs=out_specs, check_vma=False
    )
```

```python
import functools
import math

import jax
import jax.numpy as jnp
from jax import lax
from jax.experimental import pallas as pl
from jax.experimental.pallas import tpu as pltpu
from jax.sharding import PartitionSpec as P

spectrum_floor = 0.25
gradient_gain = 16.0
lane_width = 128
vmem_bytes = 40 * 1024 * 1024
owner_axes = ("field", "wave")
group_axes = ("band", "field", "wave")
bf16 = jnp.bfloat16
f32 = jnp.float32


def round_up(value, step):
    return -(-value // step) * step


def dot_nn(left, right):
    return lax.dot_general(left, right, (((1,), (0,)), ((), ())), preferred_element_type=f32)


def dot_nt(left, right):
    return lax.dot_general(left, right, (((1,), (1,)), ((), ())), preferred_element_type=f32)


def dot_tn(left, right):
    return lax.dot_general(left, right, (((0,), (0,)), ((), ())), preferred_element_type=f32)


def split_index(index, size):
    whole = jnp.floor((index + 0.5) * (1.0 / size))
    return whole, index - whole * size


def wavenumbers(owner, band, half, rest, pairs_held, pairs_part, groups, degree_count):
    part, pair = split_index(rest, pairs_part)
    part = (lax.axis_index("groups") ^ part.astype(jnp.int32)).astype(f32)
    within = (band * groups + part) * pairs_part + pair
    pair = owner * pairs_held + within
    mirrored = degree_count - 1.0 - pair
    wavenum = jnp.where(half > 0.0, mirrored, pair)
    void = (within >= pairs_held) | ((half > 0.0) & (mirrored == pair))
    return jnp.where(void, 4.0 * degree_count, wavenum)


def own_wavenumbers(lanes, pack, bands, owners, pairs_held, pairs_part, groups, degree_count):
    index = lax.broadcasted_iota(jnp.int32, (1, lanes), 1).astype(f32)
    half, index = split_index(index, lanes // 2)
    rows = groups * pairs_part // pack
    low_place, index = split_index(index, bands * owners * rows)
    block, high_place = split_index(index, rows)
    band, owner = split_index(block, owners)
    rest = high_place * pack + low_place
    return wavenumbers(owner, band, half, rest, pairs_held, pairs_part, groups, degree_count)


def move_lanes(values, moves, lanes):
    total = values.shape[1]
    moved = jnp.zeros(values.shape, f32)
    lane = lax.broadcasted_iota(jnp.int32, values.shape, 1)
    for start, width, place in moves:
        shift = (place - start) % total
        turned = pltpu.roll(values, shift, 1) if shift else values
        moved = jnp.where((lane >= place) & (lane < place + width), turned, moved)
    return moved[:, :lanes]


def cos_and_minus_sin(wavenum, points, columns, inverse):
    quarters = (4.0 * wavenum) * columns
    turns = jnp.floor(quarters * inverse + 0.5)
    angle = (quarters - turns * points) * (0.5 * math.pi * inverse)
    square = angle * angle
    sine = angle * (1.0 + square * (-1.0 / 6 + square * (1.0 / 120 + square * (-1.0 / 5040))))
    cosine = 1.0 + square * (
        -0.5 + square * (1.0 / 24 + square * (-1.0 / 720 + square * (1.0 / 40320)))
    )
    quadrant = turns.astype(jnp.int32)
    swap = (quadrant & 1) != 0
    new_cos = jnp.where(swap, sine, cosine)
    new_sin = jnp.where(swap, cosine, sine)
    new_cos = jnp.where(((quadrant + 1) & 2) != 0, -new_cos, new_cos)
    new_sin = jnp.where((quadrant & 2) != 0, new_sin, -new_sin)
    return new_cos, new_sin


def fill_tables(points_i, wavenum, coarse_ref, fine_ref, at):
    lanes = wavenum.shape[1]
    points = jnp.full((1, lanes), points_i, jnp.int32).astype(f32)
    inverse = 1.0 / points
    scale = jnp.where(2.0 * wavenum < points, 1.0 / jnp.sqrt(points), 0.0)

    def rows_of(count, step):
        return (lax.broadcasted_iota(jnp.int32, (count, lanes), 0) * step).astype(f32)

    coarse_rows = coarse_ref.shape[2]
    coarse_c, coarse_s = cos_and_minus_sin(wavenum, points, rows_of(coarse_rows, lane_width), inverse)
    coarse_ref[at, 0] = coarse_c * scale
    coarse_ref[at, 1] = coarse_s * scale
    mid_c, mid_s = cos_and_minus_sin(wavenum, points, rows_of(lane_width // 8, 8), inverse)
    unit_c, unit_s = cos_and_minus_sin(wavenum, points, rows_of(8, 1), inverse)
    for g in range(lane_width // 16):
        pieces_c = []
        pieces_s = []
        for a in (2 * g, 2 * g + 1):
            step_c = mid_c[a : a + 1]
            step_s = mid_s[a : a + 1]
            pieces_c.append(step_c * unit_c - step_s * unit_s)
            pieces_s.append(step_c * unit_s + step_s * unit_c)
        fine_ref[at, 0, 16 * g : 16 * g + 16] = jnp.concatenate(pieces_c, 0).astype(bf16)
        fine_ref[at, 1, 16 * g : 16 * g + 16] = jnp.concatenate(pieces_s, 0).astype(bf16)


def analyse_kernel(
    pack,
    wire_pack,
    groups,
    bands,
    owners,
    pairs_held,
    pairs_part,
    degree_count,
    nodes_ref,
    states_ref,
    wire_ref,
    coarse_ref,
    fine_ref,
    mask_ref,
    rows_scr,
    wide_scr,
    flat_scr,
):
    share, panel_rows, extent = states_ref.shape
    steps = extent // lane_width
    half_lanes = coarse_ref.shape[3] // 2
    first_cycle = lax.axis_index(group_axes) * share
    column = lax.broadcasted_iota(jnp.int32, (1, extent), 1)
    wavenum = own_wavenumbers(
        2 * half_lanes, pack, bands, owners, pairs_held, pairs_part, groups, degree_count
    )
    for il in range(share):
        points_i = nodes_ref[first_cycle + il]
        fill_tables(points_i, wavenum, coarse_ref, fine_ref, il)
        held = column < points_i
        mask_ref[il : il + 1, :] = held.astype(f32)
        panel = jnp.where(held, states_ref[il].astype(f32), 0.0)
        stacked = jnp.concatenate(
            [panel[:, lane_width * j : lane_width * (j + 1)] for j in range(steps)], axis=0
        ).astype(bf16)
        for h in range(2):
            lanes = slice(h * half_lanes, (h + 1) * half_lanes)
            part_c = dot_nn(stacked, fine_ref[il, 0, :, lanes])
            part_s = dot_nn(stacked, fine_ref[il, 1, :, lanes])
            total_c = jnp.zeros((panel_rows, half_lanes), f32)
            total_s = jnp.zeros((panel_rows, half_lanes), f32)
            for j in range(steps):
                turn_c = coarse_ref[il, 0, j : j + 1, lanes]
                turn_s = coarse_ref[il, 1, j : j + 1, lanes]
                piece_c = part_c[j * panel_rows : (j + 1) * panel_rows]
                piece_s = part_s[j * panel_rows : (j + 1) * panel_rows]
                total_c = total_c + (turn_c * piece_c - turn_s * piece_s)
                total_s = total_s + (turn_c * piece_s + turn_s * piece_c)
            at = (il * 2 + h) * 2 * panel_rows
            rows_scr[at : at + panel_rows, :] = total_c
            rows_scr[at + panel_rows : at + 2 * panel_rows, :] = total_s
    sources = bands * owners
    rows = groups * pairs_part // pack
    width = sources * rows
    count = rows_scr.shape[0]
    parts = pack // wire_pack
    values = rows_scr[...]
    if wide_scr.shape[0] > wire_pack * count:
        wide_scr[wire_pack * count :, :] = jnp.zeros_like(wide_scr[wire_pack * count :, :])
    for d in range(wire_pack):
        moves = [((e * wire_pack + d) * width, width, e * width) for e in range(parts)]
        wide_scr[d * count : (d + 1) * count, :] = move_lanes(values, moves, wide_scr.shape[1])
    flat_scr[...] = jnp.transpose(wide_scr[...])
    for source in range(sources):
        starts = [(e * sources + source) * rows for e in range(parts)]
        wire_ref[source] = jnp.concatenate(
            [flat_scr[at : at + rows, :] for at in starts], axis=0
        ).astype(bf16)


def take_block(rows, index, width, lanes):
    if width % lane_width == 0:
        return rows[:, index * width : (index + 1) * width]
    total = rows.shape[1]
    if index > 0:
        rows = pltpu.roll(rows, total - index * width, 1)
    return rows[:, :lanes]


def join_blocks(blocks, width, total):
    if width % lane_width == 0:
        return jnp.concatenate(blocks, axis=1)
    joined = jnp.zeros((blocks[0].shape[0], total), f32)
    lane = lax.broadcasted_iota(jnp.int32, joined.shape, 1)
    for index, block in enumerate(blocks):
        wide = jnp.concatenate([block] * (total // block.shape[1]), axis=1)
        if index > 0:
            wide = pltpu.roll(wide, index * width, 1)
        here = (lane >= index * width) & (lane < (index + 1) * width)
        joined = jnp.where(here, wide, joined)
    return joined


def roll_lanes(values, shift):
    shift = shift % values.shape[1]
    return pltpu.roll(values, shift, 1) if shift else values


def pair_sides(pair, slot, degree_count):
    low_side = slot < degree_count - pair
    low_weight = jnp.where(pair == 0, 1.0, 2.0)
    high_weight = jnp.where(2 * pair == degree_count - 1, 0.0, 2.0)
    return low_side, low_weight, high_weight


def project_kernel(
    pack,
    wire_pack,
    groups,
    bands,
    owners,
    pairs_held,
    share,
    first_part,
    last_part,
    source_ref,
    own_ref,
    *refs,
):
    is_first = first_part == 0
    remote = (last_part - first_part) * (bands - 1)
    part_refs = refs[:remote]
    if is_first:
        coef_ref, table_ref, sums_ref, left_ref, flat_scr, left_scr = refs[remote:]
    else:
        earlier_ref, coef_ref, table_ref, spectra_ref = refs[remote:]
    pairs_sub, cycle_band, slot_count = own_ref.shape
    high_places = pairs_sub // pack
    degree_count = slot_count - 1
    panel_rows = coef_ref.shape[2]
    fields = panel_rows // 2
    block_rows = 4 * panel_rows
    pairs_part = pairs_sub // groups
    group = lax.axis_index("groups")
    band = lax.axis_index("band")
    first = lax.axis_index(owner_axes) * pairs_held + band * pairs_sub
    slot = lax.broadcasted_iota(jnp.int32, (panel_rows, slot_count), 1)
    row = lax.broadcasted_iota(jnp.int32, (panel_rows, slot_count // 2), 0)
    upper = lax.broadcasted_iota(jnp.int32, (panel_rows, slot_count), 0) < fields
    zero = jnp.zeros((panel_rows, slot_count), f32)
    high_power, high_cross = zero, zero
    all_power, all_cross = zero, zero
    if is_first:
        sources, wire_rows, _ = source_ref.shape
        for k in range(bands):
            other = band ^ k
            for w in range(owners):
                at = (k * owners + w) * wire_rows
                rows = source_ref[other * owners + w].astype(f32)
                for c in range(flat_scr.shape[0]):
                    flat_scr[c, at : at + wire_rows, :] = rows[:, c * lane_width : (c + 1) * lane_width]
        for place in range(pairs_sub):
            high_place, low_place = divmod(place, pack)
            wire_row = low_place // wire_pack * high_places + high_place
            received = jnp.concatenate(
                [
                    flat_scr[c, pl.ds(wire_row, sources, stride=wire_rows), :]
                    for c in range(flat_scr.shape[0])
                ],
                axis=1,
            )
            target, at = (left_scr, place) if place < pairs_part else (left_ref, place - pairs_part)
            for il in range(share):
                target[at, pl.ds(il, sources, stride=share), :] = take_block(
                    received, low_place % wire_pack * share + il, block_rows, left_scr.shape[2]
                )
        left_ref = left_scr
    else:
        left_ref = source_ref
        all_power, all_cross = earlier_ref[0], earlier_ref[1]
    for j in range(first_part, last_part):
        part_row = (group ^ j) * pairs_part
        low_power, low_cross = zero, zero
        for q in range(pairs_part):
            at = (j - first_part) * pairs_part + q
            left = left_ref[at, :, 0:block_rows].astype(bf16)
            blocks = [own_ref[part_row + q]] + [t[q] for t in part_refs[j - first_part :: last_part - first_part]]
            table = jnp.concatenate([b.astype(f32) for b in blocks], axis=0).astype(bf16)
            table_ref[at] = table
            both_halves = dot_tn(left, table)
            pair = first + part_row + q
            low_side, low_weight, high_weight = pair_sides(pair, slot, degree_count)
            cosines = jnp.where(
                low_side, both_halves[0:panel_rows], both_halves[2 * panel_rows : 3 * panel_rows]
            )
            sines = jnp.where(
                low_side, both_halves[panel_rows : 2 * panel_rows], both_halves[3 * panel_rows :]
            )
            coef_ref[at, 0] = cosines
            coef_ref[at, 1] = sines
            weight = jnp.where(low_side, low_weight, high_weight)
            power = (cosines * cosines + sines * sines) * weight
            straight = jnp.where(upper, cosines, sines)
            swapped = pltpu.roll(jnp.where(upper, sines, cosines), fields, 0)
            cross = straight * swapped * weight
            low_power = low_power + roll_lanes(jnp.where(low_side, power, 0.0), q)
            low_cross = low_cross + roll_lanes(jnp.where(low_side, cross, 0.0), q)
            high_power = high_power + jnp.where(low_side, 0.0, power)
            high_cross = high_cross + jnp.where(low_side, 0.0, cross)
        all_power = all_power + pltpu.roll(low_power, first + part_row, 1)
        all_cross = all_cross + pltpu.roll(low_cross, first + part_row, 1)
    all_power = all_power + pltpu.roll(high_power, slot_count - 1, 1)
    all_cross = all_cross + pltpu.roll(high_cross, slot_count - 1, 1)
    if is_first:
        sums_ref[0] = all_power
        sums_ref[1] = all_cross
    else:
        all_cross = all_cross + pltpu.roll(all_cross, fields, 0)
        spectra_ref[:, 0:slot_count] = all_power
        spectra_ref[:, slot_count:] = jnp.where(
            row < fields, all_cross[:, : slot_count // 2], all_cross[:, slot_count // 2 :]
        )


def tree_sum(parts):
    while len(parts) > 1:
        parts = [parts[i] + parts[i + 1] for i in range(0, len(parts), 2)]
    return parts[0]


def gradient_kernel(pack, groups, bands, owners, pairs_held, share, spectra_parts, *refs):
    spectra_refs = refs[:spectra_parts]
    coef_refs = refs[spectra_parts : spectra_parts + 2]
    table_refs = refs[spectra_parts + 2 : spectra_parts + 4]
    wire_ref, misfit_ref, flat_scr, cycle_scr = refs[spectra_parts + 4 :]
    sources, wire_rows, wire_lanes = wire_ref.shape
    pairs_part = coef_refs[0].shape[0]
    pairs_sub = groups * pairs_part
    slot_count = table_refs[0].shape[2]
    degree_count = slot_count - 1
    panel_rows = coef_refs[0].shape[2]
    fields = panel_rows // 2
    block_rows = 4 * fields
    fields_out = fields // bands
    group = lax.axis_index("groups")
    band = lax.axis_index("band")
    first = lax.axis_index(owner_axes) * pairs_held + band * pairs_sub
    slot = lax.broadcasted_iota(jnp.int32, (panel_rows, slot_count), 1)
    row = lax.broadcasted_iota(jnp.int32, (panel_rows, slot_count), 0)
    spectra = tree_sum([s[...] for s in spectra_refs])
    power = spectra[:, :slot_count]
    packed = spectra[:, slot_count:]
    turned = pltpu.roll(packed, fields, 0)
    upper = row[:, : slot_count // 2] < fields
    cross = jnp.concatenate([jnp.where(upper, packed, turned), jnp.where(upper, turned, packed)], axis=1)
    odd_weight = (2 * slot + 1).astype(f32)
    per_degree = 1.0 / odd_weight
    power = power * per_degree + spectrum_floor
    cross = cross * per_degree
    root = jnp.sqrt(power)
    other_root = pltpu.roll(root, fields, 0)
    both_power = power + pltpu.roll(power, fields, 0)
    geo_mean = root * other_root
    over_geo = 1.0 / geo_mean
    over_power = 1.0 / power
    coherence = cross * over_geo
    term = (root - other_root) * (root - other_root) + both_power * (1.0 - coherence)
    term = jnp.where(slot < degree_count, term, 0.0)
    mean = jnp.sum(term, axis=1, keepdims=True) / degree_count
    field_row = lax.broadcasted_iota(jnp.int32, (panel_rows, 1), 0)
    misfit_ref[...] = jnp.zeros_like(misfit_ref)
    for i in range(fields_out):
        chosen = jnp.where(field_row == band * fields_out + i, mean, 0.0)
        misfit_ref[i : i + 1, :] = jnp.broadcast_to(
            jnp.sum(chosen, axis=0, keepdims=True), (1, lane_width)
        )
    grad_power = (
        gradient_gain
        * (
            1.0
            - geo_mean * over_power
            + (1.0 - coherence)
            + 0.5 * both_power * coherence * over_power
        )
        * per_degree
    )
    grad_cross = -gradient_gain * both_power * over_geo * per_degree
    by_degree = jnp.where(row < fields, 2.0 * grad_power, grad_cross)
    high_grad = pltpu.roll(by_degree, 1, 1)
    blocks = []
    for j in range(groups):
        part_row = (group ^ j) * pairs_part
        low_grad = pltpu.roll(by_degree, slot_count - first - part_row, 1)
        for q in range(pairs_part):
            place = j * pairs_part + q
            at_part = (0, q) if j == 0 else (1, place - pairs_part)
            pair = first + part_row + q
            low_side, low_weight, high_weight = pair_sides(pair, slot, degree_count)
            shifted = roll_lanes(low_grad, slot_count - q)
            gain = jnp.where(low_side, shifted * low_weight, high_grad * high_weight)
            cosines = coef_refs[at_part[0]][at_part[1], 0] * gain
            sines = coef_refs[at_part[0]][at_part[1], 1] * gain
            swapped = pltpu.roll(jnp.where(row < fields, sines, cosines), fields, 0)
            grads = jnp.where(row < fields, cosines, sines) + swapped
            masked = jnp.concatenate(
                [jnp.where(low_side, grads, 0.0), jnp.where(low_side, 0.0, grads)], axis=0
            ).astype(bf16)
            cycle_scr[place, :, 0:block_rows] = dot_nt(
                table_refs[at_part[0]][at_part[1]], masked
            )
            high_place, low_place = divmod(place, pack)
            blocks = [] if low_place == 0 else blocks
            blocks += [cycle_scr[place, pl.ds(il, sources, stride=share), :] for il in range(share)]
            if low_place == pack - 1:
                joined = join_blocks(blocks, block_rows, wire_lanes)
                for c in range(flat_scr.shape[0]):
                    flat_scr[c, pl.ds(high_place, sources, stride=wire_rows), :] = joined[
                        :, c * lane_width : (c + 1) * lane_width
                    ]
    for k in range(bands):
        other = band ^ k
        for w in range(owners):
            at = (k * owners + w) * wire_rows
            wire_ref[other * owners + w] = jnp.concatenate(
                [flat_scr[c, at : at + wire_rows, :] for c in range(flat_scr.shape[0])], axis=1
            ).astype(bf16)


def synthesise_kernel(pack, coarse_ref, fine_ref, mask_ref, wire_ref, out_ref, flat_scr):
    share, fields, extent = out_ref.shape
    sources, wire_rows, wire_lanes = wire_ref.shape
    steps = extent // lane_width
    half_lanes = coarse_ref.shape[3] // 2
    panel_rows = 2 * fields
    width = sources * wire_rows
    for source in range(sources):
        flat_scr[source * wire_rows : (source + 1) * wire_rows, :] = wire_ref[source].astype(f32)
    if flat_scr.shape[0] > width:
        flat_scr[width:, :] = jnp.zeros_like(flat_scr[width:, :])
    turned = jnp.transpose(flat_scr[...])
    count = wire_lanes // pack
    if pack > 1:
        spare = jnp.zeros((count, round_up(half_lanes, lane_width) - turned.shape[1]), f32)
        values = jnp.zeros((count, half_lanes), f32)
        for low_place in range(pack):
            block = jnp.concatenate([turned[low_place * count : (low_place + 1) * count], spare], axis=1)
            values = values + move_lanes(block, [(0, width, low_place * width)], half_lanes)
    else:
        values = turned[:, :half_lanes]
    row = lax.broadcasted_iota(jnp.int32, (panel_rows, 2 * half_lanes), 0)
    for il in range(share):
        at = il * 2 * panel_rows
        direct = jnp.concatenate(
            [values[at : at + panel_rows], values[at + panel_rows : at + 2 * panel_rows]], axis=1
        )
        crossed = pltpu.roll(direct, fields, 0)
        crossed = jnp.where(row < fields, crossed, -crossed)
        pieces = [
            direct * coarse_ref[il, 0, j : j + 1, :] + crossed * coarse_ref[il, 1, j : j + 1, :]
            for j in range(steps)
        ]
        pieces = jnp.concatenate(pieces, 0).astype(bf16)
        fine = jnp.concatenate([fine_ref[il, 0], fine_ref[il, 1]], axis=0)
        total = dot_nt(pieces, fine)
        total_c, total_s = total[:, :lane_width], total[:, lane_width:]
        mask = mask_ref[il : il + 1, :]
        for j in range(steps):
            lanes = slice(lane_width * j, lane_width * (j + 1))
            at = j * panel_rows
            piece = total_c[at : at + fields] + total_s[at + fields : at + panel_rows]
            out_ref[il, :, lanes] = (piece * mask[:, lanes]).astype(bf16)


def call(body, name, arrays, spaces, out_shapes, scratch, flops=1):
    return pl.pallas_call(
        body,
        name=name,
        cost_estimate=pl.CostEstimate(flops=flops, transcendentals=0, bytes_accessed=1),
        in_specs=[pl.BlockSpec(memory_space=space) for space in spaces],
        out_specs=tuple(pl.BlockSpec(memory_space=pltpu.VMEM) for _ in out_shapes),
        out_shape=tuple(out_shapes),
        scratch_shapes=scratch,
        compiler_params=pltpu.CompilerParams(vmem_limit_bytes=vmem_bytes),
    )(*arrays)


def exchange(array, axes, count):
    return [array] + [
        lax.ppermute(array, axes, [(i, i ^ k) for i in range(count)]) for k in range(1, count)
    ]


def per_device(predicted_state, analysis_state, nodes_per_parallel, weighted_harmonic_table):
    share, fields, extent = predicted_state.shape
    pairs_held, cycle_band, slot_count = weighted_harmonic_table.shape
    groups = lax.axis_size("groups")
    bands = lax.axis_size("band")
    owners = lax.axis_size(owner_axes)
    group = lax.axis_index("groups")
    band = lax.axis_index("band")
    sources = bands * owners
    pairs_part = -(-pairs_held // (bands * groups))
    pairs_sub = groups * pairs_part
    panel_rows = 2 * fields
    pack = max(1, lane_width // (share * 4 * fields))
    wire_pack = 1
    wire_lanes = round_up(wire_pack * share * 4 * panel_rows, lane_width)
    back_lanes = round_up(pack * share * 4 * fields, lane_width)
    block_lanes = round_up(4 * panel_rows, lane_width)
    half_lanes = sources * pairs_sub
    coarse_rows = round_up(extent // lane_width, 8)

    table = weighted_harmonic_table
    if pairs_sub * bands != pairs_held:
        table = jnp.pad(table, ((0, pairs_sub * bands - pairs_held), (0, 0), (0, 0)))

    def over_bands(array, k):
        return lax.ppermute(array, "band", [(i, i ^ k) for i in range(bands)])

    starts = [((band ^ k) * groups + (group ^ j)) * pairs_part for k in range(1, bands) for j in range(groups)]
    pieces = [
        lax.dynamic_slice_in_dim(table, start, pairs_part, 0)
        for n, start in enumerate(starts)
        if n < groups or n % groups == 0
    ]
    pieces = lax.optimization_barrier(pieces)
    near = over_bands(jnp.stack(pieces[:groups]), 1)
    near = [near[j] for j in range(groups)]
    far = [over_bands(piece, n + 2) for n, piece in enumerate(pieces[groups:])]
    states = jnp.concatenate([predicted_state, analysis_state], axis=1)
    wire, coarse, fine, mask = call(
        functools.partial(
            analyse_kernel,
            pack,
            wire_pack,
            groups,
            bands,
            owners,
            pairs_held,
            pairs_part,
            slot_count - 1,
        ),
        "analyse",
        (nodes_per_parallel, states),
        (pltpu.SMEM, pltpu.VMEM),
        (
            jax.ShapeDtypeStruct((sources, pairs_sub // wire_pack, wire_lanes), bf16),
            jax.ShapeDtypeStruct((share, 2, coarse_rows, 2 * half_lanes), f32),
            jax.ShapeDtypeStruct((share, 2, lane_width, 2 * half_lanes), bf16),
            jax.ShapeDtypeStruct((share, extent), f32),
        ),
        [
            pltpu.VMEM((share * 4 * panel_rows, half_lanes), f32),
            pltpu.VMEM((wire_lanes, round_up(half_lanes // wire_pack, lane_width)), f32),
            pltpu.VMEM((round_up(half_lanes // wire_pack, lane_width), wire_lanes), f32),
        ],
    )
    wire = lax.all_to_all(wire, group_axes, 0, 0, tiled=True)
    parts = list(near)
    for piece in far:
        parts.append(piece)
        for j in range(1, groups):
            parts.append(lax.ppermute(piece, "groups", [(i, i ^ j) for i in range(groups)]))
    far[0], own_start = lax.optimization_barrier((far[0], band * pairs_sub))
    own_table = lax.dynamic_slice_in_dim(table, own_start, pairs_sub, 0)
    sizes = (pack, wire_pack, groups, bands, owners, pairs_held, share)
    other_pairs = pairs_sub - pairs_part
    left_shape = (bands * cycle_band, block_lanes)

    def pair_shapes(count):
        return (
            jax.ShapeDtypeStruct((count, 2, panel_rows, slot_count), f32),
            jax.ShapeDtypeStruct((count, bands * cycle_band, slot_count), bf16),
        )

    own_coef, own_rows, sums, left = call(
        functools.partial(project_kernel, *sizes, 0, 1),
        "project_own",
        (wire, own_table, *parts[0::groups]),
        (pltpu.VMEM,) * (1 + bands),
        (
            *pair_shapes(pairs_part),
            jax.ShapeDtypeStruct((2, panel_rows, slot_count), f32),
            jax.ShapeDtypeStruct((other_pairs, *left_shape), f32),
        ),
        [
            pltpu.VMEM((wire_lanes // lane_width, half_lanes // wire_pack, lane_width), f32),
            pltpu.VMEM((pairs_part, *left_shape), f32),
        ],
    )
    others = [p for n, p in enumerate(parts) if n % groups > 0]
    other_coef, other_rows, spectra = call(
        functools.partial(project_kernel, *sizes, 1, groups),
        "project",
        (left, own_table, *others, sums),
        (pltpu.VMEM,) * (3 + len(others)),
        (
            *pair_shapes(other_pairs),
            jax.ShapeDtypeStruct((panel_rows, slot_count + slot_count // 2), f32),
        ),
        [],
    )
    spectra = tree_sum(exchange(spectra, "band", bands))
    spectra = exchange(spectra, owner_axes, owners)
    wire, misfit = call(
        functools.partial(gradient_kernel, pack, groups, bands, owners, pairs_held, share, len(spectra)),
        "gradient",
        (*spectra, own_coef, other_coef, own_rows, other_rows),
        (pltpu.VMEM,) * (4 + len(spectra)),
        (
            jax.ShapeDtypeStruct((sources, pairs_sub // pack, back_lanes), bf16),
            jax.ShapeDtypeStruct((round_up(fields // bands, 8), lane_width), f32),
        ),
        [
            pltpu.VMEM((back_lanes // lane_width, half_lanes // pack, lane_width), f32),
            pltpu.VMEM((pairs_sub, *left_shape), f32),
        ],
    )
    wire = lax.all_to_all(wire, group_axes, 0, 0, tiled=True)
    (sensitivity,) = call(
        functools.partial(synthesise_kernel, pack),
        "synthesise",
        (coarse, fine, mask, wire),
        (pltpu.VMEM,) * 4,
        (jax.ShapeDtypeStruct((share, fields, extent), bf16),),
        [pltpu.VMEM((round_up(half_lanes // pack, lane_width), back_lanes), f32)],
    )
    return misfit[: fields // bands, 0], sensitivity


def solution(mesh):
    in_specs = (
        P(("groups", "band", "field", "wave"), None, None),
        P(("groups", "band", "field", "wave"), None, None),
        P(),
        P(("field", "wave"), "band", None),
    )
    out_specs = (P(("groups", "band")), P(("groups", "band", "field", "wave"), None, None))
    return jax.shard_map(
        per_device, mesh=mesh, in_specs=in_specs, out_specs=out_specs, check_vma=False
    )
```

```python
import functools
import math

import jax
import jax.numpy as jnp
from jax import lax
from jax.experimental import pallas as pl
from jax.experimental.pallas import tpu as pltpu
from jax.sharding import PartitionSpec as P

spectrum_floor = 0.25
gradient_gain = 16.0
lane_width = 128
vmem_bytes = 40 * 1024 * 1024
owner_axes = ("field", "wave")
group_axes = ("band", "field", "wave")
bf16 = jnp.bfloat16
f32 = jnp.float32


def round_up(value, step):
    return -(-value // step) * step


def dot_nn(left, right):
    return lax.dot_general(left, right, (((1,), (0,)), ((), ())), preferred_element_type=f32)


def dot_nt(left, right):
    return lax.dot_general(left, right, (((1,), (1,)), ((), ())), preferred_element_type=f32)


def dot_tn(left, right):
    return lax.dot_general(left, right, (((0,), (0,)), ((), ())), preferred_element_type=f32)


def split_index(index, size):
    whole = jnp.floor((index + 0.5) * (1.0 / size))
    return whole, index - whole * size


def wavenumbers(owner, band, half, rest, pairs_held, pairs_part, groups, degree_count):
    part, pair = split_index(rest, pairs_part)
    part = (lax.axis_index("groups") ^ part.astype(jnp.int32)).astype(f32)
    within = (band * groups + part) * pairs_part + pair
    pair = owner * pairs_held + within
    mirrored = degree_count - 1.0 - pair
    wavenum = jnp.where(half > 0.0, mirrored, pair)
    void = (within >= pairs_held) | ((half > 0.0) & (mirrored == pair))
    return jnp.where(void, 4.0 * degree_count, wavenum)


def own_wavenumbers(lanes, pack, bands, owners, pairs_held, pairs_part, groups, degree_count):
    index = lax.broadcasted_iota(jnp.int32, (1, lanes), 1).astype(f32)
    half, index = split_index(index, lanes // 2)
    rows = groups * pairs_part // pack
    low_place, index = split_index(index, bands * owners * rows)
    block, high_place = split_index(index, rows)
    band, owner = split_index(block, owners)
    rest = high_place * pack + low_place
    return wavenumbers(owner, band, half, rest, pairs_held, pairs_part, groups, degree_count)


def move_lanes(values, moves, lanes):
    total = values.shape[1]
    moved = jnp.zeros(values.shape, f32)
    lane = lax.broadcasted_iota(jnp.int32, values.shape, 1)
    for start, width, place in moves:
        shift = (place - start) % total
        turned = pltpu.roll(values, shift, 1) if shift else values
        moved = jnp.where((lane >= place) & (lane < place + width), turned, moved)
    return moved[:, :lanes]


def cos_and_minus_sin(wavenum, points, columns, inverse):
    quarters = (4.0 * wavenum) * columns
    turns = jnp.floor(quarters * inverse + 0.5)
    angle = (quarters - turns * points) * (0.5 * math.pi * inverse)
    square = angle * angle
    sine = angle * (1.0 + square * (-1.0 / 6 + square * (1.0 / 120 + square * (-1.0 / 5040))))
    cosine = 1.0 + square * (
        -0.5 + square * (1.0 / 24 + square * (-1.0 / 720 + square * (1.0 / 40320)))
    )
    quadrant = turns.astype(jnp.int32)
    swap = (quadrant & 1) != 0
    new_cos = jnp.where(swap, sine, cosine)
    new_sin = jnp.where(swap, cosine, sine)
    new_cos = jnp.where(((quadrant + 1) & 2) != 0, -new_cos, new_cos)
    new_sin = jnp.where((quadrant & 2) != 0, new_sin, -new_sin)
    return new_cos, new_sin


def fill_tables(points_i, wavenum, coarse_ref, fine_ref, at):
    lanes = wavenum.shape[1]
    points = jnp.full((1, lanes), points_i, jnp.int32).astype(f32)
    inverse = 1.0 / points
    scale = jnp.where(2.0 * wavenum < points, 1.0 / jnp.sqrt(points), 0.0)

    def rows_of(count, step):
        return (lax.broadcasted_iota(jnp.int32, (count, lanes), 0) * step).astype(f32)

    coarse_rows = coarse_ref.shape[2]
    coarse_c, coarse_s = cos_and_minus_sin(wavenum, points, rows_of(coarse_rows, lane_width), inverse)
    coarse_ref[at, 0] = coarse_c * scale
    coarse_ref[at, 1] = coarse_s * scale
    mid_c, mid_s = cos_and_minus_sin(wavenum, points, rows_of(lane_width // 8, 8), inverse)
    unit_c, unit_s = cos_and_minus_sin(wavenum, points, rows_of(8, 1), inverse)
    for g in range(lane_width // 16):
        pieces_c = []
        pieces_s = []
        for a in (2 * g, 2 * g + 1):
            step_c = mid_c[a : a + 1]
            step_s = mid_s[a : a + 1]
            pieces_c.append(step_c * unit_c - step_s * unit_s)
            pieces_s.append(step_c * unit_s + step_s * unit_c)
        fine_ref[at, 0, 16 * g : 16 * g + 16] = jnp.concatenate(pieces_c, 0).astype(bf16)
        fine_ref[at, 1, 16 * g : 16 * g + 16] = jnp.concatenate(pieces_s, 0).astype(bf16)


def analyse_kernel(
    pack,
    wire_pack,
    groups,
    bands,
    owners,
    pairs_held,
    pairs_part,
    degree_count,
    nodes_ref,
    states_ref,
    wire_ref,
    coarse_ref,
    fine_ref,
    mask_ref,
    rows_scr,
    wide_scr,
    flat_scr,
):
    share, panel_rows, extent = states_ref.shape
    steps = extent // lane_width
    half_lanes = coarse_ref.shape[3] // 2
    first_cycle = lax.axis_index(group_axes) * share
    column = lax.broadcasted_iota(jnp.int32, (1, extent), 1)
    wavenum = own_wavenumbers(
        2 * half_lanes, pack, bands, owners, pairs_held, pairs_part, groups, degree_count
    )
    for il in range(share):
        points_i = nodes_ref[first_cycle + il]
        fill_tables(points_i, wavenum, coarse_ref, fine_ref, il)
        held = column < points_i
        mask_ref[il : il + 1, :] = held.astype(f32)
        panel = jnp.where(held, states_ref[il].astype(f32), 0.0)
        stacked = jnp.concatenate(
            [panel[:, lane_width * j : lane_width * (j + 1)] for j in range(steps)], axis=0
        ).astype(bf16)
        for h in range(2):
            lanes = slice(h * half_lanes, (h + 1) * half_lanes)
            part_c = dot_nn(stacked, fine_ref[il, 0, :, lanes])
            part_s = dot_nn(stacked, fine_ref[il, 1, :, lanes])
            total_c = jnp.zeros((panel_rows, half_lanes), f32)
            total_s = jnp.zeros((panel_rows, half_lanes), f32)
            for j in range(steps):
                turn_c = coarse_ref[il, 0, j : j + 1, lanes]
                turn_s = coarse_ref[il, 1, j : j + 1, lanes]
                piece_c = part_c[j * panel_rows : (j + 1) * panel_rows]
                piece_s = part_s[j * panel_rows : (j + 1) * panel_rows]
                total_c = total_c + (turn_c * piece_c - turn_s * piece_s)
                total_s = total_s + (turn_c * piece_s + turn_s * piece_c)
            at = (il * 2 + h) * 2 * panel_rows
            rows_scr[at : at + panel_rows, :] = total_c
            rows_scr[at + panel_rows : at + 2 * panel_rows, :] = total_s
    sources = bands * owners
    rows = groups * pairs_part // pack
    width = sources * rows
    count = rows_scr.shape[0]
    parts = pack // wire_pack
    values = rows_scr[...]
    if wide_scr.shape[0] > wire_pack * count:
        wide_scr[wire_pack * count :, :] = jnp.zeros_like(wide_scr[wire_pack * count :, :])
    for d in range(wire_pack):
        moves = [((e * wire_pack + d) * width, width, e * width) for e in range(parts)]
        wide_scr[d * count : (d + 1) * count, :] = move_lanes(values, moves, wide_scr.shape[1])
    flat_scr[...] = jnp.transpose(wide_scr[...])
    for source in range(sources):
        starts = [(e * sources + source) * rows for e in range(parts)]
        wire_ref[source] = jnp.concatenate(
            [flat_scr[at : at + rows, :] for at in starts], axis=0
        ).astype(bf16)


def take_block(rows, index, width, lanes):
    if width % lane_width == 0:
        return rows[:, index * width : (index + 1) * width]
    total = rows.shape[1]
    if index > 0:
        rows = pltpu.roll(rows, total - index * width, 1)
    return rows[:, :lanes]


def join_blocks(blocks, width, total):
    if width % lane_width == 0:
        return jnp.concatenate(blocks, axis=1)
    joined = jnp.zeros((blocks[0].shape[0], total), f32)
    lane = lax.broadcasted_iota(jnp.int32, joined.shape, 1)
    for index, block in enumerate(blocks):
        wide = jnp.concatenate([block] * (total // block.shape[1]), axis=1)
        if index > 0:
            wide = pltpu.roll(wide, index * width, 1)
        here = (lane >= index * width) & (lane < (index + 1) * width)
        joined = jnp.where(here, wide, joined)
    return joined


def roll_lanes(values, shift):
    shift = shift % values.shape[1]
    return pltpu.roll(values, shift, 1) if shift else values


def pair_sides(pair, slot, degree_count):
    low_side = slot < degree_count - pair
    low_weight = jnp.where(pair == 0, 1.0, 2.0)
    high_weight = jnp.where(2 * pair == degree_count - 1, 0.0, 2.0)
    return low_side, low_weight, high_weight


def project_kernel(
    pack,
    wire_pack,
    groups,
    bands,
    owners,
    pairs_held,
    share,
    first_part,
    last_part,
    source_ref,
    own_ref,
    *refs,
):
    is_first = first_part == 0
    remote = (last_part - first_part) * (bands - 1)
    part_refs = refs[:remote]
    if is_first:
        coef_ref, table_ref, sums_ref, left_ref, flat_scr, left_scr = refs[remote:]
    else:
        earlier_ref, coef_ref, table_ref, spectra_ref = refs[remote:]
    pairs_sub, cycle_band, slot_count = own_ref.shape
    high_places = pairs_sub // pack
    degree_count = slot_count - 1
    panel_rows = coef_ref.shape[2]
    fields = panel_rows // 2
    block_rows = 4 * panel_rows
    pairs_part = pairs_sub // groups
    group = lax.axis_index("groups")
    band = lax.axis_index("band")
    first = lax.axis_index(owner_axes) * pairs_held + band * pairs_sub
    slot = lax.broadcasted_iota(jnp.int32, (panel_rows, slot_count), 1)
    row = lax.broadcasted_iota(jnp.int32, (panel_rows, slot_count // 2), 0)
    upper = lax.broadcasted_iota(jnp.int32, (panel_rows, slot_count), 0) < fields
    zero = jnp.zeros((panel_rows, slot_count), f32)
    high_power, high_cross = zero, zero
    all_power, all_cross = zero, zero
    if is_first:
        sources, wire_rows, _ = source_ref.shape
        for k in range(bands):
            other = band ^ k
            for w in range(owners):
                at = (k * owners + w) * wire_rows
                rows = source_ref[other * owners + w].astype(f32)
                for c in range(flat_scr.shape[0]):
                    flat_scr[c, at : at + wire_rows, :] = rows[:, c * lane_width : (c + 1) * lane_width]
        for place in range(pairs_sub):
            high_place, low_place = divmod(place, pack)
            wire_row = low_place // wire_pack * high_places + high_place
            received = jnp.concatenate(
                [
                    flat_scr[c, pl.ds(wire_row, sources, stride=wire_rows), :]
                    for c in range(flat_scr.shape[0])
                ],
                axis=1,
            )
            target, at = (left_scr, place) if place < pairs_part else (left_ref, place - pairs_part)
            for il in range(share):
                target[at, pl.ds(il, sources, stride=share), :] = take_block(
                    received, low_place % wire_pack * share + il, block_rows, left_scr.shape[2]
                )
        left_ref = left_scr
    else:
        left_ref = source_ref
        all_power, all_cross = earlier_ref[0], earlier_ref[1]
    for j in range(first_part, last_part):
        part_row = (group ^ j) * pairs_part
        low_power, low_cross = zero, zero
        for q in range(pairs_part):
            at = (j - first_part) * pairs_part + q
            left = left_ref[at, :, 0:block_rows].astype(bf16)
            blocks = [own_ref[part_row + q]] + [t[q] for t in part_refs[j - first_part :: last_part - first_part]]
            table = jnp.concatenate([b.astype(f32) for b in blocks], axis=0).astype(bf16)
            table_ref[at] = table
            both_halves = dot_tn(left, table)
            pair = first + part_row + q
            low_side, low_weight, high_weight = pair_sides(pair, slot, degree_count)
            cosines = jnp.where(
                low_side, both_halves[0:panel_rows], both_halves[2 * panel_rows : 3 * panel_rows]
            )
            sines = jnp.where(
                low_side, both_halves[panel_rows : 2 * panel_rows], both_halves[3 * panel_rows :]
            )
            coef_ref[at, 0] = cosines
            coef_ref[at, 1] = sines
            weight = jnp.where(low_side, low_weight, high_weight)
            power = (cosines * cosines + sines * sines) * weight
            straight = jnp.where(upper, cosines, sines)
            swapped = pltpu.roll(jnp.where(upper, sines, cosines), fields, 0)
            cross = straight * swapped * weight
            low_power = low_power + roll_lanes(jnp.where(low_side, power, 0.0), q)
            low_cross = low_cross + roll_lanes(jnp.where(low_side, cross, 0.0), q)
            high_power = high_power + jnp.where(low_side, 0.0, power)
            high_cross = high_cross + jnp.where(low_side, 0.0, cross)
        all_power = all_power + pltpu.roll(low_power, first + part_row, 1)
        all_cross = all_cross + pltpu.roll(low_cross, first + part_row, 1)
    all_power = all_power + pltpu.roll(high_power, slot_count - 1, 1)
    all_cross = all_cross + pltpu.roll(high_cross, slot_count - 1, 1)
    if is_first:
        sums_ref[0] = all_power
        sums_ref[1] = all_cross
    else:
        all_cross = all_cross + pltpu.roll(all_cross, fields, 0)
        spectra_ref[:, 0:slot_count] = all_power
        spectra_ref[:, slot_count:] = jnp.where(
            row < fields, all_cross[:, : slot_count // 2], all_cross[:, slot_count // 2 :]
        )


def tree_sum(parts):
    while len(parts) > 1:
        parts = [parts[i] + parts[i + 1] for i in range(0, len(parts), 2)]
    return parts[0]


def gradient_kernel(pack, groups, bands, owners, pairs_held, share, spectra_parts, *refs):
    spectra_refs = refs[:spectra_parts]
    coef_refs = refs[spectra_parts : spectra_parts + 2]
    table_refs = refs[spectra_parts + 2 : spectra_parts + 4]
    wire_ref, misfit_ref, flat_scr, cycle_scr = refs[spectra_parts + 4 :]
    sources, wire_rows, wire_lanes = wire_ref.shape
    pairs_part = coef_refs[0].shape[0]
    pairs_sub = groups * pairs_part
    slot_count = table_refs[0].shape[2]
    degree_count = slot_count - 1
    panel_rows = coef_refs[0].shape[2]
    fields = panel_rows // 2
    block_rows = 4 * fields
    fields_out = fields // bands
    group = lax.axis_index("groups")
    band = lax.axis_index("band")
    first = lax.axis_index(owner_axes) * pairs_held + band * pairs_sub
    slot = lax.broadcasted_iota(jnp.int32, (panel_rows, slot_count), 1)
    row = lax.broadcasted_iota(jnp.int32, (panel_rows, slot_count), 0)
    spectra = tree_sum([s[...] for s in spectra_refs])
    power = spectra[:, :slot_count]
    packed = spectra[:, slot_count:]
    turned = pltpu.roll(packed, fields, 0)
    upper = row[:, : slot_count // 2] < fields
    cross = jnp.concatenate([jnp.where(upper, packed, turned), jnp.where(upper, turned, packed)], axis=1)
    odd_weight = (2 * slot + 1).astype(f32)
    per_degree = 1.0 / odd_weight
    power = power * per_degree + spectrum_floor
    cross = cross * per_degree
    root = jnp.sqrt(power)
    other_root = pltpu.roll(root, fields, 0)
    both_power = power + pltpu.roll(power, fields, 0)
    geo_mean = root * other_root
    over_geo = 1.0 / geo_mean
    over_power = 1.0 / power
    coherence = cross * over_geo
    term = (root - other_root) * (root - other_root) + both_power * (1.0 - coherence)
    term = jnp.where(slot < degree_count, term, 0.0)
    mean = jnp.sum(term, axis=1, keepdims=True) / degree_count
    field_row = lax.broadcasted_iota(jnp.int32, (panel_rows, 1), 0)
    misfit_ref[...] = jnp.zeros_like(misfit_ref)
    for i in range(fields_out):
        chosen = jnp.where(field_row == band * fields_out + i, mean, 0.0)
        misfit_ref[i : i + 1, :] = jnp.broadcast_to(
            jnp.sum(chosen, axis=0, keepdims=True), (1, lane_width)
        )
    grad_power = (
        gradient_gain
        * (
            1.0
            - geo_mean * over_power
            + (1.0 - coherence)
            + 0.5 * both_power * coherence * over_power
        )
        * per_degree
    )
    grad_cross = -gradient_gain * both_power * over_geo * per_degree
    by_degree = jnp.where(row < fields, 2.0 * grad_power, grad_cross)
    high_grad = pltpu.roll(by_degree, 1, 1)
    blocks = []
    for j in range(groups):
        part_row = (group ^ j) * pairs_part
        low_grad = pltpu.roll(by_degree, slot_count - first - part_row, 1)
        for q in range(pairs_part):
            place = j * pairs_part + q
            at_part = (0, q) if j == 0 else (1, place - pairs_part)
            pair = first + part_row + q
            low_side, low_weight, high_weight = pair_sides(pair, slot, degree_count)
            shifted = roll_lanes(low_grad, slot_count - q)
            gain = jnp.where(low_side, shifted * low_weight, high_grad * high_weight)
            cosines = coef_refs[at_part[0]][at_part[1], 0] * gain
            sines = coef_refs[at_part[0]][at_part[1], 1] * gain
            swapped = pltpu.roll(jnp.where(row < fields, sines, cosines), fields, 0)
            grads = jnp.where(row < fields, cosines, sines) + swapped
            masked = jnp.concatenate(
                [jnp.where(low_side, grads, 0.0), jnp.where(low_side, 0.0, grads)], axis=0
            ).astype(bf16)
            cycle_scr[place, :, 0:block_rows] = dot_nt(
                table_refs[at_part[0]][at_part[1]], masked
            )
            high_place, low_place = divmod(place, pack)
            blocks = [] if low_place == 0 else blocks
            blocks += [cycle_scr[place, pl.ds(il, sources, stride=share), :] for il in range(share)]
            if low_place == pack - 1:
                joined = join_blocks(blocks, block_rows, wire_lanes)
                for c in range(flat_scr.shape[0]):
                    flat_scr[c, pl.ds(high_place, sources, stride=wire_rows), :] = joined[
                        :, c * lane_width : (c + 1) * lane_width
                    ]
    for k in range(bands):
        other = band ^ k
        for w in range(owners):
            at = (k * owners + w) * wire_rows
            wire_ref[other * owners + w] = jnp.concatenate(
                [flat_scr[c, at : at + wire_rows, :] for c in range(flat_scr.shape[0])], axis=1
            ).astype(bf16)


def synthesise_kernel(pack, coarse_ref, fine_ref, mask_ref, wire_ref, out_ref, flat_scr):
    share, fields, extent = out_ref.shape
    sources, wire_rows, wire_lanes = wire_ref.shape
    steps = extent // lane_width
    half_lanes = coarse_ref.shape[3] // 2
    panel_rows = 2 * fields
    width = sources * wire_rows
    for source in range(sources):
        flat_scr[source * wire_rows : (source + 1) * wire_rows, :] = wire_ref[source].astype(f32)
    if flat_scr.shape[0] > width:
        flat_scr[width:, :] = jnp.zeros_like(flat_scr[width:, :])
    turned = jnp.transpose(flat_scr[...])
    count = wire_lanes // pack
    if pack > 1:
        spare = jnp.zeros((count, round_up(half_lanes, lane_width) - turned.shape[1]), f32)
        values = jnp.zeros((count, half_lanes), f32)
        for low_place in range(pack):
            block = jnp.concatenate([turned[low_place * count : (low_place + 1) * count], spare], axis=1)
            values = values + move_lanes(block, [(0, width, low_place * width)], half_lanes)
    else:
        values = turned[:, :half_lanes]
    row = lax.broadcasted_iota(jnp.int32, (panel_rows, 2 * half_lanes), 0)
    for il in range(share):
        at = il * 2 * panel_rows
        direct = jnp.concatenate(
            [values[at : at + panel_rows], values[at + panel_rows : at + 2 * panel_rows]], axis=1
        )
        crossed = pltpu.roll(direct, fields, 0)
        crossed = jnp.where(row < fields, crossed, -crossed)
        pieces = [
            direct * coarse_ref[il, 0, j : j + 1, :] + crossed * coarse_ref[il, 1, j : j + 1, :]
            for j in range(steps)
        ]
        pieces = jnp.concatenate(pieces, 0).astype(bf16)
        fine = jnp.concatenate([fine_ref[il, 0], fine_ref[il, 1]], axis=0)
        total = dot_nt(pieces, fine)
        total_c, total_s = total[:, :lane_width], total[:, lane_width:]
        mask = mask_ref[il : il + 1, :]
        for j in range(steps):
            lanes = slice(lane_width * j, lane_width * (j + 1))
            at = j * panel_rows
            piece = total_c[at : at + fields] + total_s[at + fields : at + panel_rows]
            out_ref[il, :, lanes] = (piece * mask[:, lanes]).astype(bf16)


def call(body, name, arrays, spaces, out_shapes, scratch, flops=1):
    return pl.pallas_call(
        body,
        name=name,
        cost_estimate=pl.CostEstimate(flops=flops, transcendentals=0, bytes_accessed=1),
        in_specs=[pl.BlockSpec(memory_space=space) for space in spaces],
        out_specs=tuple(pl.BlockSpec(memory_space=pltpu.VMEM) for _ in out_shapes),
        out_shape=tuple(out_shapes),
        scratch_shapes=scratch,
        compiler_params=pltpu.CompilerParams(vmem_limit_bytes=vmem_bytes),
    )(*arrays)


def exchange(array, axes, count):
    return [array] + [
        lax.ppermute(array, axes, [(i, i ^ k) for i in range(count)]) for k in range(1, count)
    ]


def per_device(predicted_state, analysis_state, nodes_per_parallel, weighted_harmonic_table):
    share, fields, extent = predicted_state.shape
    pairs_held, cycle_band, slot_count = weighted_harmonic_table.shape
    groups = lax.axis_size("groups")
    bands = lax.axis_size("band")
    owners = lax.axis_size(owner_axes)
    group = lax.axis_index("groups")
    band = lax.axis_index("band")
    sources = bands * owners
    pairs_part = -(-pairs_held // (bands * groups))
    pairs_sub = groups * pairs_part
    panel_rows = 2 * fields
    pack = max(1, lane_width // (share * 4 * fields))
    wire_pack = 1
    wire_lanes = round_up(wire_pack * share * 4 * panel_rows, lane_width)
    back_lanes = round_up(pack * share * 4 * fields, lane_width)
    block_lanes = round_up(4 * panel_rows, lane_width)
    half_lanes = sources * pairs_sub
    coarse_rows = round_up(extent // lane_width, 8)

    table = weighted_harmonic_table
    if pairs_sub * bands != pairs_held:
        table = jnp.pad(table, ((0, pairs_sub * bands - pairs_held), (0, 0), (0, 0)))

    def over_bands(array, k):
        return lax.ppermute(array, "band", [(i, i ^ k) for i in range(bands)])

    starts = [((band ^ k) * groups + (group ^ j)) * pairs_part for k in range(1, bands) for j in range(groups)]
    pieces = [
        lax.dynamic_slice_in_dim(table, start, pairs_part, 0)
        for n, start in enumerate(starts)
        if n < groups or n % groups == 0
    ]
    pieces = lax.optimization_barrier(pieces)
    near = over_bands(jnp.stack(pieces[:groups]), 1)
    near = [near[j] for j in range(groups)]
    far = [over_bands(piece, n + 2) for n, piece in reversed(list(enumerate(pieces[groups:])))][::-1]
    states = jnp.concatenate([predicted_state, analysis_state], axis=1)
    wire, coarse, fine, mask = call(
        functools.partial(
            analyse_kernel,
            pack,
            wire_pack,
            groups,
            bands,
            owners,
            pairs_held,
            pairs_part,
            slot_count - 1,
        ),
        "analyse",
        (nodes_per_parallel, states),
        (pltpu.SMEM, pltpu.VMEM),
        (
            jax.ShapeDtypeStruct((sources, pairs_sub // wire_pack, wire_lanes), bf16),
            jax.ShapeDtypeStruct((share, 2, coarse_rows, 2 * half_lanes), f32),
            jax.ShapeDtypeStruct((share, 2, lane_width, 2 * half_lanes), bf16),
            jax.ShapeDtypeStruct((share, extent), f32),
        ),
        [
            pltpu.VMEM((share * 4 * panel_rows, half_lanes), f32),
            pltpu.VMEM((wire_lanes, round_up(half_lanes // wire_pack, lane_width)), f32),
            pltpu.VMEM((round_up(half_lanes // wire_pack, lane_width), wire_lanes), f32),
        ],
    )
    wire = lax.all_to_all(wire, group_axes, 0, 0, tiled=True)
    parts = list(near)
    for piece in far:
        parts.append(piece)
        for j in range(1, groups):
            parts.append(lax.ppermute(piece, "groups", [(i, i ^ j) for i in range(groups)]))
    far[-1], own_start = lax.optimization_barrier((far[-1], band * pairs_sub))
    own_table = lax.dynamic_slice_in_dim(table, own_start, pairs_sub, 0)
    sizes = (pack, wire_pack, groups, bands, owners, pairs_held, share)
    other_pairs = pairs_sub - pairs_part
    left_shape = (bands * cycle_band, block_lanes)

    def pair_shapes(count):
        return (
            jax.ShapeDtypeStruct((count, 2, panel_rows, slot_count), f32),
            jax.ShapeDtypeStruct((count, bands * cycle_band, slot_count), bf16),
        )

    own_coef, own_rows, sums, left = call(
        functools.partial(project_kernel, *sizes, 0, 1),
        "project_own",
        (wire, own_table, *parts[0::groups]),
        (pltpu.VMEM,) * (1 + bands),
        (
            *pair_shapes(pairs_part),
            jax.ShapeDtypeStruct((2, panel_rows, slot_count), f32),
            jax.ShapeDtypeStruct((other_pairs, *left_shape), f32),
        ),
        [
            pltpu.VMEM((wire_lanes // lane_width, half_lanes // wire_pack, lane_width), f32),
            pltpu.VMEM((pairs_part, *left_shape), f32),
        ],
    )
    others = [p for n, p in enumerate(parts) if n % groups > 0]
    other_coef, other_rows, spectra = call(
        functools.partial(project_kernel, *sizes, 1, groups),
        "project",
        (left, own_table, *others, sums),
        (pltpu.VMEM,) * (3 + len(others)),
        (
            *pair_shapes(other_pairs),
            jax.ShapeDtypeStruct((panel_rows, slot_count + slot_count // 2), f32),
        ),
        [],
    )
    spectra = tree_sum(exchange(spectra, "band", bands))
    spectra = exchange(spectra, owner_axes, owners)
    wire, misfit = call(
        functools.partial(gradient_kernel, pack, groups, bands, owners, pairs_held, share, len(spectra)),
        "gradient",
        (*spectra, own_coef, other_coef, own_rows, other_rows),
        (pltpu.VMEM,) * (4 + len(spectra)),
        (
            jax.ShapeDtypeStruct((sources, pairs_sub // pack, back_lanes), bf16),
            jax.ShapeDtypeStruct((round_up(fields // bands, 8), lane_width), f32),
        ),
        [
            pltpu.VMEM((back_lanes // lane_width, half_lanes // pack, lane_width), f32),
            pltpu.VMEM((pairs_sub, *left_shape), f32),
        ],
    )
    wire = lax.all_to_all(wire, group_axes, 0, 0, tiled=True)
    (sensitivity,) = call(
        functools.partial(synthesise_kernel, pack),
        "synthesise",
        (coarse, fine, mask, wire),
        (pltpu.VMEM,) * 4,
        (jax.ShapeDtypeStruct((share, fields, extent), bf16),),
        [pltpu.VMEM((round_up(half_lanes // pack, lane_width), back_lanes), f32)],
    )
    return misfit[: fields // bands, 0], sensitivity


def solution(mesh):
    in_specs = (
        P(("groups", "band", "field", "wave"), None, None),
        P(("groups", "band", "field", "wave"), None, None),
        P(),
        P(("field", "wave"), "band", None),
    )
    out_specs = (P(("groups", "band")), P(("groups", "band", "field", "wave"), None, None))
    return jax.shard_map(
        per_device, mesh=mesh, in_specs=in_specs, out_specs=out_specs, check_vma=False
    )
```
